128 devices in a mesh: tm: 16 (over z_lo, y, core), gz: 8 (over z_hi, x).
Axes of the slice: x: 4, y: 4, z: 4 (z_hi: 2, z_lo: 2; z = z_hi * 2 + z_lo), core: 2. Of those that a mesh axis runs over, the one named last changes fastest.
Arguments:
- prev_term: float32 [16, 512, 32, 512], P('tm', None, 'gz'), may hold values from -6 to 6
- last_term: float32 [16, 512, 32, 512], P('tm', None, 'gz'), may hold values from -6 to 6
- cos_sum: float32 [16, 512, 32, 512], P('tm', None, 'gz'), may hold values from -2 to 2
- sin_sum: float32 [16, 512, 32, 512], P('tm', None, 'gz'), may hold values from -2 to 2
- speed_sq: float32 [512, 32, 512], P(None, 'gz'), may hold values from 0.5 to 2
- series_coeffs: float32 [16, 4], P('tm'), may hold values from -1 to 1
Outputs:
- displacement: float32 [512, 32, 512], P('tm', 'gz')
- velocity: float32 [512, 32, 512], P('tm', 'gz')
The draws below stay inside these ranges and needn't reach their ends.
All inputs are finite; a program needn't handle non-finite values.
Results may differ from the reference program's by a relative error of at most 0.00002.
Values sent between devices are 32-bit elements; how exact they have to be, the bound alone decides.
No kernel may reach another device: no remote copies, remote signals or barrier semaphores. Data moves between devices by JAX's collectives and lax.ppermute only.
A program may use at most 256 MiB of HBM per device.

```python
import math
import jax
import jax.numpy as jnp
from jax import lax

NX = 512
NY = 512
NZ = 32
INTERVALS = 16


def raised(array, stream_key, source, target, shards_of, factor):
    def block_of(dim):
        return (jnp.arange(array.shape[dim]) // (array.shape[dim] // shards_of)).reshape((-1,) + (1,) * (array.ndim - 1 - dim))

    near = jax.random.permutation(stream_key, shards_of)[block_of(target)]
    second = (block_of(target) + shards_of // 2) % shards_of
    return jnp.where((block_of(source) == near) | (block_of(source) == second), factor * array, array)


def levels(rng, dims, split, low, top_value):
    gain = 1.0
    for dim, shards_of in split:
        draws = jax.random.uniform(jax.random.fold_in(jax.random.fold_in(rng, 6), dim), (shards_of,), jnp.float32, low / len(split), top_value / len(split))
        gain = gain * jnp.repeat(jnp.exp(draws), dims[dim] // shards_of).reshape((-1,) + (1,) * (len(dims) - 1 - dim))
    return gain


def normal_values(stream_key, extent, deviation, most, shards=(), dtype=jnp.bfloat16):
    values = jax.random.normal(stream_key, extent, jnp.float32) * deviation
    if len(shards) > 0:
        values = levels(stream_key, extent, shards, -0.22, 0.18) * values
    return jnp.clip(values, min=-most, max=most).astype(dtype)


def heavy_noise(stream_key, shape, width, bound, pieces, heavy, held_as=jnp.bfloat16):
    result = width * jax.random.normal(stream_key, shape, jnp.float32)
    if pieces:
        result = result * levels(stream_key, shape, pieces, -0.22, 0.18)
    return jnp.clip(raised(result, jax.random.fold_in(stream_key, 3), *heavy), -bound, bound).astype(held_as)


def setup_inputs(seed: int = 0) -> dict:
    keys = jax.random.split(jax.random.key(seed), 7)
    return {
        "prev_term": normal_values(keys[0], (INTERVALS, NX, NZ, NY), 1.0, 6.0, ((0, 16), (2, 8)), jnp.float32),
        "last_term": normal_values(keys[1], (INTERVALS, NX, NZ, NY), 1.0, 6.0, ((0, 16), (2, 8)), jnp.float32),
        "cos_sum": heavy_noise(keys[2], (INTERVALS, NX, NZ, NY), 0.25, 2.0, ((0, 16), (2, 8)), (0, 1, 16, 2.0), jnp.float32),
        "sin_sum": heavy_noise(keys[3], (INTERVALS, NX, NZ, NY), 0.25, 2.0, ((0, 16), (2, 8)), (0, 1, 16, 2.0), jnp.float32),
        "speed_sq": jnp.clip(jnp.exp(math.log(2.0) - 1.3862944 * jax.random.uniform(keys[4], (NX, NZ, NY), jnp.float32) ** levels(keys[4], (NX, NZ, NY), ((1, 8),), -0.2, 0.2)), 0.5, 2.0),
        "series_coeffs": normal_values(keys[5], (INTERVALS, 4), 0.25, 1.0, ((0, 16),), jnp.float32),
    }


inverse_bound = 1.0 / 12.0


def operate(field, speed):
    fpad = jnp.pad(field, ((0, 0), (0, 0), (1, 1)))
    kpad = jnp.pad(speed, ((0, 0), (0, 0), (1, 1)))
    center = fpad[1:-1, 1:-1, 1:-1]
    kcenter = kpad[1:-1, 1:-1, 1:-1]
    total = jnp.zeros(center.shape, jnp.float32)
    for slicer in ((slice(2, None), slice(1, -1), slice(1, -1)), (slice(0, -2), slice(1, -1), slice(1, -1)),
                   (slice(1, -1), slice(2, None), slice(1, -1)), (slice(1, -1), slice(0, -2), slice(1, -1)),
                   (slice(1, -1), slice(1, -1), slice(2, None)), (slice(1, -1), slice(1, -1), slice(0, -2))):
        total = total + 0.5 * (kcenter + kpad[slicer]) * (center - fpad[slicer])
    return total * inverse_bound - center


def padded(field):
    return jnp.pad(field, ((1, 1), (1, 1), (0, 0)))


def reference(prev_term, last_term, cos_sum, sin_sum, speed_sq, series_coeffs):
    speed_pad = padded(speed_sq)

    def interval(carry, items):
        previous, current, part_cos, part_sin, coeffs = items
        nextterm = 2.0 * operate(padded(current), speed_pad) - previous
        finalterm = 2.0 * operate(padded(nextterm), speed_pad) - current
        disp = part_cos + coeffs[0] * nextterm + coeffs[1] * finalterm
        veloc = part_sin + coeffs[2] * nextterm + coeffs[3] * finalterm
        return (carry[0] + disp, carry[1] + veloc), None

    zeros = jnp.zeros(speed_sq.shape, jnp.float32)
    totals, unused = lax.scan(interval, (zeros, zeros), (prev_term, last_term, cos_sum, sin_sum, series_coeffs))
    return totals[0], totals[1]
```

```python
import functools

import jax
import jax.numpy as jnp
from jax import lax
from jax.experimental import pallas as pl
from jax.experimental.pallas import tpu as pltpu
from jax.sharding import PartitionSpec as P

ROWS = 4
VMEM = 16 * 1024 * 1024
F32 = jnp.float32


def packed(cells):
    x = cells.shape[0]
    return cells.reshape(x, 4, 4, 128).transpose(0, 2, 1, 3).reshape(x, 2, 8, 128)


def unpacked(cells):
    x = cells.shape[0]
    return cells.reshape(x, 4, 4, 128).transpose(0, 2, 1, 3).reshape(x, 4, 512)


def roll(cells, shift):
    return pltpu.roll(cells, shift % 8, 1)


def places(n):
    sub = lax.broadcasted_iota(jnp.int32, (n, 8, 128), 1)
    return sub, lax.rem(sub, 4), lax.broadcasted_iota(jnp.int32, (n, 8, 128), 2)


def spread(field, speed, row, n, lower, upper):
    sub, z, lane = places(n)
    first, at_start, at_end = sub < 4, lane == 0, lane == 127
    v = [field[pl.ds(row + 1, n), h] for h in (0, 1)]
    k = [speed[pl.ds(row + 1, n), h] for h in (0, 1)]

    def ahead(a, b):
        ra, rb = pltpu.roll(a, 127, 2), pltpu.roll(b, 127, 2)
        qa, qb = roll(ra, 4), roll(rb, 4)
        return (
            jnp.where(at_end, jnp.where(first, qa, qb), ra),
            jnp.where(at_end, jnp.where(first, qb, 0.0), rb),
        )

    def behind(a, b, edge):
        ra, rb = pltpu.roll(a, 1, 2), pltpu.roll(b, 1, 2)
        qa, qb = roll(ra, 4), roll(rb, 4)
        return (
            jnp.where(at_start, jnp.where(first, edge, qa), ra),
            jnp.where(at_start, jnp.where(first, qa, qb), rb),
        )

    v_y, k_y = ahead(*v), ahead(*k)
    f_y = [(k[h] + k_y[h]) * (v_y[h] - v[h]) for h in (0, 1)]
    b_y = behind(*f_y, k[0] * v[0])
    out = []
    for h in (0, 1):
        kv = k[h] * v[h]
        f_z = jnp.where(z == 3, -upper * kv, (k[h] + roll(k[h], -1)) * (roll(v[h], -1) - v[h]))
        b_z = jnp.where(z == 0, lower * kv, roll(f_z, 1))
        f_x = (k[h] + speed[pl.ds(row + 2, n), h]) * (field[pl.ds(row + 2, n), h] - v[h])
        b_x = (k[h] + speed[pl.ds(row, n), h]) * (v[h] - field[pl.ds(row, n), h])
        out.append((f_x - b_x) + (f_y[h] - b_y[h]) + (f_z - b_z))
    return v, out


def widen(scratch, main, before, after, block, blocks):
    rows = main.shape[0]
    scratch[pl.ds(1, rows)] = main[...]
    scratch[pl.ds(0, 1)] = jnp.where(block > 0, before[...], 0.0)
    scratch[pl.ds(rows + 1, 1)] = jnp.where(block < blocks - 1, after[...], 0.0)


def next_kernel(real, u, u_b, u_a, k, k_b, k_a, p, n_out, up_out, down_out, own_out, us, ks):
    block, blocks = pl.program_id(0), pl.num_programs(0)
    rows = u.shape[0]
    widen(us, u, u_b, u_a, block, blocks)
    widen(ks, k, k_b, k_a, block, blocks)
    lower, upper = real[0], real[1]
    z = places(ROWS // 2)[1]
    z_all = places(ROWS)[1]

    def pair(cells):
        both = cells.reshape(ROWS // 2, 2, 8, 128)
        return both[:, 0], both[:, 1]

    def top(uu, nn):
        even, odd = pair(jnp.where(z_all == 3, nn, roll(uu, -1)))
        return jnp.where(z < 2, roll(even, -2), odd)

    def bottom(uu, nn):
        even, odd = pair(jnp.where(z_all == 0, uu, roll(nn, 1)))
        return jnp.where(z < 2, even, roll(odd, 2))

    def step(i, carry):
        row = i * ROWS
        v, out = spread(us, ks, row, ROWS, lower, upper)
        n = []
        for h in (0, 1):
            n.append(out[h] * (-1.0 / 12.0) - 2.0 * v[h] - p[pl.ds(row, ROWS), h])
            n_out[pl.ds(row, ROWS), h] = n[h]
        half = pl.ds(i * (ROWS // 2), ROWS // 2)
        up_out[half] = top(v[0], n[0])
        down_out[half] = bottom(v[1], n[1])
        own_out[0, half] = bottom(v[0], n[0])
        own_out[1, half] = top(v[1], n[1])
        return carry

    lax.fori_loop(0, rows // ROWS, step, 0)


def series_kernel(place, real, n, n_b, n_a, k, k_b, k_a, u, cos, sin, d_out, v_out, ns, ks, *, blocks, block_of):
    block = block_of(pl.program_id(0), place)
    rows = u.shape[0]
    widen(ns, n, n_b, n_a, block, blocks)
    widen(ks, k, k_b, k_a, block, blocks)
    lower, upper = real[0], real[1]
    c0, c1, c2, c3 = real[2], real[3], real[4], real[5]

    def step(i, carry):
        row = i * ROWS
        here = pl.ds(row, ROWS)
        v, out = spread(ns, ks, row, ROWS, lower, upper)
        for h in (0, 1):
            final = out[h] * (-1.0 / 12.0) - 2.0 * v[h] - u[here, h]
            d_out[0, here, h] = cos[here, h] + c0 * v[h] + c1 * final
            v_out[0, here, h] = sin[here, h] + c2 * v[h] + c3 * final
        return carry

    lax.fori_loop(0, rows // ROWS, step, 0)


def jump_kernel(place, real, *refs, blocks, block_of):
    own, own_b, own_a, low, low_b, low_a, high, high_b, high_a, other_out, same_out = refs
    turn = pl.program_id(0)
    block = block_of(turn, pl.program_id(1), place)
    pairs = low.shape[0]
    c0, c1, c2, c3 = real[2], real[3], real[4], real[5]

    def moments(jump):
        n = jump.shape[0]
        z = places(n)[1]
        even_slot = lax.rem(z, 2) == 0
        du = jnp.where(even_slot, jump, roll(jump, 1))
        dn = jnp.where(even_slot, roll(jump, -1), jump)
        ca = jnp.where(z == 0, c1, jnp.where(z == 1, c0, jnp.where(z == 2, c3, c2)))
        cb = jnp.where(z == 1, c1, jnp.where(z == 3, c3, 0.0))
        even = ca * jnp.where(z < 2, du, roll(du, 2)) + cb * jnp.where(z < 2, dn, roll(dn, 2))
        odd = ca * jnp.where(z >= 2, du, roll(du, -2)) + cb * jnp.where(z >= 2, dn, roll(dn, -2))
        return even, odd

    def fill(out):
        for h, jumps in (
            (0, [own_b[0] - low_b[...], own[0] - low[...], own_a[0] - low_a[...]]),
            (1, [high_b[...] - own_b[1], high[...] - own[1], high_a[...] - own_a[1]]),
        ):
            _, odd = moments(jumps[0])
            out[0, h, pl.ds(0, 1)] = jnp.where(block > 0, odd, 0.0)
            even, odd = moments(jumps[1])
            out[0, h, pl.ds(1, 2 * pairs)] = jnp.stack([even, odd], axis=1).reshape(2 * pairs, 8, 128)
            even, _ = moments(jumps[2])
            out[0, h, pl.ds(2 * pairs + 1, 1)] = jnp.where(block < blocks - 1, even, 0.0)

    @pl.when(turn == 0)
    def _():
        fill(other_out)

    @pl.when(turn == 1)
    def _():
        fill(same_out)


def mend_kernel(real, d, v, e, e_low, e_high, k, k_low, k_high, d_out, v_out, ds, vs):
    rows = d.shape[0]
    lower, upper = real[0], real[1]
    wide = rows + 2
    z = places(wide)[1]
    factor = []
    for h in (0, 1):
        below = (1.0 - lower) * (k[:, h] + roll(k_low[:, h], -3))
        above = (1.0 - upper) * (k[:, h] + roll(k_high[:, h], 3))
        factor.append(jnp.where(z == 0, below, jnp.where(z == 3, -above, 0.0)) * (1.0 / 12.0))
    from_low = [e[0], e_low[...]]
    from_high = [e_high[...], e[1]]
    direct = []
    for field, slot in ((ds, 0), (vs, 2)):
        for h in (0, 1):
            a = jnp.where(z == 0, roll(from_low[h], -slot), roll(from_high[h], 3 - slot))
            b = jnp.where(z == 0, roll(from_low[h], -slot - 1), roll(from_high[h], 2 - slot))
            w = factor[h] * a
            field[:, h] = w
            direct.append((factor[h] * b + 2.0 * jnp.abs(factor[h]) * w)[1 : rows + 1])
    for field, given, out, direct_of in ((ds, d, d_out, direct[:2]), (vs, v, v_out, direct[2:])):
        w, outflow = spread(field, k, 0, rows, lower, upper)
        for h in (0, 1):
            out[:, h] = given[:, h] + direct_of[h] - outflow[h] * (1.0 / 12.0) - 2.0 * w[h]


def row_specs(rows, total, block_of, tail):
    zeros = (0,) * len(tail)
    return [
        pl.BlockSpec((rows, *tail), lambda *i: (block_of(*i), *zeros)),
        pl.BlockSpec((1, *tail), lambda *i: (jnp.maximum(block_of(*i) * rows - 1, 0), *zeros)),
        pl.BlockSpec((1, *tail), lambda *i: (jnp.minimum(block_of(*i) * rows + rows, total - 1), *zeros)),
    ]


SMEM = pl.BlockSpec(memory_space=pltpu.SMEM)
CELL = (2, 8, 128)


def params():
    return pltpu.CompilerParams(vmem_limit_bytes=VMEM)


def cost(reads, flops=0):
    return pl.CostEstimate(flops=flops, bytes_accessed=reads, transcendentals=0)


def next_terms(real, u, k, p, blocks):
    x = u.shape[0]
    rows = x // blocks
    plain = lambda i: i
    main = pl.BlockSpec((rows, *CELL), lambda i: (i, 0, 0, 0))
    half = pl.BlockSpec((rows // 2, 8, 128), lambda i: (i, 0, 0))
    shape = functools.partial(jax.ShapeDtypeStruct, dtype=F32)
    return pl.pallas_call(
        next_kernel,
        grid=(blocks,),
        out_shape=(shape((x, *CELL)), shape((x // 2, 8, 128)), shape((x // 2, 8, 128)), shape((2, x // 2, 8, 128))),
        in_specs=[SMEM, *row_specs(rows, x, plain, CELL), *row_specs(rows, x, plain, CELL), main],
        out_specs=(main, half, half, pl.BlockSpec((2, rows // 2, 8, 128), lambda i: (0, i, 0, 0))),
        scratch_shapes=[pltpu.VMEM((rows + 2, *CELL), F32)] * 2,
        compiler_params=params(),
        cost_estimate=cost(24 * 1024 * 1024),
    )(real, u, u, u, k, k, k, p)


def target(side, turn, place, core):
    way = 1 - 2 * core
    return ((lax.rem(place[0] + side, 2)) * 4 + lax.rem(place[1] + way * turn + 4, 4)) * 2 + core


def series(place, real, n, k, u, cos, sin, blocks, flip):
    x = u.shape[0]
    rows = x // blocks

    def block_of(j, place):
        core = lax.rem(place[2] + flip, 2)
        return target(j // 4, lax.rem(j, 4), place, core)

    main = pl.BlockSpec((rows, *CELL), lambda j, place: (block_of(j, place), 0, 0, 0))
    shape = jax.ShapeDtypeStruct((blocks // 2, rows, *CELL), F32)
    return pl.pallas_call(
        functools.partial(series_kernel, blocks=blocks, block_of=block_of),
        grid_spec=pltpu.PrefetchScalarGridSpec(
            num_scalar_prefetch=1,
            grid=(blocks // 2,),
            in_specs=[SMEM, *row_specs(rows, x, block_of, CELL), *row_specs(rows, x, block_of, CELL), main, main, main],
            out_specs=(
                pl.BlockSpec((1, rows, *CELL), lambda j, place: (j, 0, 0, 0, 0)),
                pl.BlockSpec((1, rows, *CELL), lambda j, place: (lax.rem(j, 4) * 2 + j // 4, 0, 0, 0, 0)),
            ),
            scratch_shapes=[pltpu.VMEM((rows + 2, *CELL), F32)] * 2,
        ),
        out_shape=(shape, shape),
        compiler_params=params(),
        cost_estimate=cost(14 * 1024 * 1024),
    )(place, real, n, n, n, k, k, k, u, cos, sin)


def jumps(place, real, own, low, high, blocks):
    x = own.shape[1] * 2
    rows = x // blocks
    pairs = rows // 2

    def block_of(turn, j, place):
        core = lax.rem(place[2] + 1 - turn, 2)
        return target(lax.rem(j, 2), j // 2, place, core)

    plane = row_specs(pairs, x // 2, block_of, (8, 128))
    own_specs = [
        pl.BlockSpec((2, n, 8, 128), lambda *i, spec=spec: (0, *spec.index_map(*i)))
        for n, spec in zip((pairs, 1, 1), plane)
    ]
    shape = jax.ShapeDtypeStruct((blocks // 2, 2, rows + 2, 8, 128), F32)
    last = blocks // 2 - 1
    return pl.pallas_call(
        functools.partial(jump_kernel, blocks=blocks, block_of=block_of),
        grid_spec=pltpu.PrefetchScalarGridSpec(
            num_scalar_prefetch=1,
            grid=(2, blocks // 2),
            in_specs=[SMEM, *own_specs, *plane, *plane],
            out_specs=(
                pl.BlockSpec((1, 2, rows + 2, 8, 128), lambda i, j, place: (jnp.where(i == 0, j, last), 0, 0, 0, 0)),
                pl.BlockSpec((1, 2, rows + 2, 8, 128), lambda i, j, place: (jnp.where(i == 0, 0, j), 0, 0, 0, 0)),
            ),
        ),
        out_shape=(shape, shape),
        compiler_params=params(),
        cost_estimate=cost(8 * 1024 * 1024),
    )(place, real, own, own, own, low, low, low, high, high, high)


def mend(real, d, v, e, e_low, e_high, k, k_low, k_high):
    shape = jax.ShapeDtypeStruct(d.shape, F32)
    whole = pl.BlockSpec(memory_space=pltpu.VMEM)
    return pl.pallas_call(
        mend_kernel,
        out_shape=(shape, shape),
        in_specs=[SMEM] + [whole] * 8,
        out_specs=(whole, whole),
        scratch_shapes=[pltpu.VMEM(k.shape, F32)] * 2,
        compiler_params=params(),
        cost_estimate=cost(4 * 1024 * 1024),
    )(real, d, v, e, e_low, e_high, k, k_low, k_high)


COUNT = 16
SLABS = 8


def along_y(sign):
    def goal(i):
        z, y, core = i // 8, (i // 2) % 4, i % 2
        return z * 8 + ((y + sign * (1 - 2 * core)) % 4) * 2 + core

    return [(i, goal(i)) for i in range(COUNT)]


FORTH, BACK = along_y(1), along_y(-1)
ACROSS = [(i, i ^ 8) for i in range(COUNT)]
SIBLING = [(i, i ^ 1) for i in range(COUNT)]
UP = [(i, i + 1) for i in range(SLABS - 1)]
DOWN = [(i + 1, i) for i in range(SLABS - 1)]


def ring(two, one, back, own):
    relayed = lax.ppermute(two, "tm", FORTH)
    direct = lax.ppermute(back, "tm", BACK)
    rest = lax.ppermute(one + relayed, "tm", FORTH)
    return own + direct + rest


def y_then_z(cells):
    cells = cells.reshape(4, 2, *cells.shape[1:])
    mine = ring(cells[2], cells[1], cells[3], cells[0])
    return mine[0] + lax.ppermute(mine[1], "tm", ACROSS)


def z_then_y(cells):
    half = cells.shape[0] // 2
    mine = cells[:half] + lax.ppermute(cells[half:], "tm", ACROSS)
    return ring(mine[2], mine[1], mine[3], mine[0])


def local(prev_term, last_term, cos_sum, sin_sum, speed_sq, series_coeffs):
    u, p, k = packed(last_term[0]), packed(prev_term[0]), packed(speed_sq)
    cos, sin = packed(cos_sum[0]), packed(sin_sum[0])
    blocks = lax.axis_size("tm")
    rows = u.shape[0] // blocks
    me, slab = lax.axis_index("tm"), lax.axis_index("gz")
    place = jnp.stack([me // 8, (me // 2) % 4, me % 2]).astype(jnp.int32)
    ends = jnp.stack([slab == 0, slab == lax.axis_size("gz") - 1]).astype(F32)
    real = jnp.concatenate([ends, series_coeffs[0]])

    start = me * rows
    k_before = lax.dynamic_slice_in_dim(k, jnp.maximum(start - 1, 0), 1)
    k_after = lax.dynamic_slice_in_dim(k, jnp.minimum(start + rows, u.shape[0] - 1), 1)
    k_here = jnp.concatenate(
        [
            jnp.where(me > 0, k_before, 0.0),
            lax.dynamic_slice_in_dim(k, start, rows),
            jnp.where(me < blocks - 1, k_after, 0.0),
        ]
    )
    k_low, k_high = lax.ppermute(k_here, "gz", UP), lax.ppermute(k_here, "gz", DOWN)

    n, up, down, own = next_terms(real, u, k, p, blocks)
    low, high = lax.ppermute(up, "gz", UP), lax.ppermute(down, "gz", DOWN)

    d_other, v_other = series(place, real, n, k, u, cos, sin, blocks, 1)
    d_came, v_came = lax.ppermute(d_other, "tm", SIBLING), lax.ppermute(v_other, "tm", SIBLING)
    d_same, v_same = series(place, real, n, k, u, cos, sin, blocks, 0)
    d = z_then_y(d_same + d_came)
    v = y_then_z(v_same + v_came)

    e_other, e_same = jumps(place, real, own, low, high, blocks)
    e = y_then_z(e_same + lax.ppermute(e_other, "tm", SIBLING))
    e_low, e_high = lax.ppermute(e[1], "gz", UP), lax.ppermute(e[0], "gz", DOWN)

    d, v = mend(real, d, v, e, e_low, e_high, k_here, k_low, k_high)
    return unpacked(d), unpacked(v)


def solution(mesh):
    return jax.shard_map(
        local,
        mesh=mesh,
        in_specs=(
            P("tm", None, "gz", None),
            P("tm", None, "gz", None),
            P("tm", None, "gz", None),
            P("tm", None, "gz", None),
            P(None, "gz", None),
            P("tm", None),
        ),
        out_specs=(P("tm", "gz", None), P("tm", "gz", None)),
        check_vma=False,
    )
```

```python
import jax
import jax.numpy as jnp
from jax import lax
from jax.experimental import pallas as pl
from jax.experimental.pallas import tpu as pltpu
from jax.sharding import PartitionSpec as P

CHIPS = 8
GROUP = 16
PLANES = ((3, 0), (0, 1), (0, 0), (3, 1))
MIB = 1024 * 1024
F32 = jnp.float32


def packed(cells):
    x = cells.shape[0]
    return cells.reshape(x, 4, 4, 128).transpose(0, 2, 1, 3).reshape(x, 2, 8, 128)


def unpacked(cells):
    x = cells.shape[0]
    return cells.reshape(x, 4, 4, 128).transpose(0, 2, 1, 3).reshape(x, 4, 512)


def roll(cells, shift):
    return pltpu.roll(cells, shift % 8, 1)


def places(n):
    sub = lax.broadcasted_iota(jnp.int32, (n, 8, 128), 1)
    return sub, lax.rem(sub, 4), lax.broadcasted_iota(jnp.int32, (n, 8, 128), 2)


def spread(field, speed, row, n, lower, upper):
    sub, z, lane = places(n)
    first, at_start, at_end = sub < 4, lane == 0, lane == 127
    v = [field[pl.ds(row + 1, n), h] for h in (0, 1)]
    k = [speed[pl.ds(row + 1, n), h] for h in (0, 1)]

    def ahead(a, b):
        ra, rb = pltpu.roll(a, 127, 2), pltpu.roll(b, 127, 2)
        qa, qb = roll(ra, 4), roll(rb, 4)
        return (
            jnp.where(at_end, jnp.where(first, qa, qb), ra),
            jnp.where(at_end, jnp.where(first, qb, 0.0), rb),
        )

    def behind(a, b, edge):
        ra, rb = pltpu.roll(a, 1, 2), pltpu.roll(b, 1, 2)
        qa, qb = roll(ra, 4), roll(rb, 4)
        return (
            jnp.where(at_start, jnp.where(first, edge, qa), ra),
            jnp.where(at_start, jnp.where(first, qa, qb), rb),
        )

    v_y, k_y = ahead(*v), ahead(*k)
    f_y = [(k[h] + k_y[h]) * (v_y[h] - v[h]) for h in (0, 1)]
    b_y = behind(*f_y, k[0] * v[0])
    out = []
    for h in (0, 1):
        kv = k[h] * v[h]
        f_z = jnp.where(z == 3, -upper * kv, (k[h] + roll(k[h], -1)) * (roll(v[h], -1) - v[h]))
        b_z = jnp.where(z == 0, lower * kv, roll(f_z, 1))
        f_x = (k[h] + speed[pl.ds(row + 2, n), h]) * (field[pl.ds(row + 2, n), h] - v[h])
        b_x = (k[h] + speed[pl.ds(row, n), h]) * (v[h] - field[pl.ds(row, n), h])
        out.append((f_x - b_x) + (f_y[h] - b_y[h]) + (f_z - b_z))
    return v, out


def widen(scratch, main, before, after, block, blocks):
    rows = main.shape[0]
    scratch[pl.ds(1, rows)] = main[...]
    scratch[pl.ds(0, 1)] = jnp.where(block > 0, before[...], 0.0)
    scratch[pl.ds(rows + 1, 1)] = jnp.where(block < blocks - 1, after[...], 0.0)


def series_kernel(place, real, u, k, p, cos, sin, d_other, d_same, v_other, v_same, n_up, n_down, n_low, n_high,
                  us, ks, ns, ds, vs, fx, fy, fw, fz, fm, planes, in_sem, out_sem, plane_sem):
    cells = u.shape[0] // 16
    rows = cells // CHIPS
    half_rows = rows // 2
    lower, upper, c0, c1, c2, c3 = (real[i] for i in range(6))
    sub = lax.broadcasted_iota(jnp.int32, (8, 128), 0)
    lane = lax.broadcasted_iota(jnp.int32, (8, 128), 1)
    z = lax.rem(sub, 4)
    first, at_start, at_end = sub < 4, lane == 0, lane == 127
    open_up, open_down = jnp.where(z == 3, 0.0, 1.0), jnp.where(z == 0, 0.0, 1.0)
    y_first, y_last = jnp.logical_and(first, at_start), jnp.logical_and(jnp.logical_not(first), at_end)
    outer = jnp.where(z == 0, lower, 0.0) + jnp.where(z == 3, upper, 0.0)

    def arrays():
        return ((u, us, 16), (k, ks, 16), (p, ns, 16), (cos, ds, 0), (sin, vs, 0))

    def loads(c, which):
        return [
            pltpu.make_async_copy(a.at[pl.ds(c * rows * 16, rows * 16)], b.at[pl.ds(c * rows * 16 + off, rows * 16)], in_sem.at[i, c])
            for i, (a, b, off) in enumerate(arrays()) if i in which
        ]

    for c in range(CHIPS):
        for copy in loads(c, (0, 1, 2)):
            copy.start()
        if c:
            for copy in loads(c - 1, (3, 4)):
                copy.start()
    for copy in loads(CHIPS - 1, (3, 4)):
        copy.start()
    nothing = jnp.zeros((16, 128), F32)
    fx[0:16] = nothing
    fz[0:16] = nothing
    for ref in (us, ks, ns):
        ref[0:16] = nothing
        ref[(cells + 1) * 16 : (cells + 2) * 16] = nothing

    def at(ref, row, by=0):
        return ref[pl.ds(row + by, 8), :]

    def ahead(ref, row, here):
        return pltpu.roll(jnp.where(at_start, at(ref, row, 4), here), 127, 1)

    def behind(ref, row, here):
        return pltpu.roll(jnp.where(at_end, at(ref, row, -4), here), 1, 1)

    def up(here):
        return pltpu.roll(here, 7, 0)

    def down(here):
        return pltpu.roll(here, 1, 0)

    def first_pass(c):
        def step(i, carry):
            start = (c * rows + i * GROUP + 1) * 16
            kk, uu, kx = {}, {}, {}

            def center(seen, ref, g, h):
                if (g, h) not in seen:
                    seen[g, h] = at(ref, start + g * 16 + h * 8)
                return seen[g, h]

            for h in (0, 1):
                kx[-1, h] = center(kk, ks, -1, h) + center(kk, ks, 0, h)
            for g in range(GROUP):
                for h in (0, 1):
                    row = start + g * 16 + h * 8
                    k0 = center(kk, ks, g, h)
                    kx[g, h] = k0 + center(kk, ks, g + 1, h)
                    ky, kw = k0 + ahead(ks, row, k0), k0 + behind(ks, row, k0)
                    if h == 0:
                        face_w = jnp.where(y_first, k0, kw)
                        face_y, kw = ky, jnp.where(y_first, 0.0, kw)
                    else:
                        face_y = jnp.where(y_last, k0, ky)
                        face_w, ky = kw, jnp.where(y_last, 0.0, ky)
                    kz, kv = (k0 + up(k0)) * open_up, (k0 + down(k0)) * open_down
                    mid = 24.0 - (((kx[g, h] + kx[g - 1, h]) + (face_y + face_w)) + ((kz + kv) + outer * k0))
                    for ref, value in ((fx, kx[g, h]), (fy, ky), (fw, kw), (fz, kz), (fm, mid)):
                        ref[pl.ds(row, 8), :] = value
                    v = center(uu, us, g, h)
                    out = (kx[g, h] * center(uu, us, g + 1, h) + kx[g - 1, h] * center(uu, us, g - 1, h)) + (kz * up(v) + kv * down(v))
                    out = out + (ky * ahead(us, row, v) + kw * behind(us, row, v)) + mid * v
                    ns[pl.ds(row, 8), :] = out * (-1.0 / 12.0) - at(ns, row)
            return carry

        lax.fori_loop(0, rows // GROUP, step, 0)

        def gather(i, carry):
            for b in range(2):
                x = c * rows + i * 16 + b * 8
                for j, (zz, h) in enumerate(PLANES):
                    for q in (0, 1):
                        planes[j, pl.ds(x, 8), q * 128 : (q + 1) * 128] = ns[pl.ds((x + 1) * 16 + h * 8 + q * 4 + zz, 8, stride=16), :]
            return carry

        lax.fori_loop(0, rows // 16, gather, 0)

    def second_pass(c):
        def step(i, carry):
            start = (c * rows + i * GROUP + 1) * 16
            nn, kx = {}, {}

            def center(seen, ref, g, h):
                if (g, h) not in seen:
                    seen[g, h] = at(ref, start + g * 16 + h * 8)
                return seen[g, h]

            for g in range(GROUP):
                for h in (0, 1):
                    row = start + g * 16 + h * 8
                    v = center(nn, ns, g, h)
                    kz = at(fz, row)
                    out = center(kx, fx, g, h) * center(nn, ns, g + 1, h) + center(kx, fx, g - 1, h) * center(nn, ns, g - 1, h)
                    out = out + (kz * up(v) + down(kz) * down(v))
                    out = out + (at(fy, row) * ahead(ns, row, v) + at(fw, row) * behind(ns, row, v)) + at(fm, row) * v
                    final = out * (-1.0 / 12.0) - at(us, row)
                    ds[pl.ds(row - 16, 8), :] = at(ds, row, -16) + c0 * v + c1 * final
                    vs[pl.ds(row - 16, 8), :] = at(vs, row, -16) + c2 * v + c3 * final
            return carry

        lax.fori_loop(0, rows // GROUP, step, 0)

    def plane_stores(c):
        here = pl.ds(c * rows, rows)
        return [
            pltpu.make_async_copy(planes.at[j, here], out.at[here], plane_sem.at[j, c])
            for j, out in enumerate((n_up, n_down, n_low, n_high))
        ]

    def stores(c, core, same):
        way = 1 - 2 * core
        turn = lax.rem(way * (lax.rem(c, 4) - place[1]) + 8, 4)
        side = lax.rem(c // 4 + place[0], 2)
        here = pl.ds((c * rows + core * half_rows) * 16, half_rows * 16)
        d_to, v_to = (d_same, v_same) if same else (d_other, v_other)
        return [
            pltpu.make_async_copy(ds.at[here], d_to.at[side * 4 + turn], out_sem.at[0, core, c]),
            pltpu.make_async_copy(vs.at[here], v_to.at[turn * 2 + side], out_sem.at[1, core, c]),
        ]

    def chunk(c, carry):
        @pl.when(c < CHIPS)
        def _():
            @pl.when(c == 0)
            def _():
                for copy in loads(c, (0, 1, 2)):
                    copy.wait()

            @pl.when(c + 1 < CHIPS)
            def _():
                for copy in loads(c + 1, (0, 1, 2)):
                    copy.wait()

            first_pass(c)
            for copy in plane_stores(c):
                copy.start()

        @pl.when(c > 0)
        def _():
            for copy in loads(c - 1, (3, 4)):
                copy.wait()
            second_pass(c - 1)
            for core in (0, 1):
                for same in (True, False):
                    @pl.when((place[2] == core) == same)
                    def _():
                        for copy in stores(c - 1, core, same):
                            copy.start()

        return carry

    lax.fori_loop(0, CHIPS + 1, chunk, 0)

    def end(c, carry):
        for copy in plane_stores(c):
            copy.wait()
        for core in (0, 1):
            for copy in stores(c, core, True):
                copy.wait()
        return carry

    lax.fori_loop(0, CHIPS, end, 0)

def mend_kernel(real, d, v, e, e_low, e_high, k, k_low, k_high, d_out, v_out, ds, vs):
    rows = d.shape[0]
    lower, upper = real[0], real[1]
    wide = rows + 2
    z = places(wide)[1]
    factor = []
    for h in (0, 1):
        below = (1.0 - lower) * (k[:, h] + roll(k_low[:, h], -3))
        above = (1.0 - upper) * (k[:, h] + roll(k_high[:, h], 3))
        factor.append(jnp.where(z == 0, below, jnp.where(z == 3, -above, 0.0)) * (1.0 / 12.0))
    from_low = [e[0], e_low[...]]
    from_high = [e_high[...], e[1]]
    direct = []
    for field, slot in ((ds, 0), (vs, 2)):
        for h in (0, 1):
            a = jnp.where(z == 0, roll(from_low[h], -slot), roll(from_high[h], 3 - slot))
            b = jnp.where(z == 0, roll(from_low[h], -slot - 1), roll(from_high[h], 2 - slot))
            w = factor[h] * a
            field[:, h] = w
            direct.append((factor[h] * b + 2.0 * jnp.abs(factor[h]) * w)[1 : rows + 1])
    for field, given, out, direct_of in ((ds, d, d_out, direct[:2]), (vs, v, v_out, direct[2:])):
        w, outflow = spread(field, k, 0, rows, lower, upper)
        for h in (0, 1):
            out[:, h] = given[:, h] + direct_of[h] - outflow[h] * (1.0 / 12.0) - 2.0 * w[h]


def planes_kernel(u, *refs):
    outs, (us, planes, in_sem, out_sem) = refs[:4], refs[4:]
    cells = u.shape[0] // 16
    rows = cells // CHIPS

    def load(c):
        here = pl.ds(c * rows * 16, rows * 16)
        return pltpu.make_async_copy(u.at[here], us.at[here], in_sem.at[c])

    def stores(c):
        here = pl.ds(c * rows, rows)
        return [pltpu.make_async_copy(planes.at[j, here], out.at[here], out_sem.at[j, c]) for j, out in enumerate(outs)]

    for c in range(CHIPS):
        load(c).start()

    def chunk(c, carry):
        load(c).wait()
        for i in range(rows // 8):
            x = c * rows + i * 8
            for j, (z, h) in enumerate(PLANES):
                for q in (0, 1):
                    planes[j, pl.ds(x, 8), q * 128 : (q + 1) * 128] = us[pl.ds(x * 16 + h * 8 + q * 4 + z, 8, stride=16), :]
        for copy in stores(c):
            copy.start()
        return carry

    lax.fori_loop(0, CHIPS, chunk, 0)

    def end(c, carry):
        for copy in stores(c):
            copy.wait()
        return carry

    lax.fori_loop(0, CHIPS, end, 0)


def jumps_kernel(place, real, *refs):
    ins, other, same, es, buffers, in_sem, out_sem = refs[:8], *refs[8:]
    cells = ins[0].shape[0]
    parts = 2 * CHIPS
    rows = cells // parts
    chunks = 4
    size = cells // chunks
    c0, c1, c2, c3 = (real[2 + i] for i in range(4))

    def loads(c):
        here = pl.ds(c * size, size)
        return [pltpu.make_async_copy(a.at[here], buffers.at[j, here], in_sem.at[j, c]) for j, a in enumerate(ins)]

    def stores(d, is_same):
        chip, core = d // 2, d % 2
        way = 1 - 2 * core
        slot = lax.rem(way * (chip % 4 - place[1]) + 8, 4) * 2 + lax.rem(chip // 4 + place[0], 2)
        here = pl.ds(d * rows * 8, (rows + 2) * 8)
        to = same if is_same else other
        return [pltpu.make_async_copy(es.at[h, here], to.at[slot, h], out_sem.at[h, d]) for h in (0, 1)]

    def send(d):
        for is_same in (True, False):
            @pl.when((place[2] == d % 2) == is_same)
            def _():
                for copy in stores(d, is_same):
                    copy.start()

    for c in range(chunks):
        for copy in loads(c):
            copy.start()
    nothing = jnp.zeros((8, 128), F32)
    for h in (0, 1):
        es[h, 0:8] = nothing
        es[h, (cells + 1) * 8 : (cells + 2) * 8] = nothing
    sent = 0
    for c in range(chunks):
        for copy in loads(c):
            copy.wait()

        def step(i, carry):
            x = c * size + i * 8
            for h in (0, 1):
                for q in (0, 1):
                    u_own, n_own, u_near, n_near = (buffers[4 * h + j, pl.ds(x, 8), q * 128 : (q + 1) * 128] for j in range(4))
                    du, dn = (u_own - u_near, n_own - n_near) if h == 0 else (u_near - u_own, n_near - n_own)
                    for m, value in enumerate((c1 * du, c0 * du + c1 * dn, c3 * du, c2 * du + c3 * dn)):
                        es[h, pl.ds((x + 1) * 8 + q * 4 + m, 8, stride=8), :] = value
            return carry

        lax.fori_loop(0, size // 8, step, 0, unroll=2)
        ready = parts if c == chunks - 1 else (c + 1) * size // rows - 1
        for d in range(sent, ready):
            send(d)
        sent = ready
    for d in range(parts):
        for copy in stores(d, True):
            copy.wait()


ANYWHERE = pl.BlockSpec(memory_space=pl.ANY)
SMEM = pl.BlockSpec(memory_space=pltpu.SMEM)


def params(mib):
    return pltpu.CompilerParams(vmem_limit_bytes=mib * MIB)


def cost(mib):
    return pl.CostEstimate(flops=0, bytes_accessed=mib * MIB, transcendentals=0)


def flat(cells):
    return cells.reshape(-1, 128)


def planes_of(u):
    cells = u.shape[0] // 16
    return pl.pallas_call(
        planes_kernel,
        out_shape=(jax.ShapeDtypeStruct((cells, 256), F32),) * 4,
        in_specs=[ANYWHERE],
        out_specs=(ANYWHERE,) * 4,
        scratch_shapes=[
            pltpu.VMEM((cells * 16, 128), F32),
            pltpu.VMEM((4, cells, 256), F32),
            pltpu.SemaphoreType.DMA((CHIPS,)),
            pltpu.SemaphoreType.DMA((4, CHIPS)),
        ],
        compiler_params=params(48),
        cost_estimate=cost(6),
    )(u)


def series(place, real, u, k, p, cos, sin):
    cells = u.shape[0] // 16
    share = jax.ShapeDtypeStruct((CHIPS, cells, 128), F32)
    plane = jax.ShapeDtypeStruct((cells, 256), F32)
    wide = pltpu.VMEM(((cells + 2) * 16, 128), F32)
    exact = pltpu.VMEM((cells * 16, 128), F32)
    return pl.pallas_call(
        series_kernel,
        out_shape=(share,) * 4 + (plane,) * 4,
        in_specs=[SMEM, SMEM] + [ANYWHERE] * 5,
        out_specs=(ANYWHERE,) * 8,
        scratch_shapes=[wide, wide, wide, exact, exact, wide, wide, wide, wide, wide]
        + [
            pltpu.VMEM((4, cells, 256), F32),
            pltpu.SemaphoreType.DMA((5, CHIPS)),
            pltpu.SemaphoreType.DMA((2, 2, CHIPS)),
            pltpu.SemaphoreType.DMA((4, CHIPS)),
        ],
        compiler_params=params(56),
        cost_estimate=cost(45),
    )(place, real, u, k, p, cos, sin)


def jumps(place, real, below, above):
    cells = below[0].shape[0]
    rows = cells // (2 * CHIPS)
    shape = jax.ShapeDtypeStruct((CHIPS, 2, (rows + 2) * 8, 128), F32)
    return pl.pallas_call(
        jumps_kernel,
        out_shape=(shape, shape),
        in_specs=[SMEM, SMEM] + [ANYWHERE] * 8,
        out_specs=(ANYWHERE,) * 2,
        scratch_shapes=[
            pltpu.VMEM((2, (cells + 2) * 8, 128), F32),
            pltpu.VMEM((8, cells, 256), F32),
            pltpu.SemaphoreType.DMA((8, 4)),
            pltpu.SemaphoreType.DMA((2, 2 * CHIPS)),
        ],
        compiler_params=params(24),
        cost_estimate=cost(9),
    )(place, real, *below, *above)


def mend(real, d, v, e, e_low, e_high, k, k_low, k_high):
    shape = jax.ShapeDtypeStruct(d.shape, F32)
    whole = pl.BlockSpec(memory_space=pltpu.VMEM)
    return pl.pallas_call(
        mend_kernel,
        out_shape=(shape, shape),
        in_specs=[SMEM] + [whole] * 8,
        out_specs=(whole, whole),
        scratch_shapes=[pltpu.VMEM(k.shape, F32)] * 2,
        compiler_params=params(16),
        cost_estimate=cost(4),
    )(real, d, v, e, e_low, e_high, k, k_low, k_high)


CELL = (2, 8, 128)
COUNT = 16
SLABS = 8


def along_y(sign):
    def goal(i):
        z, y, core = i // 8, (i // 2) % 4, i % 2
        return z * 8 + ((y + sign * (1 - 2 * core)) % 4) * 2 + core

    return [(i, goal(i)) for i in range(COUNT)]


FORTH, BACK = along_y(1), along_y(-1)
ACROSS = [(i, i ^ 8) for i in range(COUNT)]
SIBLING = [(i, i ^ 1) for i in range(COUNT)]
UP = [(i, i + 1) for i in range(SLABS - 1)]
DOWN = [(i + 1, i) for i in range(SLABS - 1)]


def ring(two, one, back, own):
    relayed = lax.ppermute(two, "tm", FORTH)
    direct = lax.ppermute(back, "tm", BACK)
    rest = lax.ppermute(one + relayed, "tm", FORTH)
    return own + direct + rest


def y_then_z(cells):
    cells = cells.reshape(4, 2, *cells.shape[1:])
    mine = ring(cells[2], cells[1], cells[3], cells[0])
    return mine[0] + lax.ppermute(mine[1], "tm", ACROSS)


def z_then_y(cells):
    half = cells.shape[0] // 2
    mine = cells[:half] + lax.ppermute(cells[half:], "tm", ACROSS)
    return ring(mine[2], mine[1], mine[3], mine[0])


def local(prev_term, last_term, cos_sum, sin_sum, speed_sq, series_coeffs):
    u, p, k = packed(last_term[0]), packed(prev_term[0]), packed(speed_sq)
    cos, sin = packed(cos_sum[0]), packed(sin_sum[0])
    blocks = lax.axis_size("tm")
    rows = u.shape[0] // blocks
    me, slab = lax.axis_index("tm"), lax.axis_index("gz")
    place = jnp.stack([me // 8, (me // 2) % 4, me % 2]).astype(jnp.int32)
    ends = jnp.stack([slab == 0, slab == lax.axis_size("gz") - 1]).astype(F32)
    real = jnp.concatenate([ends, series_coeffs[0]])

    start = me * rows
    k_before = lax.dynamic_slice_in_dim(k, jnp.maximum(start - 1, 0), 1)
    k_after = lax.dynamic_slice_in_dim(k, jnp.minimum(start + rows, u.shape[0] - 1), 1)
    k_here = jnp.concatenate(
        [
            jnp.where(me > 0, k_before, 0.0),
            lax.dynamic_slice_in_dim(k, start, rows),
            jnp.where(me < blocks - 1, k_after, 0.0),
        ]
    )
    k_low, k_high = lax.ppermute(k_here, "gz", UP), lax.ppermute(k_here, "gz", DOWN)

    u_flat = flat(u)
    u_up, u_down, u_low, u_high = planes_of(u_flat)
    u_below, u_above = lax.ppermute(u_up, "gz", UP), lax.ppermute(u_down, "gz", DOWN)

    d_other, d_same, v_other, v_same, n_up, n_down, n_low, n_high = series(place, real, u_flat, flat(k), flat(p), flat(cos), flat(sin))
    n_below, n_above = lax.ppermute(n_up, "gz", UP), lax.ppermute(n_down, "gz", DOWN)
    d = z_then_y(d_same + lax.ppermute(d_other, "tm", SIBLING)).reshape(rows, *CELL)
    v = y_then_z(v_same + lax.ppermute(v_other, "tm", SIBLING)).reshape(rows, *CELL)

    e_other, e_same = jumps(place, real, (u_low, n_low, u_below, n_below), (u_high, n_high, u_above, n_above))
    e = y_then_z(e_same + lax.ppermute(e_other, "tm", SIBLING)).reshape(2, rows + 2, 8, 128)
    e_low, e_high = lax.ppermute(e[1], "gz", UP), lax.ppermute(e[0], "gz", DOWN)

    d, v = mend(real, d, v, e, e_low, e_high, k_here, k_low, k_high)
    return unpacked(d), unpacked(v)


def solution(mesh):
    return jax.shard_map(
        local,
        mesh=mesh,
        in_specs=(
            P("tm", None, "gz", None),
            P("tm", None, "gz", None),
            P("tm", None, "gz", None),
            P("tm", None, "gz", None),
            P(None, "gz", None),
            P("tm", None),
        ),
        out_specs=(P("tm", "gz", None), P("tm", "gz", None)),
        check_vma=False,
    )
```

```python
import jax
import jax.numpy as jnp
from jax import lax
from jax.experimental import pallas as pl
from jax.experimental.pallas import tpu as pltpu
from jax.sharding import PartitionSpec as P

CHIPS = 8
COUNT = 16
SLABS = 8
GROUP = 16
KEPT = ((0, 0), (3, 1))
MIB = 1024 * 1024
F32 = jnp.float32


def packed(cells):
    x = cells.shape[0]
    return cells.reshape(x, 4, 4, 128).transpose(0, 2, 1, 3).reshape(x, 2, 8, 128)


def unpacked(cells):
    x = cells.shape[0]
    return cells.reshape(x, 4, 4, 128).transpose(0, 2, 1, 3).reshape(x, 4, 512)


def roll(cells, shift):
    return pltpu.roll(cells, shift % 8, 1)


def places(n):
    sub = lax.broadcasted_iota(jnp.int32, (n, 8, 128), 1)
    return sub, lax.rem(sub, 4), lax.broadcasted_iota(jnp.int32, (n, 8, 128), 2)


def spread(field, speed, row, n, lower, upper):
    sub, z, lane = places(n)
    first, at_start, at_end = sub < 4, lane == 0, lane == 127
    v = [field[pl.ds(row + 1, n), h] for h in (0, 1)]
    k = [speed[pl.ds(row + 1, n), h] for h in (0, 1)]

    def ahead(a, b):
        ra, rb = pltpu.roll(a, 127, 2), pltpu.roll(b, 127, 2)
        qa, qb = roll(ra, 4), roll(rb, 4)
        return (
            jnp.where(at_end, jnp.where(first, qa, qb), ra),
            jnp.where(at_end, jnp.where(first, qb, 0.0), rb),
        )

    def behind(a, b, edge):
        ra, rb = pltpu.roll(a, 1, 2), pltpu.roll(b, 1, 2)
        qa, qb = roll(ra, 4), roll(rb, 4)
        return (
            jnp.where(at_start, jnp.where(first, edge, qa), ra),
            jnp.where(at_start, jnp.where(first, qa, qb), rb),
        )

    v_y, k_y = ahead(*v), ahead(*k)
    f_y = [(k[h] + k_y[h]) * (v_y[h] - v[h]) for h in (0, 1)]
    b_y = behind(*f_y, k[0] * v[0])
    out = []
    for h in (0, 1):
        kv = k[h] * v[h]
        f_z = jnp.where(z == 3, -upper * kv, (k[h] + roll(k[h], -1)) * (roll(v[h], -1) - v[h]))
        b_z = jnp.where(z == 0, lower * kv, roll(f_z, 1))
        f_x = (k[h] + speed[pl.ds(row + 2, n), h]) * (field[pl.ds(row + 2, n), h] - v[h])
        b_x = (k[h] + speed[pl.ds(row, n), h]) * (v[h] - field[pl.ds(row, n), h])
        out.append((f_x - b_x) + (f_y[h] - b_y[h]) + (f_z - b_z))
    return v, out


def widen(scratch, main, before, after, block, blocks):
    rows = main.shape[0]
    scratch[pl.ds(1, rows)] = main[...]
    scratch[pl.ds(0, 1)] = jnp.where(block > 0, before[...], 0.0)
    scratch[pl.ds(rows + 1, 1)] = jnp.where(block < blocks - 1, after[...], 0.0)


def series_kernel(coeffs, u, k, p, cos, sin, d_other, d_same, v_other, v_same, below, above,
                  us, ks, ns, ds, vs, fx, fy, fw, fz, fm, planes, in_sem, out_sem, plane_sem):
    cells = u.shape[0] // 16
    rows = cells // CHIPS
    half_rows = rows // 2
    my_z, my_y, my_core = where_am_i()
    slab = lax.axis_index("gz")
    lower, upper = jnp.where(slab == 0, 1.0, 0.0), jnp.where(slab == SLABS - 1, 1.0, 0.0)
    c0, c1, c2, c3 = (coeffs[0, i] for i in range(4))
    sub = lax.broadcasted_iota(jnp.int32, (8, 128), 0)
    lane = lax.broadcasted_iota(jnp.int32, (8, 128), 1)
    z = lax.rem(sub, 4)
    first, at_start, at_end = sub < 4, lane == 0, lane == 127
    open_up, open_down = jnp.where(z == 3, 0.0, 1.0), jnp.where(z == 0, 0.0, 1.0)
    y_first, y_last = jnp.logical_and(first, at_start), jnp.logical_and(jnp.logical_not(first), at_end)
    outer = jnp.where(z == 0, lower, 0.0) + jnp.where(z == 3, upper, 0.0)

    def arrays():
        return ((u, us, 16), (k, ks, 16), (p, ns, 16), (cos, ds, 0), (sin, vs, 0))

    def loads(c, which):
        return [
            pltpu.make_async_copy(a.at[pl.ds(c * rows * 16, rows * 16)], b.at[pl.ds(c * rows * 16 + off, rows * 16)], in_sem.at[i, c])
            for i, (a, b, off) in enumerate(arrays()) if i in which
        ]

    for c in range(CHIPS):
        for copy in loads(c, (0, 1, 2)):
            copy.start()
        if c:
            for copy in loads(c - 1, (3, 4)):
                copy.start()
    for copy in loads(CHIPS - 1, (3, 4)):
        copy.start()
    nothing = jnp.zeros((16, 128), F32)
    fx[0:16] = nothing
    fz[0:16] = nothing
    for ref in (us, ks, ns):
        ref[0:16] = nothing
        ref[(cells + 1) * 16 : (cells + 2) * 16] = nothing

    def at(ref, row, by=0):
        return ref[pl.ds(row + by, 8), :]

    def ahead(ref, row, here):
        return pltpu.roll(jnp.where(at_start, at(ref, row, 4), here), 127, 1)

    def behind(ref, row, here):
        return pltpu.roll(jnp.where(at_end, at(ref, row, -4), here), 1, 1)

    def up(here):
        return pltpu.roll(here, 7, 0)

    def down(here):
        return pltpu.roll(here, 1, 0)

    def first_pass(c):
        def step(i, carry):
            start = (c * rows + i * GROUP + 1) * 16
            kk, uu, kx = {}, {}, {}

            def center(seen, ref, g, h):
                if (g, h) not in seen:
                    seen[g, h] = at(ref, start + g * 16 + h * 8)
                return seen[g, h]

            for h in (0, 1):
                kx[-1, h] = center(kk, ks, -1, h) + center(kk, ks, 0, h)
            for g in range(GROUP):
                for h in (0, 1):
                    row = start + g * 16 + h * 8
                    k0 = center(kk, ks, g, h)
                    kx[g, h] = k0 + center(kk, ks, g + 1, h)
                    ky, kw = k0 + ahead(ks, row, k0), k0 + behind(ks, row, k0)
                    if h == 0:
                        face_w = jnp.where(y_first, k0, kw)
                        face_y, kw = ky, jnp.where(y_first, 0.0, kw)
                    else:
                        face_y = jnp.where(y_last, k0, ky)
                        face_w, ky = kw, jnp.where(y_last, 0.0, ky)
                    kz, kv = (k0 + up(k0)) * open_up, (k0 + down(k0)) * open_down
                    mid = 24.0 - (((kx[g, h] + kx[g - 1, h]) + (face_y + face_w)) + ((kz + kv) + outer * k0))
                    for ref, value in ((fx, kx[g, h]), (fy, ky), (fw, kw), (fz, kz), (fm, mid)):
                        ref[pl.ds(row, 8), :] = value
                    v = center(uu, us, g, h)
                    out = (kx[g, h] * center(uu, us, g + 1, h) + kx[g - 1, h] * center(uu, us, g - 1, h)) + (kz * up(v) + kv * down(v))
                    out = out + (ky * ahead(us, row, v) + kw * behind(us, row, v)) + mid * v
                    ns[pl.ds(row, 8), :] = out * (-1.0 / 12.0) - at(ns, row)
            return carry

        lax.fori_loop(0, rows // GROUP, step, 0)

        def gather(i, carry):
            for b in range(2):
                x = c * rows + i * 16 + b * 8
                for j, (z, h) in enumerate(KEPT):
                    for f, ref in enumerate((us, ns)):
                        for q in (0, 1):
                            lanes = pl.ds(f * 256 + q * 128, 128)
                            planes[j, pl.ds(x, 8), lanes] = ref[pl.ds((x + 1) * 16 + h * 8 + q * 4 + z, 8, stride=16), :]
            return carry

        lax.fori_loop(0, rows // 16, gather, 0)

    def second_pass(c):
        def step(i, carry):
            start = (c * rows + i * GROUP + 1) * 16
            nn, kx = {}, {}

            def center(seen, ref, g, h):
                if (g, h) not in seen:
                    seen[g, h] = at(ref, start + g * 16 + h * 8)
                return seen[g, h]

            for g in range(GROUP):
                for h in (0, 1):
                    row = start + g * 16 + h * 8
                    v = center(nn, ns, g, h)
                    kz = at(fz, row)
                    out = center(kx, fx, g, h) * center(nn, ns, g + 1, h) + center(kx, fx, g - 1, h) * center(nn, ns, g - 1, h)
                    out = out + (kz * up(v) + down(kz) * down(v))
                    out = out + (at(fy, row) * ahead(ns, row, v) + at(fw, row) * behind(ns, row, v)) + at(fm, row) * v
                    final = out * (-1.0 / 12.0) - at(us, row)
                    ds[pl.ds(row - 16, 8), :] = at(ds, row, -16) + c0 * v + c1 * final
                    vs[pl.ds(row - 16, 8), :] = at(vs, row, -16) + c2 * v + c3 * final
            return carry

        lax.fori_loop(0, rows // GROUP, step, 0)

    def plane_stores(c):
        here = pl.ds(c * rows, rows)
        return [
            pltpu.make_async_copy(planes.at[j, here], out.at[here], plane_sem.at[j, c])
            for j, out in enumerate((below, above))
        ]

    def stores(c, core, same):
        way = 1 - 2 * core
        turn = lax.rem(way * (lax.rem(c, 4) - my_y) + 8, 4)
        side = lax.rem(c // 4 + my_z, 2)
        here = pl.ds((c * rows + core * half_rows) * 16, half_rows * 16)
        d_to, v_to = (d_same, v_same) if same else (d_other, v_other)
        return [
            pltpu.make_async_copy(ds.at[here], d_to.at[side * 4 + turn], out_sem.at[0, core, c]),
            pltpu.make_async_copy(vs.at[here], v_to.at[turn * 2 + side], out_sem.at[1, core, c]),
        ]

    def chunk(c, carry):
        @pl.when(c < CHIPS)
        def _():
            @pl.when(c == 0)
            def _():
                for copy in loads(c, (0, 1, 2)):
                    copy.wait()

            @pl.when(c + 1 < CHIPS)
            def _():
                for copy in loads(c + 1, (0, 1, 2)):
                    copy.wait()

            first_pass(c)
            for copy in plane_stores(c):
                copy.start()

        @pl.when(c > 0)
        def _():
            for copy in loads(c - 1, (3, 4)):
                copy.wait()
            second_pass(c - 1)
            for core in (0, 1):
                for same in (True, False):
                    @pl.when((my_core == core) == same)
                    def _():
                        for copy in stores(c - 1, core, same):
                            copy.start()

        return carry

    lax.fori_loop(0, CHIPS + 1, chunk, 0)

    def end(c, carry):
        for copy in plane_stores(c):
            copy.wait()
        for core in (0, 1):
            for copy in stores(c, core, True):
                copy.wait()
        return carry

    lax.fori_loop(0, CHIPS, end, 0)

def mend_kernel(d, v, e, e_low, e_high, k, k_low, k_high, d_out, v_out, ds, vs):
    rows = d.shape[0]
    slab = lax.axis_index("gz")
    lower, upper = jnp.where(slab == 0, 1.0, 0.0), jnp.where(slab == SLABS - 1, 1.0, 0.0)
    wide = rows + 2
    z = places(wide)[1]
    factor = []
    for h in (0, 1):
        below = (1.0 - lower) * (k[:, h] + roll(k_low[:, h], -3))
        above = (1.0 - upper) * (k[:, h] + roll(k_high[:, h], 3))
        factor.append(jnp.where(z == 0, below, jnp.where(z == 3, -above, 0.0)) * (1.0 / 12.0))
    from_low = [e[0], e_low[...]]
    from_high = [e_high[...], e[1]]
    direct = []
    for field, slot in ((ds, 0), (vs, 2)):
        for h in (0, 1):
            a = jnp.where(z == 0, roll(from_low[h], -slot), roll(from_high[h], 3 - slot))
            b = jnp.where(z == 0, roll(from_low[h], -slot - 1), roll(from_high[h], 2 - slot))
            w = factor[h] * a
            field[:, h] = w
            direct.append((factor[h] * b + 2.0 * jnp.abs(factor[h]) * w)[1 : rows + 1])
    for field, given, out, direct_of in ((ds, d, d_out, direct[:2]), (vs, v, v_out, direct[2:])):
        w, outflow = spread(field, k, 0, rows, lower, upper)
        for h in (0, 1):
            out[:, h] = given[:, h] + direct_of[h] - outflow[h] * (1.0 / 12.0) - 2.0 * w[h]


def where_am_i():
    me = lax.axis_index("tm")
    return me // 8, lax.rem(me // 2, 4), lax.rem(me, 2)


def edge_kernel(u, k, p, up, down, k_here, us, ks, ps, edges, kb, in_sem, out_sem, k_sem):
    cells = u.shape[0] // 16
    rows = cells // CHIPS
    mine = cells // (2 * CHIPS)
    me = lax.axis_index("tm")

    def loads(c):
        here, there = pl.ds(c * rows * 16, rows * 16), pl.ds((c * rows + 1) * 16, rows * 16)
        return [
            pltpu.make_async_copy(u.at[here], us.at[there], in_sem.at[0, c]),
            pltpu.make_async_copy(k.at[here], ks.at[there], in_sem.at[1, c]),
            pltpu.make_async_copy(p.at[here], ps.at[here], in_sem.at[2, c]),
        ]

    def stores(c):
        here = pl.ds(c * rows, rows)
        return [pltpu.make_async_copy(edges.at[j, here], out.at[here], out_sem.at[j, c]) for j, out in enumerate((up, down))]

    own = pltpu.make_async_copy(k.at[pl.ds(me * mine * 16, mine * 16)], kb.at[pl.ds(16, mine * 16)], k_sem.at[0])
    before = pltpu.make_async_copy(k.at[pl.ds(jnp.maximum(me * mine - 1, 0) * 16, 16)], kb.at[pl.ds(0, 16)], k_sem.at[1])
    after = pltpu.make_async_copy(
        k.at[pl.ds(jnp.minimum((me + 1) * mine, cells - 1) * 16, 16)], kb.at[pl.ds((mine + 1) * 16, 16)], k_sem.at[2]
    )
    own.start()
    before.start()
    after.start()
    for c in range(CHIPS):
        for copy in loads(c):
            copy.start()
    nothing = jnp.zeros((16, 128), F32)
    for ref in (us, ks):
        ref[0:16] = nothing
        ref[(cells + 1) * 16 : (cells + 2) * 16] = nothing
    own.wait()
    before.wait()
    after.wait()

    @pl.when(me == 0)
    def _():
        kb[0:16] = nothing

    @pl.when(me == 2 * CHIPS - 1)
    def _():
        kb[(mine + 1) * 16 : (mine + 2) * 16] = nothing

    speeds = pltpu.make_async_copy(kb, k_here, k_sem.at[3])
    speeds.start()
    lane = lax.broadcasted_iota(jnp.int32, (8, 128), 1)
    at_start, at_end = lane == 0, lane == 127

    def shifted(cells_of, yt):
        after = pltpu.roll(cells_of[yt + 1], 127, 1) if yt < 3 else 0.0
        before = pltpu.roll(cells_of[yt - 1], 1, 1) if yt > 0 else 0.0
        here = cells_of[yt]
        return (
            jnp.where(at_end, after, pltpu.roll(here, 127, 1)),
            jnp.where(at_start, before, pltpu.roll(here, 1, 1)),
        )

    def chunk(c, carry):
        @pl.when(c == 0)
        def _():
            for copy in loads(c):
                copy.wait()

        @pl.when(c + 1 < CHIPS)
        def _():
            for copy in loads(c + 1):
                copy.wait()

        def step(i, carry):
            for g in range(4):
                x = c * rows + i * 32 + g * 8
                for j, (z, inner, turns) in enumerate(((3, 2, (0, 1)), (0, 1, (2, 3)))):

                    def at(ref, yt, by=0, zz=z):
                        return ref[pl.ds((x + 1 + by) * 16 + yt * 4 + zz, 8, stride=16), :]

                    near = [yt for yt in range(4) if turns[0] - 1 <= yt <= turns[1] + 1]
                    vs, qs = {yt: at(us, yt) for yt in near}, {yt: at(ks, yt) for yt in near}
                    for yt in turns:
                        v, q = vs[yt], qs[yt]
                        pairs = [*zip(shifted(vs, yt), shifted(qs, yt))]
                        pairs += [(at(us, yt, by), at(ks, yt, by)) for by in (1, -1)]
                        pairs.append((at(us, yt, 0, inner), at(ks, yt, 0, inner)))
                        flows = [(q + q_n) * (v_n - v) for v_n, q_n in pairs]
                        flow = (flows[0] + flows[1]) + (flows[2] + flows[3]) + flows[4]
                        n = flow * (-1.0 / 12.0) - 2.0 * v - ps[pl.ds(x * 16 + yt * 4 + z, 8, stride=16), :]
                        here = (yt - turns[0]) * 128
                        edges[j, pl.ds(x, 8), here : here + 128] = v
                        edges[j, pl.ds(x, 8), here + 256 : here + 384] = n
            return carry

        lax.fori_loop(0, rows // 32, step, 0)
        for copy in stores(c):
            copy.start()
        return carry

    lax.fori_loop(0, CHIPS, chunk, 0)

    def end(c, carry):
        for copy in stores(c):
            copy.wait()
        return carry

    lax.fori_loop(0, CHIPS, end, 0)
    speeds.wait()


def jumps_kernel(coeffs, *refs):
    ins, other, same, es, buffers, in_sem, out_sem = refs[:4], *refs[4:]
    cells = ins[0].shape[0]
    parts = 2 * CHIPS
    rows = cells // parts
    chunks = 4
    size = cells // chunks
    c0, c1, c2, c3 = (coeffs[0, i] for i in range(4))
    my_z, my_y, my_core = where_am_i()

    def loads(c):
        here = pl.ds(c * size, size)
        return [pltpu.make_async_copy(a.at[here], buffers.at[j, here], in_sem.at[j, c]) for j, a in enumerate(ins)]

    def stores(d, is_same):
        chip, core = d // 2, d % 2
        way = 1 - 2 * core
        slot = lax.rem(way * (chip % 4 - my_y) + 8, 4) * 2 + lax.rem(chip // 4 + my_z, 2)
        here = pl.ds(d * rows * 8, (rows + 2) * 8)
        to = same if is_same else other
        return [pltpu.make_async_copy(es.at[h, here], to.at[slot, h], out_sem.at[h, d]) for h in (0, 1)]

    def send(d):
        for is_same in (True, False):
            @pl.when((my_core == d % 2) == is_same)
            def _():
                for copy in stores(d, is_same):
                    copy.start()

    for c in range(chunks):
        for copy in loads(c):
            copy.start()
    nothing = jnp.zeros((8, 128), F32)
    for h in (0, 1):
        es[h, 0:8] = nothing
        es[h, (cells + 1) * 8 : (cells + 2) * 8] = nothing
    sent = 0
    for c in range(chunks):
        for copy in loads(c):
            copy.wait()

        def step(i, carry):
            x = c * size + i * 8
            for h in (0, 1):
                for q in (0, 1):
                    du, dn = (
                        (1 - 2 * h) * (buffers[2 * h, pl.ds(x, 8), at : at + 128] - buffers[2 * h + 1, pl.ds(x, 8), at : at + 128])
                        for at in (q * 128, 256 + q * 128)
                    )
                    for m, value in enumerate((c1 * du, c0 * du + c1 * dn, c3 * du, c2 * du + c3 * dn)):
                        es[h, pl.ds((x + 1) * 8 + q * 4 + m, 8, stride=8), :] = value
            return carry

        lax.fori_loop(0, size // 8, step, 0, unroll=8)
        ready = parts if c == chunks - 1 else (c + 1) * size // rows - 1
        for d in range(sent, ready):
            send(d)
        sent = ready
    for d in range(parts):
        for copy in stores(d, True):
            copy.wait()


ANYWHERE = pl.BlockSpec(memory_space=pl.ANY)
SMEM = pl.BlockSpec(memory_space=pltpu.SMEM)


def params(mib):
    return pltpu.CompilerParams(vmem_limit_bytes=mib * MIB)


def cost(mib):
    return pl.CostEstimate(flops=0, bytes_accessed=mib * MIB, transcendentals=0)


def flat(cells):
    return cells.reshape(-1, 128)


def edges_of(u, k, p):
    cells = u.shape[0] // 16
    mine = cells // (2 * CHIPS)
    wide = pltpu.VMEM(((cells + 2) * 16, 128), F32)
    edge = jax.ShapeDtypeStruct((cells, 512), F32)
    return pl.pallas_call(
        edge_kernel,
        out_shape=(edge, edge, jax.ShapeDtypeStruct(((mine + 2) * 16, 128), F32)),
        in_specs=[ANYWHERE] * 3,
        out_specs=(ANYWHERE,) * 3,
        scratch_shapes=[
            wide,
            wide,
            pltpu.VMEM((cells * 16, 128), F32),
            pltpu.VMEM((2, cells, 512), F32),
            pltpu.VMEM(((mine + 2) * 16, 128), F32),
            pltpu.SemaphoreType.DMA((3, CHIPS)),
            pltpu.SemaphoreType.DMA((2, CHIPS)),
            pltpu.SemaphoreType.DMA((4,)),
        ],
        compiler_params=params(56),
        cost_estimate=cost(16),
    )(u, k, p)


def series(coeffs, u, k, p, cos, sin):
    cells = u.shape[0] // 16
    share = jax.ShapeDtypeStruct((CHIPS, cells, 128), F32)
    plane = jax.ShapeDtypeStruct((cells, 512), F32)
    wide = pltpu.VMEM(((cells + 2) * 16, 128), F32)
    exact = pltpu.VMEM((cells * 16, 128), F32)
    return pl.pallas_call(
        series_kernel,
        out_shape=(share,) * 4 + (plane,) * 2,
        in_specs=[SMEM] + [ANYWHERE] * 5,
        out_specs=(ANYWHERE,) * 6,
        scratch_shapes=[wide, wide, wide, exact, exact, wide, wide, wide, wide, wide]
        + [
            pltpu.VMEM((2, cells, 512), F32),
            pltpu.SemaphoreType.DMA((5, CHIPS)),
            pltpu.SemaphoreType.DMA((2, 2, CHIPS)),
            pltpu.SemaphoreType.DMA((2, CHIPS)),
        ],
        compiler_params=params(56),
        cost_estimate=cost(45),
    )(coeffs, u, k, p, cos, sin)


def jumps(coeffs, below, above):
    cells = below[0].shape[0]
    rows = cells // (2 * CHIPS)
    shape = jax.ShapeDtypeStruct((CHIPS, 2, (rows + 2) * 8, 128), F32)
    return pl.pallas_call(
        jumps_kernel,
        out_shape=(shape, shape),
        in_specs=[SMEM] + [ANYWHERE] * 4,
        out_specs=(ANYWHERE,) * 2,
        scratch_shapes=[
            pltpu.VMEM((2, (cells + 2) * 8, 128), F32),
            pltpu.VMEM((4, cells, 512), F32),
            pltpu.SemaphoreType.DMA((4, 4)),
            pltpu.SemaphoreType.DMA((2, 2 * CHIPS)),
        ],
        compiler_params=params(24),
        cost_estimate=cost(9),
    )(coeffs, *below, *above)


def mend(d, v, e, e_low, e_high, k, k_low, k_high):
    shape = jax.ShapeDtypeStruct(d.shape, F32)
    whole = pl.BlockSpec(memory_space=pltpu.VMEM)
    return pl.pallas_call(
        mend_kernel,
        out_shape=(shape, shape),
        in_specs=[whole] * 8,
        out_specs=(whole, whole),
        scratch_shapes=[pltpu.VMEM(k.shape, F32)] * 2,
        compiler_params=params(16),
        cost_estimate=cost(4),
    )(d, v, e, e_low, e_high, k, k_low, k_high)


CELL = (2, 8, 128)


def along_y(sign):
    def goal(i):
        z, y, core = i // 8, (i // 2) % 4, i % 2
        return z * 8 + ((y + sign * (1 - 2 * core)) % 4) * 2 + core

    return [(i, goal(i)) for i in range(COUNT)]


FORTH, BACK = along_y(1), along_y(-1)
ACROSS = [(i, i ^ 8) for i in range(COUNT)]
SIBLING = [(i, i ^ 1) for i in range(COUNT)]
UP = [(i, i + 1) for i in range(SLABS - 1)]
DOWN = [(i + 1, i) for i in range(SLABS - 1)]


def ring(two, one, back, own):
    relayed = lax.ppermute(two, "tm", FORTH)
    direct = lax.ppermute(back, "tm", BACK)
    rest = lax.ppermute(one + relayed, "tm", FORTH)
    return own + direct + rest


def y_then_z(cells):
    cells = cells.reshape(4, 2, *cells.shape[1:])
    mine = ring(cells[2], cells[1], cells[3], cells[0])
    return mine[0] + lax.ppermute(mine[1], "tm", ACROSS)


def z_then_y(cells):
    half = cells.shape[0] // 2
    mine = cells[:half] + lax.ppermute(cells[half:], "tm", ACROSS)
    return ring(mine[2], mine[1], mine[3], mine[0])


def local(prev_term, last_term, cos_sum, sin_sum, speed_sq, series_coeffs):
    u, p, k = flat(packed(last_term[0])), flat(packed(prev_term[0])), flat(packed(speed_sq))
    cos, sin = flat(packed(cos_sum[0])), flat(packed(sin_sum[0]))
    rows = last_term.shape[1] // COUNT

    up, down, k_here = edges_of(u, k, p)
    from_below, from_above = lax.ppermute(up, "gz", UP), lax.ppermute(down, "gz", DOWN)
    k_low, k_high = lax.ppermute(k_here, "gz", UP), lax.ppermute(k_here, "gz", DOWN)

    d_other, d_same, v_other, v_same, below, above = series(series_coeffs, u, k, p, cos, sin)
    d_sum = d_same + lax.ppermute(d_other, "tm", SIBLING)
    v_sum = v_same + lax.ppermute(v_other, "tm", SIBLING)
    _, _, from_below, from_above, k_low, k_high = lax.optimization_barrier(
        (d_sum, v_sum, from_below, from_above, k_low, k_high)
    )
    d = z_then_y(d_sum).reshape(rows, *CELL)
    v = y_then_z(v_sum).reshape(rows, *CELL)

    e_other, e_same = jumps(series_coeffs, (below, from_below), (above, from_above))
    e = y_then_z(e_same + lax.ppermute(e_other, "tm", SIBLING)).reshape(2, rows + 2, 8, 128)
    e_low, e_high = lax.ppermute(e[1], "gz", UP), lax.ppermute(e[0], "gz", DOWN)

    k_here, k_low, k_high = (a.reshape(rows + 2, *CELL) for a in (k_here, k_low, k_high))
    d, v = mend(d, v, e, e_low, e_high, k_here, k_low, k_high)
    return unpacked(d), unpacked(v)


def solution(mesh):
    return jax.shard_map(
        local,
        mesh=mesh,
        in_specs=(
            P("tm", None, "gz", None),
            P("tm", None, "gz", None),
            P("tm", None, "gz", None),
            P("tm", None, "gz", None),
            P(None, "gz", None),
            P("tm", None),
        ),
        out_specs=(P("tm", "gz", None), P("tm", "gz", None)),
        check_vma=False,
    )
```

```python
import jax
import jax.numpy as jnp
from jax import lax
from jax.experimental import pallas as pl
from jax.experimental.pallas import tpu as pltpu
from jax.sharding import PartitionSpec as P

CHIPS = 8
COUNT = 16
SLABS = 8
GROUP = 16
MIB = 1024 * 1024
F32 = jnp.float32


def packed(cells):
    x = cells.shape[0]
    return cells.reshape(x, 4, 4, 128).transpose(0, 2, 1, 3).reshape(x, 2, 8, 128)


def unpacked(cells):
    x = cells.shape[0]
    return cells.reshape(x, 4, 4, 128).transpose(0, 2, 1, 3).reshape(x, 4, 512)


def roll(cells, shift):
    return pltpu.roll(cells, shift % 8, 1)


def places(n):
    sub = lax.broadcasted_iota(jnp.int32, (n, 8, 128), 1)
    return sub, lax.rem(sub, 4), lax.broadcasted_iota(jnp.int32, (n, 8, 128), 2)


def spread(field, speed, row, n, lower, upper):
    sub, z, lane = places(n)
    first, at_start, at_end = sub < 4, lane == 0, lane == 127
    v = [field[pl.ds(row + 1, n), h] for h in (0, 1)]
    k = [speed[pl.ds(row + 1, n), h] for h in (0, 1)]

    def ahead(a, b):
        ra, rb = pltpu.roll(a, 127, 2), pltpu.roll(b, 127, 2)
        qa, qb = roll(ra, 4), roll(rb, 4)
        return (
            jnp.where(at_end, jnp.where(first, qa, qb), ra),
            jnp.where(at_end, jnp.where(first, qb, 0.0), rb),
        )

    def behind(a, b, edge):
        ra, rb = pltpu.roll(a, 1, 2), pltpu.roll(b, 1, 2)
        qa, qb = roll(ra, 4), roll(rb, 4)
        return (
            jnp.where(at_start, jnp.where(first, edge, qa), ra),
            jnp.where(at_start, jnp.where(first, qa, qb), rb),
        )

    v_y, k_y = ahead(*v), ahead(*k)
    f_y = [(k[h] + k_y[h]) * (v_y[h] - v[h]) for h in (0, 1)]
    b_y = behind(*f_y, k[0] * v[0])
    out = []
    for h in (0, 1):
        kv = k[h] * v[h]
        f_z = jnp.where(z == 3, -upper * kv, (k[h] + roll(k[h], -1)) * (roll(v[h], -1) - v[h]))
        b_z = jnp.where(z == 0, lower * kv, roll(f_z, 1))
        f_x = (k[h] + speed[pl.ds(row + 2, n), h]) * (field[pl.ds(row + 2, n), h] - v[h])
        b_x = (k[h] + speed[pl.ds(row, n), h]) * (v[h] - field[pl.ds(row, n), h])
        out.append((f_x - b_x) + (f_y[h] - b_y[h]) + (f_z - b_z))
    return v, out


def widen(scratch, main, before, after, block, blocks):
    rows = main.shape[0]
    scratch[pl.ds(1, rows)] = main[...]
    scratch[pl.ds(0, 1)] = jnp.where(block > 0, before[...], 0.0)
    scratch[pl.ds(rows + 1, 1)] = jnp.where(block < blocks - 1, after[...], 0.0)


def where_am_i():
    me = lax.axis_index("tm")
    return me // 8, lax.rem(me // 2, 4), lax.rem(me, 2)


def series_kernel(coeffs, u, k, p, cos, sin, d_other, d_same, v_other, v_same, low_other, low_same, high_other, high_same,
                  us, ks, ns, ds, vs, fx, fy, fw, fz, fm, es, in_sem, out_sem, edge_sem):
    cells = u.shape[0] // 16
    rows = cells // CHIPS
    half_rows = rows // 2
    my_z, my_y, my_core = where_am_i()
    slab = lax.axis_index("gz")
    lower, upper = jnp.where(slab == 0, 1.0, 0.0), jnp.where(slab == SLABS - 1, 1.0, 0.0)
    c0, c1, c2, c3 = (coeffs[0, i] for i in range(4))
    sub = lax.broadcasted_iota(jnp.int32, (8, 128), 0)
    lane = lax.broadcasted_iota(jnp.int32, (8, 128), 1)
    z = lax.rem(sub, 4)
    first, at_start, at_end = sub < 4, lane == 0, lane == 127
    open_up, open_down = jnp.where(z == 3, 0.0, 1.0), jnp.where(z == 0, 0.0, 1.0)
    of_u = jnp.where(z == 0, c1, jnp.where(z == 1, c0, jnp.where(z == 2, c3, c2)))
    of_n = jnp.where(z == 1, c1, jnp.where(z == 3, c3, 0.0))
    y_first, y_last = jnp.logical_and(first, at_start), jnp.logical_and(jnp.logical_not(first), at_end)
    outer = jnp.where(z == 0, lower, 0.0) + jnp.where(z == 3, upper, 0.0)

    def arrays():
        return ((u, us, 16), (k, ks, 16), (p, ns, 16), (cos, ds, 0), (sin, vs, 0))

    def loads(c, which):
        return [
            pltpu.make_async_copy(a.at[pl.ds(c * rows * 16, rows * 16)], b.at[pl.ds(c * rows * 16 + off, rows * 16)], in_sem.at[i, c])
            for i, (a, b, off) in enumerate(arrays()) if i in which
        ]

    for c in range(CHIPS):
        for copy in loads(c, (0, 1, 2)):
            copy.start()
        if c:
            for copy in loads(c - 1, (3, 4)):
                copy.start()
    for copy in loads(CHIPS - 1, (3, 4)):
        copy.start()
    nothing = jnp.zeros((16, 128), F32)
    fx[0:16] = nothing
    fz[0:16] = nothing
    for side in (0, 1):
        es[side, 0:16] = nothing
        es[side, (cells + 1) * 16 : (cells + 2) * 16] = nothing
    for ref in (us, ks, ns):
        ref[0:16] = nothing
        ref[(cells + 1) * 16 : (cells + 2) * 16] = nothing

    def at(ref, row, by=0):
        return ref[pl.ds(row + by, 8), :]

    def ahead(ref, row, here):
        return pltpu.roll(jnp.where(at_start, at(ref, row, 4), here), 127, 1)

    def behind(ref, row, here):
        return pltpu.roll(jnp.where(at_end, at(ref, row, -4), here), 1, 1)

    def up(here):
        return pltpu.roll(here, 7, 0)

    def down(here):
        return pltpu.roll(here, 1, 0)

    def first_pass(c):
        def step(i, carry):
            start = (c * rows + i * GROUP + 1) * 16
            kk, uu, kx = {}, {}, {}

            def center(seen, ref, g, h):
                if (g, h) not in seen:
                    seen[g, h] = at(ref, start + g * 16 + h * 8)
                return seen[g, h]

            for h in (0, 1):
                kx[-1, h] = center(kk, ks, -1, h) + center(kk, ks, 0, h)
            for g in range(GROUP):
                for h in (0, 1):
                    row = start + g * 16 + h * 8
                    k0 = center(kk, ks, g, h)
                    kx[g, h] = k0 + center(kk, ks, g + 1, h)
                    ky, kw = k0 + ahead(ks, row, k0), k0 + behind(ks, row, k0)
                    if h == 0:
                        face_w = jnp.where(y_first, k0, kw)
                        face_y, kw = ky, jnp.where(y_first, 0.0, kw)
                    else:
                        face_y = jnp.where(y_last, k0, ky)
                        face_w, ky = kw, jnp.where(y_last, 0.0, ky)
                    kz, kv = (k0 + up(k0)) * open_up, (k0 + down(k0)) * open_down
                    mid = 24.0 - (((kx[g, h] + kx[g - 1, h]) + (face_y + face_w)) + ((kz + kv) + outer * k0))
                    for ref, value in ((fx, kx[g, h]), (fy, ky), (fw, kw), (fz, kz), (fm, mid)):
                        ref[pl.ds(row, 8), :] = value
                    v = center(uu, us, g, h)
                    out = (kx[g, h] * center(uu, us, g + 1, h) + kx[g - 1, h] * center(uu, us, g - 1, h)) + (kz * up(v) + kv * down(v))
                    out = out + (ky * ahead(us, row, v) + kw * behind(us, row, v)) + mid * v
                    ns[pl.ds(row, 8), :] = out * (-1.0 / 12.0) - at(ns, row)
            return carry

        lax.fori_loop(0, rows // GROUP, step, 0)

    def moments(c):
        def spread(ref, row, plane):
            return jnp.where(first, ref[pl.ds(row + plane, 1), :], ref[pl.ds(row + 4 + plane, 1), :])

        def step(i, carry):
            for g in range(2 * GROUP):
                row = (c * rows + 1) * 16 + (i * 2 * GROUP + g) * 8
                for side, plane in ((0, 0), (1, 3)):
                    es[side, pl.ds(row, 8), :] = of_u * spread(us, row, plane) + of_n * spread(ns, row, plane)
            return carry

        lax.fori_loop(0, rows // GROUP, step, 0)

    def second_pass(c):
        def step(i, carry):
            start = (c * rows + i * GROUP + 1) * 16
            nn, kx = {}, {}

            def center(seen, ref, g, h):
                if (g, h) not in seen:
                    seen[g, h] = at(ref, start + g * 16 + h * 8)
                return seen[g, h]

            for g in range(GROUP):
                for h in (0, 1):
                    row = start + g * 16 + h * 8
                    v = center(nn, ns, g, h)
                    kz = at(fz, row)
                    out = center(kx, fx, g, h) * center(nn, ns, g + 1, h) + center(kx, fx, g - 1, h) * center(nn, ns, g - 1, h)
                    out = out + (kz * up(v) + down(kz) * down(v))
                    out = out + (at(fy, row) * ahead(ns, row, v) + at(fw, row) * behind(ns, row, v)) + at(fm, row) * v
                    final = out * (-1.0 / 12.0) - at(us, row)
                    ds[pl.ds(row - 16, 8), :] = at(ds, row, -16) + c0 * v + c1 * final
                    vs[pl.ds(row - 16, 8), :] = at(vs, row, -16) + c2 * v + c3 * final
            return carry

        lax.fori_loop(0, rows // GROUP, step, 0)

    def slots(c, core):
        turn = lax.rem((1 - 2 * core) * (lax.rem(c, 4) - my_y) + 8, 4)
        side = lax.rem(c // 4 + my_z, 2)
        return turn * 2 + side, side * 4 + turn

    def stores(c, core, same):
        here = pl.ds((c * rows + core * half_rows) * 16, half_rows * 16)
        y_slot, z_slot = slots(c, core)
        return [
            pltpu.make_async_copy(ds.at[here], (d_same if same else d_other).at[y_slot], out_sem.at[0, core, c]),
            pltpu.make_async_copy(vs.at[here], (v_same if same else v_other).at[z_slot], out_sem.at[1, core, c]),
        ]

    def edge_stores(c, core, same):
        here = pl.ds((c * rows + core * half_rows) * 16, (half_rows + 2) * 16)
        y_slot, z_slot = slots(c, core)
        return [
            pltpu.make_async_copy(es.at[0, here], (low_same if same else low_other).at[y_slot], edge_sem.at[0, core, c]),
            pltpu.make_async_copy(es.at[1, here], (high_same if same else high_other).at[z_slot], edge_sem.at[1, core, c]),
        ]

    def send(copies, c, core):
        for same in (True, False):
            @pl.when((my_core == core) == same)
            def _():
                for copy in copies(c, core, same):
                    copy.start()

    def chunk(c, carry):
        @pl.when(c < CHIPS)
        def _():
            @pl.when(c == 0)
            def _():
                for copy in loads(c, (0, 1, 2)):
                    copy.wait()

            @pl.when(c + 1 < CHIPS)
            def _():
                for copy in loads(c + 1, (0, 1, 2)):
                    copy.wait()

            first_pass(c)
            moments(c)
            send(edge_stores, c, 0)

        @pl.when(c > 0)
        def _():
            send(edge_stores, c - 1, 1)
            for copy in loads(c - 1, (3, 4)):
                copy.wait()
            second_pass(c - 1)
            for core in (0, 1):
                send(stores, c - 1, core)

        return carry

    lax.fori_loop(0, CHIPS + 1, chunk, 0)

    def end(c, carry):
        for core in (0, 1):
            for copy in stores(c, core, True) + edge_stores(c, core, True):
                copy.wait()
        return carry

    lax.fori_loop(0, CHIPS, end, 0)


def mend_kernel(d, v, low, high, below, above, k, k_low, k_high, d_out, v_out, ds, vs):
    rows = d.shape[0]
    slab = lax.axis_index("gz")
    lower, upper = jnp.where(slab == 0, 1.0, 0.0), jnp.where(slab == SLABS - 1, 1.0, 0.0)
    wide = rows + 2
    z = places(wide)[1]
    factor = []
    for h in (0, 1):
        under = (1.0 - lower) * (k[:, h] + roll(k_low[:, h], -3))
        over = (1.0 - upper) * (k[:, h] + roll(k_high[:, h], 3))
        factor.append(jnp.where(z == 0, under, jnp.where(z == 3, -over, 0.0)) * (1.0 / 12.0))
    from_low = [low[:, h] - below[:, h] for h in (0, 1)]
    from_high = [above[:, h] - high[:, h] for h in (0, 1)]
    direct = []
    for field, slot in ((ds, 0), (vs, 2)):
        for h in (0, 1):
            a = jnp.where(z == 0, roll(from_low[h], -slot), roll(from_high[h], 3 - slot))
            b = jnp.where(z == 0, roll(from_low[h], -slot - 1), roll(from_high[h], 2 - slot))
            w = factor[h] * a
            field[:, h] = w
            direct.append((factor[h] * b + 2.0 * jnp.abs(factor[h]) * w)[1 : rows + 1])
    for field, given, out, direct_of in ((ds, d, d_out, direct[:2]), (vs, v, v_out, direct[2:])):
        w, outflow = spread(field, k, 0, rows, lower, upper)
        for h in (0, 1):
            out[:, h] = given[:, h] + direct_of[h] - outflow[h] * (1.0 / 12.0) - 2.0 * w[h]


ANYWHERE = pl.BlockSpec(memory_space=pl.ANY)
SMEM = pl.BlockSpec(memory_space=pltpu.SMEM)


def params(mib):
    return pltpu.CompilerParams(vmem_limit_bytes=mib * MIB)


def cost(mib):
    return pl.CostEstimate(flops=0, bytes_accessed=mib * MIB, transcendentals=0)


def flat(cells):
    return cells.reshape(-1, 128)


def series(coeffs, u, k, p, cos, sin):
    cells = u.shape[0] // 16
    share = jax.ShapeDtypeStruct((CHIPS, cells, 128), F32)
    edge = jax.ShapeDtypeStruct((CHIPS, (cells // COUNT + 2) * 16, 128), F32)
    wide = pltpu.VMEM(((cells + 2) * 16, 128), F32)
    exact = pltpu.VMEM((cells * 16, 128), F32)
    return pl.pallas_call(
        series_kernel,
        out_shape=(share,) * 4 + (edge,) * 4,
        in_specs=[SMEM] + [ANYWHERE] * 5,
        out_specs=(ANYWHERE,) * 8,
        scratch_shapes=[wide, wide, wide, exact, exact, wide, wide, wide, wide, wide]
        + [
            pltpu.VMEM((2, (cells + 2) * 16, 128), F32),
            pltpu.SemaphoreType.DMA((5, CHIPS)),
            pltpu.SemaphoreType.DMA((2, 2, CHIPS)),
            pltpu.SemaphoreType.DMA((2, 2, CHIPS)),
        ],
        compiler_params=params(56),
        cost_estimate=cost(45),
    )(coeffs, u, k, p, cos, sin)


def mend(d, v, low, high, below, above, k, k_low, k_high):
    shape = jax.ShapeDtypeStruct(d.shape, F32)
    whole = pl.BlockSpec(memory_space=pltpu.VMEM)
    return pl.pallas_call(
        mend_kernel,
        out_shape=(shape, shape),
        in_specs=[whole] * 9,
        out_specs=(whole, whole),
        scratch_shapes=[pltpu.VMEM(k.shape, F32)] * 2,
        compiler_params=params(16),
        cost_estimate=cost(4),
    )(d, v, low, high, below, above, k, k_low, k_high)


CELL = (2, 8, 128)


def along_y(sign):
    def goal(i):
        z, y, core = i // 8, (i // 2) % 4, i % 2
        return z * 8 + ((y + sign * (1 - 2 * core)) % 4) * 2 + core

    return [(i, goal(i)) for i in range(COUNT)]


FORTH, BACK = along_y(1), along_y(-1)
ACROSS = [(i, i ^ 8) for i in range(COUNT)]
SIBLING = [(i, i ^ 1) for i in range(COUNT)]
UP = [(i, i + 1) for i in range(SLABS - 1)]
DOWN = [(i + 1, i) for i in range(SLABS - 1)]


def swap(same, other):
    return same + lax.ppermute(other, "tm", SIBLING)


def ring_ends(two, back):
    return lax.ppermute(two, "tm", FORTH), lax.ppermute(back, "tm", BACK)


def ring_close(one, own, relayed, direct):
    return own + direct + lax.ppermute(one + relayed, "tm", FORTH)


def local(prev_term, last_term, cos_sum, sin_sum, speed_sq, series_coeffs):
    u, p, k = flat(packed(last_term[0])), flat(packed(prev_term[0])), flat(packed(speed_sq))
    cos, sin = flat(packed(cos_sum[0])), flat(packed(sin_sum[0]))
    rows = last_term.shape[1] // COUNT
    me = lax.axis_index("tm")

    d_other, d_same, v_other, v_same, low_other, low_same, high_other, high_same = series(series_coeffs, u, k, p, cos, sin)
    low, high = swap(low_same, low_other), swap(high_same, high_other)
    d_other, v_other, low, high = lax.optimization_barrier((d_other, v_other, low, high))
    d, v = swap(d_same, d_other), swap(v_same, v_other)

    start = me * rows * 16
    k_here = jnp.concatenate(
        [
            jnp.where(me > 0, lax.dynamic_slice_in_dim(k, jnp.maximum(start - 16, 0), 16), 0.0),
            lax.dynamic_slice_in_dim(k, start, rows * 16),
            jnp.where(me < COUNT - 1, lax.dynamic_slice_in_dim(k, jnp.minimum(start + rows * 16, k.shape[0] - 16), 16), 0.0),
        ]
    )
    k_low, k_high = lax.ppermute(k_here, "gz", UP), lax.ppermute(k_here, "gz", DOWN)

    low, d = (a.reshape(4, 2, *a.shape[1:]) for a in (low, d))
    low_ends, d_ends = ring_ends(low[2], low[3]), ring_ends(d[2], d[3])
    high = high[:4] + lax.ppermute(high[4:], "tm", ACROSS)
    v = v[:4] + lax.ppermute(v[4:], "tm", ACROSS)
    low = ring_close(low[1], low[0], *low_ends)
    high = ring_close(high[1], high[0], *ring_ends(high[2], high[3]))
    low = low[0] + lax.ppermute(low[1], "tm", ACROSS)
    below, above = lax.ppermute(high, "gz", UP), lax.ppermute(low, "gz", DOWN)
    d = ring_close(d[1], d[0], *d_ends)
    v = ring_close(v[1], v[0], *ring_ends(v[2], v[3]))
    d = d[0] + lax.ppermute(d[1], "tm", ACROSS)

    wide = (a.reshape(rows + 2, *CELL) for a in (low, high, below, above, k_here, k_low, k_high))
    d, v = mend(d.reshape(rows, *CELL), v.reshape(rows, *CELL), *wide)
    return unpacked(d), unpacked(v)


def solution(mesh):
    return jax.shard_map(
        local,
        mesh=mesh,
        in_specs=(
            P("tm", None, "gz", None),
            P("tm", None, "gz", None),
            P("tm", None, "gz", None),
            P("tm", None, "gz", None),
            P(None, "gz", None),
            P("tm", None),
        ),
        out_specs=(P("tm", "gz", None), P("tm", "gz", None)),
        check_vma=False,
    )
```

```python
import jax
import jax.numpy as jnp
from jax import lax
from jax.experimental import pallas as pl
from jax.experimental.pallas import tpu as pltpu
from jax.sharding import PartitionSpec as P

CHIPS = 8
COUNT = 16
SLABS = 8
GROUP = 16
MIB = 1024 * 1024
F32 = jnp.float32


def packed(cells):
    x = cells.shape[0]
    return cells.reshape(x, 4, 4, 128).transpose(0, 2, 1, 3).reshape(x, 2, 8, 128)


def unpacked(cells):
    x = cells.shape[0]
    return cells.reshape(x, 4, 4, 128).transpose(0, 2, 1, 3).reshape(x, 4, 512)


def roll(cells, shift):
    return pltpu.roll(cells, shift % 8, 1)


def places(n):
    sub = lax.broadcasted_iota(jnp.int32, (n, 8, 128), 1)
    return sub, lax.rem(sub, 4), lax.broadcasted_iota(jnp.int32, (n, 8, 128), 2)


def spread(field, speed, row, n, lower, upper):
    sub, z, lane = places(n)
    first, at_start, at_end = sub < 4, lane == 0, lane == 127
    v = [field[pl.ds(row + 1, n), h] for h in (0, 1)]
    k = [speed[pl.ds(row + 1, n), h] for h in (0, 1)]

    def ahead(a, b):
        ra, rb = pltpu.roll(a, 127, 2), pltpu.roll(b, 127, 2)
        qa, qb = roll(ra, 4), roll(rb, 4)
        return (
            jnp.where(at_end, jnp.where(first, qa, qb), ra),
            jnp.where(at_end, jnp.where(first, qb, 0.0), rb),
        )

    def behind(a, b, edge):
        ra, rb = pltpu.roll(a, 1, 2), pltpu.roll(b, 1, 2)
        qa, qb = roll(ra, 4), roll(rb, 4)
        return (
            jnp.where(at_start, jnp.where(first, edge, qa), ra),
            jnp.where(at_start, jnp.where(first, qa, qb), rb),
        )

    v_y, k_y = ahead(*v), ahead(*k)
    f_y = [(k[h] + k_y[h]) * (v_y[h] - v[h]) for h in (0, 1)]
    b_y = behind(*f_y, k[0] * v[0])
    out = []
    for h in (0, 1):
        kv = k[h] * v[h]
        f_z = jnp.where(z == 3, -upper * kv, (k[h] + roll(k[h], -1)) * (roll(v[h], -1) - v[h]))
        b_z = jnp.where(z == 0, lower * kv, roll(f_z, 1))
        f_x = (k[h] + speed[pl.ds(row + 2, n), h]) * (field[pl.ds(row + 2, n), h] - v[h])
        b_x = (k[h] + speed[pl.ds(row, n), h]) * (v[h] - field[pl.ds(row, n), h])
        out.append((f_x - b_x) + (f_y[h] - b_y[h]) + (f_z - b_z))
    return v, out


def widen(scratch, main, before, after, block, blocks):
    rows = main.shape[0]
    scratch[pl.ds(1, rows)] = main[...]
    scratch[pl.ds(0, 1)] = jnp.where(block > 0, before[...], 0.0)
    scratch[pl.ds(rows + 1, 1)] = jnp.where(block < blocks - 1, after[...], 0.0)


def where_am_i():
    me = lax.axis_index("tm")
    return me // 8, lax.rem(me // 2, 4), lax.rem(me, 2)


def series_kernel(coeffs, u, k, p, cos, sin, d_other, d_same, v_other, v_same, low_other, low_same, high_other, high_same,
                  us, ks, ns, ds, vs, fx, fy, fw, fz, fm, es, in_sem, out_sem, edge_sem):
    cells = u.shape[0] // 16
    rows = cells // CHIPS
    half_rows = rows // 2
    my_z, my_y, my_core = where_am_i()
    slab = lax.axis_index("gz")
    lower, upper = jnp.where(slab == 0, 1.0, 0.0), jnp.where(slab == SLABS - 1, 1.0, 0.0)
    c0, c1, c2, c3 = (coeffs[0, i] for i in range(4))
    sub = lax.broadcasted_iota(jnp.int32, (8, 128), 0)
    lane = lax.broadcasted_iota(jnp.int32, (8, 128), 1)
    z = lax.rem(sub, 4)
    first, at_start, at_end = sub < 4, lane == 0, lane == 127
    open_up, open_down = jnp.where(z == 3, 0.0, 1.0), jnp.where(z == 0, 0.0, 1.0)
    of_u = jnp.where(z == 0, c1, jnp.where(z == 1, c0, jnp.where(z == 2, c3, c2)))
    of_n = jnp.where(z == 1, c1, jnp.where(z == 3, c3, 0.0))
    y_first, y_last = jnp.logical_and(first, at_start), jnp.logical_and(jnp.logical_not(first), at_end)
    outer = jnp.where(z == 0, lower, 0.0) + jnp.where(z == 3, upper, 0.0)

    def arrays():
        return ((u, us, 16), (k, ks, 16), (p, ns, 16), (cos, ds, 0), (sin, vs, 0))

    def loads(c, which):
        return [
            pltpu.make_async_copy(a.at[pl.ds(c * rows * 16, rows * 16)], b.at[pl.ds(c * rows * 16 + off, rows * 16)], in_sem.at[i, c])
            for i, (a, b, off) in enumerate(arrays()) if i in which
        ]

    for c in range(CHIPS):
        for copy in loads(c, (0, 1, 2)):
            copy.start()
        if c:
            for copy in loads(c - 1, (3, 4)):
                copy.start()
    for copy in loads(CHIPS - 1, (3, 4)):
        copy.start()
    nothing = jnp.zeros((16, 128), F32)
    fx[0:16] = nothing
    fz[0:16] = nothing
    for side in (0, 1):
        es[side, 0:16] = nothing
        es[side, (cells + 1) * 16 : (cells + 2) * 16] = nothing
    for ref in (us, ks, ns):
        ref[0:16] = nothing
        ref[(cells + 1) * 16 : (cells + 2) * 16] = nothing

    def at(ref, row, by=0):
        return ref[pl.ds(row + by, 8), :]

    def ahead(ref, row, here):
        return pltpu.roll(jnp.where(at_start, at(ref, row, 4), here), 127, 1)

    def behind(ref, row, here):
        return pltpu.roll(jnp.where(at_end, at(ref, row, -4), here), 1, 1)

    def up(here):
        return pltpu.roll(here, 7, 0)

    def down(here):
        return pltpu.roll(here, 1, 0)

    def first_pass(c):
        def step(i, carry):
            start = (c * rows + i * GROUP + 1) * 16
            kk, uu, kx = {}, {}, {}

            def center(seen, ref, g, h):
                if (g, h) not in seen:
                    seen[g, h] = at(ref, start + g * 16 + h * 8)
                return seen[g, h]

            for h in (0, 1):
                kx[-1, h] = center(kk, ks, -1, h) + center(kk, ks, 0, h)
            for g in range(GROUP):
                for h in (0, 1):
                    row = start + g * 16 + h * 8
                    k0 = center(kk, ks, g, h)
                    kx[g, h] = k0 + center(kk, ks, g + 1, h)
                    ky, kw = k0 + ahead(ks, row, k0), k0 + behind(ks, row, k0)
                    if h == 0:
                        face_w = jnp.where(y_first, k0, kw)
                        face_y, kw = ky, jnp.where(y_first, 0.0, kw)
                    else:
                        face_y = jnp.where(y_last, k0, ky)
                        face_w, ky = kw, jnp.where(y_last, 0.0, ky)
                    kz, kv = (k0 + up(k0)) * open_up, (k0 + down(k0)) * open_down
                    mid = 24.0 - (((kx[g, h] + kx[g - 1, h]) + (face_y + face_w)) + ((kz + kv) + outer * k0))
                    for ref, value in ((fx, kx[g, h]), (fy, ky), (fw, kw), (fz, kz), (fm, mid)):
                        ref[pl.ds(row, 8), :] = value
                    v = center(uu, us, g, h)
                    out = (kx[g, h] * center(uu, us, g + 1, h) + kx[g - 1, h] * center(uu, us, g - 1, h)) + (kz * up(v) + kv * down(v))
                    out = out + (ky * ahead(us, row, v) + kw * behind(us, row, v)) + mid * v
                    ns[pl.ds(row, 8), :] = out * (-1.0 / 12.0) - at(ns, row)
            return carry

        lax.fori_loop(0, rows // GROUP, step, 0)

    def moments(c):
        def spread(ref, row, plane):
            return jnp.where(first, ref[pl.ds(row + plane, 1), :], ref[pl.ds(row + 4 + plane, 1), :])

        def step(i, carry):
            for g in range(2 * GROUP):
                row = (c * rows + 1) * 16 + (i * 2 * GROUP + g) * 8
                for side, plane in ((0, 0), (1, 3)):
                    es[side, pl.ds(row, 8), :] = of_u * spread(us, row, plane) + of_n * spread(ns, row, plane)
            return carry

        lax.fori_loop(0, rows // GROUP, step, 0)

    def second_pass(c):
        def step(i, carry):
            start = (c * rows + i * GROUP + 1) * 16
            nn, kx = {}, {}

            def center(seen, ref, g, h):
                if (g, h) not in seen:
                    seen[g, h] = at(ref, start + g * 16 + h * 8)
                return seen[g, h]

            for g in range(GROUP):
                for h in (0, 1):
                    row = start + g * 16 + h * 8
                    v = center(nn, ns, g, h)
                    kz = at(fz, row)
                    out = center(kx, fx, g, h) * center(nn, ns, g + 1, h) + center(kx, fx, g - 1, h) * center(nn, ns, g - 1, h)
                    out = out + (kz * up(v) + down(kz) * down(v))
                    out = out + (at(fy, row) * ahead(ns, row, v) + at(fw, row) * behind(ns, row, v)) + at(fm, row) * v
                    final = out * (-1.0 / 12.0) - at(us, row)
                    ds[pl.ds(row - 16, 8), :] = at(ds, row, -16) + c0 * v + c1 * final
                    vs[pl.ds(row - 16, 8), :] = at(vs, row, -16) + c2 * v + c3 * final
            return carry

        lax.fori_loop(0, rows // GROUP, step, 0)

    def slots(c, core):
        turn = lax.rem((1 - 2 * core) * (lax.rem(c, 4) - my_y) + 8, 4)
        side = lax.rem(c // 4 + my_z, 2)
        return turn * 2 + side, side * 4 + turn

    def stores(c, core, same):
        here = pl.ds((c * rows + core * half_rows) * 16, half_rows * 16)
        y_slot, z_slot = slots(c, core)
        return [
            pltpu.make_async_copy(ds.at[here], (d_same if same else d_other).at[y_slot], out_sem.at[0, core, c]),
            pltpu.make_async_copy(vs.at[here], (v_same if same else v_other).at[z_slot], out_sem.at[1, core, c]),
        ]

    def edge_stores(c, core, same):
        here = pl.ds((c * rows + core * half_rows) * 16, (half_rows + 2) * 16)
        y_slot, z_slot = slots(c, core)
        return [
            pltpu.make_async_copy(es.at[0, here], (low_same if same else low_other).at[y_slot], edge_sem.at[0, core, c]),
            pltpu.make_async_copy(es.at[1, here], (high_same if same else high_other).at[z_slot], edge_sem.at[1, core, c]),
        ]

    def send(copies, c, core):
        for same in (True, False):
            @pl.when((my_core == core) == same)
            def _():
                for copy in copies(c, core, same):
                    copy.start()

    def chunk(c, carry):
        @pl.when(c < CHIPS)
        def _():
            @pl.when(c == 0)
            def _():
                for copy in loads(c, (0, 1, 2)):
                    copy.wait()

            @pl.when(c + 1 < CHIPS)
            def _():
                for copy in loads(c + 1, (0, 1, 2)):
                    copy.wait()

            first_pass(c)
            moments(c)
            send(edge_stores, c, 0)

        @pl.when(c > 0)
        def _():
            send(edge_stores, c - 1, 1)
            for copy in loads(c - 1, (3, 4)):
                copy.wait()
            second_pass(c - 1)
            for core in (0, 1):
                send(stores, c - 1, core)

        return carry

    lax.fori_loop(0, CHIPS + 1, chunk, 0)

    def end(c, carry):
        for core in (0, 1):
            for copy in stores(c, core, True) + edge_stores(c, core, True):
                copy.wait()
        return carry

    lax.fori_loop(0, CHIPS, end, 0)


def mend_kernel(d, v, low, high, below, above, k, k_low, k_high, d_out, v_out, ds, vs):
    rows = d.shape[0]
    slab = lax.axis_index("gz")
    lower, upper = jnp.where(slab == 0, 1.0, 0.0), jnp.where(slab == SLABS - 1, 1.0, 0.0)
    wide = rows + 2
    z = places(wide)[1]
    factor = []
    for h in (0, 1):
        under = (1.0 - lower) * (k[:, h] + roll(k_low[:, h], -3))
        over = (1.0 - upper) * (k[:, h] + roll(k_high[:, h], 3))
        factor.append(jnp.where(z == 0, under, jnp.where(z == 3, -over, 0.0)) * (1.0 / 12.0))
    from_low = [low[:, h] - below[:, h] for h in (0, 1)]
    from_high = [above[:, h] - high[:, h] for h in (0, 1)]
    direct = []
    for field, slot in ((ds, 0), (vs, 2)):
        for h in (0, 1):
            a = jnp.where(z == 0, roll(from_low[h], -slot), roll(from_high[h], 3 - slot))
            b = jnp.where(z == 0, roll(from_low[h], -slot - 1), roll(from_high[h], 2 - slot))
            w = factor[h] * a
            field[:, h] = w
            direct.append((factor[h] * b + 2.0 * jnp.abs(factor[h]) * w)[1 : rows + 1])
    for field, given, out, direct_of in ((ds, d, d_out, direct[:2]), (vs, v, v_out, direct[2:])):
        w, outflow = spread(field, k, 0, rows, lower, upper)
        for h in (0, 1):
            out[:, h] = given[:, h] + direct_of[h] - outflow[h] * (1.0 / 12.0) - 2.0 * w[h]


ANYWHERE = pl.BlockSpec(memory_space=pl.ANY)
SMEM = pl.BlockSpec(memory_space=pltpu.SMEM)


def params(mib):
    return pltpu.CompilerParams(vmem_limit_bytes=mib * MIB)


def cost(mib):
    return pl.CostEstimate(flops=0, bytes_accessed=mib * MIB, transcendentals=0)


def flat(cells):
    return cells.reshape(-1, 128)


def series(coeffs, u, k, p, cos, sin):
    cells = u.shape[0] // 16
    share = jax.ShapeDtypeStruct((CHIPS, cells, 128), F32)
    edge = jax.ShapeDtypeStruct((CHIPS, (cells // COUNT + 2) * 16, 128), F32)
    wide = pltpu.VMEM(((cells + 2) * 16, 128), F32)
    exact = pltpu.VMEM((cells * 16, 128), F32)
    return pl.pallas_call(
        series_kernel,
        out_shape=(share,) * 4 + (edge,) * 4,
        in_specs=[SMEM] + [ANYWHERE] * 5,
        out_specs=(ANYWHERE,) * 8,
        scratch_shapes=[wide, wide, wide, exact, exact, wide, wide, wide, wide, wide]
        + [
            pltpu.VMEM((2, (cells + 2) * 16, 128), F32),
            pltpu.SemaphoreType.DMA((5, CHIPS)),
            pltpu.SemaphoreType.DMA((2, 2, CHIPS)),
            pltpu.SemaphoreType.DMA((2, 2, CHIPS)),
        ],
        compiler_params=params(56),
        cost_estimate=cost(45),
    )(coeffs, u, k, p, cos, sin)


def mend(d, v, low, high, below, above, k, k_low, k_high):
    shape = jax.ShapeDtypeStruct(d.shape, F32)
    whole = pl.BlockSpec(memory_space=pltpu.VMEM)
    return pl.pallas_call(
        mend_kernel,
        out_shape=(shape, shape),
        in_specs=[whole] * 9,
        out_specs=(whole, whole),
        scratch_shapes=[pltpu.VMEM(k.shape, F32)] * 2,
        compiler_params=params(16),
        cost_estimate=cost(4),
    )(d, v, low, high, below, above, k, k_low, k_high)


CELL = (2, 8, 128)


def along_y(sign):
    def goal(i):
        z, y, core = i // 8, (i // 2) % 4, i % 2
        return z * 8 + ((y + sign * (1 - 2 * core)) % 4) * 2 + core

    return [(i, goal(i)) for i in range(COUNT)]


FORTH, BACK = along_y(1), along_y(-1)
ACROSS = [(i, i ^ 8) for i in range(COUNT)]
SIBLING = [(i, i ^ 1) for i in range(COUNT)]
UP = [(i, i + 1) for i in range(SLABS - 1)]
DOWN = [(i + 1, i) for i in range(SLABS - 1)]


def to_sibling(other):
    return lax.ppermute(other, "tm", SIBLING)


def forth(cells):
    return lax.ppermute(cells, "tm", FORTH)


def back(cells):
    return lax.ppermute(cells, "tm", BACK)


def across(cells):
    return lax.ppermute(cells, "tm", ACROSS)


def after(first, then):
    return lax.optimization_barrier((first, then))


def local(prev_term, last_term, cos_sum, sin_sum, speed_sq, series_coeffs):
    u, p, k = flat(packed(last_term[0])), flat(packed(prev_term[0])), flat(packed(speed_sq))
    cos, sin = flat(packed(cos_sum[0])), flat(packed(sin_sum[0]))
    rows = last_term.shape[1] // COUNT
    me = lax.axis_index("tm")

    d_other, d_same, v_other, v_same, low_other, low_same, high_other, high_same = series(series_coeffs, u, k, p, cos, sin)

    def blocks(same, came, *at):
        return lax.slice_in_dim(same, *at) + lax.slice_in_dim(came, *at)

    high_came, low_came = to_sibling(high_other), to_sibling(low_other)
    (high_came, low_came), (d_other, v_other) = after((high_came, low_came), (d_other, v_other))
    d_came, v_came = to_sibling(d_other), to_sibling(v_other)

    high_far = across(blocks(high_same, high_came, 4, 8))
    low_two = forth(blocks(low_same, low_came, 4, 6))
    low_back = back(blocks(low_same, low_came, 6, 8))
    d_two = forth(blocks(d_same, d_came, 4, 6))
    d_back = back(blocks(d_same, d_came, 6, 8))

    start = me * rows * 16
    k_here = jnp.concatenate(
        [
            jnp.where(me > 0, lax.dynamic_slice_in_dim(k, jnp.maximum(start - 16, 0), 16), 0.0),
            lax.dynamic_slice_in_dim(k, start, rows * 16),
            jnp.where(me < COUNT - 1, lax.dynamic_slice_in_dim(k, jnp.minimum(start + rows * 16, k.shape[0] - 16), 16), 0.0),
        ]
    )
    k_low, k_high = lax.ppermute(k_here, "gz", UP), lax.ppermute(k_here, "gz", DOWN)

    low_rest = forth(blocks(low_same, low_came, 2, 4) + low_two)
    v_sent = blocks(v_same, v_came, 4, 8)
    (d_two, v_sent, k_low, k_high), high_far = after((d_two, v_sent, k_low, k_high), high_far)
    v_far = across(v_sent)
    d_rest = forth(blocks(d_same, d_came, 2, 4) + d_two)

    high = blocks(high_same, high_came, 0, 4) + high_far
    high_two, high_back = forth(high[2]), back(high[3])
    low = blocks(low_same, low_came, 0, 2) + low_back + low_rest
    low_far = across(low[1])
    high_rest = forth(high[1] + high_two)
    low = low[0] + low_far
    high = high[0] + high_back + high_rest
    above, below = lax.ppermute(low, "gz", DOWN), lax.ppermute(high, "gz", UP)

    d = blocks(d_same, d_came, 0, 2) + d_back + d_rest
    d = d[0] + across(d[1])
    v = blocks(v_same, v_came, 0, 4) + v_far
    v_two, v_back = forth(v[2]), back(v[3])
    (above, below), v_two = after((above, below), v_two)
    v = v[0] + v_back + forth(v[1] + v_two)

    wide = (a.reshape(rows + 2, *CELL) for a in (low, high, below, above, k_here, k_low, k_high))
    d, v = mend(d.reshape(rows, *CELL), v.reshape(rows, *CELL), *wide)
    return unpacked(d), unpacked(v)


def solution(mesh):
    return jax.shard_map(
        local,
        mesh=mesh,
        in_specs=(
            P("tm", None, "gz", None),
            P("tm", None, "gz", None),
            P("tm", None, "gz", None),
            P("tm", None, "gz", None),
            P(None, "gz", None),
            P("tm", None),
        ),
        out_specs=(P("tm", "gz", None), P("tm", "gz", None)),
        check_vma=False,
    )
```

```python
import jax
import jax.numpy as jnp
from jax import lax
from jax.experimental import pallas as pl
from jax.experimental.pallas import tpu as pltpu
from jax.sharding import PartitionSpec as P

CHIPS = 8
COUNT = 16
SLABS = 8
GROUP = 16
MIB = 1024 * 1024
F32 = jnp.float32


def packed(cells):
    x = cells.shape[0]
    return cells.reshape(x, 4, 4, 128).transpose(0, 2, 1, 3).reshape(x, 2, 8, 128)


def unpacked(cells):
    x = cells.shape[0]
    return cells.reshape(x, 4, 4, 128).transpose(0, 2, 1, 3).reshape(x, 4, 512)


def roll(cells, shift):
    return pltpu.roll(cells, shift % 8, 1)


def places(n):
    sub = lax.broadcasted_iota(jnp.int32, (n, 8, 128), 1)
    return sub, lax.rem(sub, 4), lax.broadcasted_iota(jnp.int32, (n, 8, 128), 2)


def spread(field, speed, row, n, lower, upper):
    sub, z, lane = places(n)
    first, at_start, at_end = sub < 4, lane == 0, lane == 127
    v = [field[pl.ds(row + 1, n), h] for h in (0, 1)]
    k = [speed[pl.ds(row + 1, n), h] for h in (0, 1)]

    def ahead(a, b):
        ra, rb = pltpu.roll(a, 127, 2), pltpu.roll(b, 127, 2)
        qa, qb = roll(ra, 4), roll(rb, 4)
        return (
            jnp.where(at_end, jnp.where(first, qa, qb), ra),
            jnp.where(at_end, jnp.where(first, qb, 0.0), rb),
        )

    def behind(a, b, edge):
        ra, rb = pltpu.roll(a, 1, 2), pltpu.roll(b, 1, 2)
        qa, qb = roll(ra, 4), roll(rb, 4)
        return (
            jnp.where(at_start, jnp.where(first, edge, qa), ra),
            jnp.where(at_start, jnp.where(first, qa, qb), rb),
        )

    v_y, k_y = ahead(*v), ahead(*k)
    f_y = [(k[h] + k_y[h]) * (v_y[h] - v[h]) for h in (0, 1)]
    b_y = behind(*f_y, k[0] * v[0])
    out = []
    for h in (0, 1):
        kv = k[h] * v[h]
        f_z = jnp.where(z == 3, -upper * kv, (k[h] + roll(k[h], -1)) * (roll(v[h], -1) - v[h]))
        b_z = jnp.where(z == 0, lower * kv, roll(f_z, 1))
        f_x = (k[h] + speed[pl.ds(row + 2, n), h]) * (field[pl.ds(row + 2, n), h] - v[h])
        b_x = (k[h] + speed[pl.ds(row, n), h]) * (v[h] - field[pl.ds(row, n), h])
        out.append((f_x - b_x) + (f_y[h] - b_y[h]) + (f_z - b_z))
    return v, out


def widen(scratch, main, before, after, block, blocks):
    rows = main.shape[0]
    scratch[pl.ds(1, rows)] = main[...]
    scratch[pl.ds(0, 1)] = jnp.where(block > 0, before[...], 0.0)
    scratch[pl.ds(rows + 1, 1)] = jnp.where(block < blocks - 1, after[...], 0.0)


def where_am_i():
    me = lax.axis_index("tm")
    return me // 8, lax.rem(me // 2, 4), lax.rem(me, 2)


def series_kernel(coeffs, u, k, p, cos, sin, d_other, d_same, v_other, v_same, low_other, low_same, high_other, high_same,
                  us, ks, ns, ds, vs, fx, fy, fw, fz, fm, es, in_sem, out_sem, edge_sem):
    cells = u.shape[0] // 16
    rows = cells // CHIPS
    half_rows = rows // 2
    my_z, my_y, my_core = where_am_i()
    slab = lax.axis_index("gz")
    lower, upper = jnp.where(slab == 0, 1.0, 0.0), jnp.where(slab == SLABS - 1, 1.0, 0.0)
    c0, c1, c2, c3 = (coeffs[0, i] for i in range(4))
    sub = lax.broadcasted_iota(jnp.int32, (8, 128), 0)
    lane = lax.broadcasted_iota(jnp.int32, (8, 128), 1)
    z = lax.rem(sub, 4)
    first, at_start, at_end = sub < 4, lane == 0, lane == 127
    open_up, open_down = jnp.where(z == 3, 0.0, 1.0), jnp.where(z == 0, 0.0, 1.0)
    of_u = jnp.where(z == 0, c1, jnp.where(z == 1, c0, jnp.where(z == 2, c3, c2)))
    of_n = jnp.where(z == 1, c1, jnp.where(z == 3, c3, 0.0))
    y_first, y_last = jnp.logical_and(first, at_start), jnp.logical_and(jnp.logical_not(first), at_end)
    outer = jnp.where(z == 0, lower, 0.0) + jnp.where(z == 3, upper, 0.0)

    def arrays():
        return ((u, us, 16), (k, ks, 16), (p, ns, 16), (cos, ds, 0), (sin, vs, 0))

    def loads(c, which):
        return [
            pltpu.make_async_copy(a.at[pl.ds(c * rows * 16, rows * 16)], b.at[pl.ds(c * rows * 16 + off, rows * 16)], in_sem.at[i, c])
            for i, (a, b, off) in enumerate(arrays()) if i in which
        ]

    for c in range(CHIPS):
        for copy in loads(c, (0, 1, 2)):
            copy.start()
        if c:
            for copy in loads(c - 1, (3, 4)):
                copy.start()
    for copy in loads(CHIPS - 1, (3, 4)):
        copy.start()
    nothing = jnp.zeros((16, 128), F32)
    for side in (0, 1):
        es[side, 0:16] = nothing
        es[side, (cells + 1) * 16 : (cells + 2) * 16] = nothing
    for ref in (us, ks, ns):
        ref[0:16] = nothing
        ref[(cells + 1) * 16 : (cells + 2) * 16] = nothing

    def at(ref, row, by=0):
        return ref[pl.ds(row + by, 8), :]

    def ahead(ref, row, here):
        return pltpu.roll(jnp.where(at_start, at(ref, row, 4), here), 127, 1)

    def behind(ref, row, here):
        return pltpu.roll(jnp.where(at_end, at(ref, row, -4), here), 1, 1)

    def up(here):
        return pltpu.roll(here, 7, 0)

    def down(here):
        return pltpu.roll(here, 1, 0)

    def first_pass(c):
        def step(i, carry):
            start = (c * rows + i * GROUP + 1) * 16
            ring = (lax.rem(c, 2) * rows + i * GROUP) * 16
            kk, uu, kx = {}, {}, {}

            def center(seen, ref, g, h):
                if (g, h) not in seen:
                    seen[g, h] = at(ref, start + g * 16 + h * 8)
                return seen[g, h]

            for h in (0, 1):
                kx[-1, h] = center(kk, ks, -1, h) + center(kk, ks, 0, h)
            for g in range(GROUP):
                for h in (0, 1):
                    row = start + g * 16 + h * 8
                    k0 = center(kk, ks, g, h)
                    kx[g, h] = k0 + center(kk, ks, g + 1, h)
                    ky, kw = k0 + ahead(ks, row, k0), k0 + behind(ks, row, k0)
                    if h == 0:
                        face_w = jnp.where(y_first, k0, kw)
                        face_y, kw = ky, jnp.where(y_first, 0.0, kw)
                    else:
                        face_y = jnp.where(y_last, k0, ky)
                        face_w, ky = kw, jnp.where(y_last, 0.0, ky)
                    kz, kv = (k0 + up(k0)) * open_up, (k0 + down(k0)) * open_down
                    mid = 24.0 - (((kx[g, h] + kx[g - 1, h]) + (face_y + face_w)) + ((kz + kv) + outer * k0))
                    for ref, value in ((fx, kx[g, h]), (fy, ky), (fw, kw), (fz, kz), (fm, mid)):
                        ref[pl.ds(ring + g * 16 + h * 8, 8), :] = value
                    v = center(uu, us, g, h)
                    out = (kx[g, h] * center(uu, us, g + 1, h) + kx[g - 1, h] * center(uu, us, g - 1, h)) + (kz * up(v) + kv * down(v))
                    out = out + (ky * ahead(us, row, v) + kw * behind(us, row, v)) + mid * v
                    ns[pl.ds(row, 8), :] = out * (-1.0 / 12.0) - at(ns, row)
            return carry

        lax.fori_loop(0, rows // GROUP, step, 0)

    def moments(c):
        def spread(ref, row, plane):
            return jnp.where(first, ref[pl.ds(row + plane, 1), :], ref[pl.ds(row + 4 + plane, 1), :])

        def step(i, carry):
            for g in range(2 * GROUP):
                row = (c * rows + 1) * 16 + (i * 2 * GROUP + g) * 8
                for side, plane in ((0, 0), (1, 3)):
                    es[side, pl.ds(row, 8), :] = of_u * spread(us, row, plane) + of_n * spread(ns, row, plane)
            return carry

        lax.fori_loop(0, rows // GROUP, step, 0)

    def second_pass(c):
        def step(i, carry):
            start = (c * rows + i * GROUP + 1) * 16
            ring = (lax.rem(c, 2) * rows + i * GROUP) * 16
            nn, kx = {}, {}

            def center(g, h):
                if (g, h) not in nn:
                    nn[g, h] = at(ns, start + g * 16 + h * 8)
                return nn[g, h]

            for h in (0, 1):
                kx[-1, h] = at(ks, start + h * 8, -16) + at(ks, start + h * 8)
            for g in range(GROUP):
                for h in (0, 1):
                    row = start + g * 16 + h * 8
                    v = center(g, h)
                    kx[g, h], ky, kw, kz, mid = (at(ref, ring + g * 16 + h * 8) for ref in (fx, fy, fw, fz, fm))
                    out = kx[g, h] * center(g + 1, h) + kx[g - 1, h] * center(g - 1, h)
                    out = out + (kz * up(v) + down(kz) * down(v))
                    out = out + (ky * ahead(ns, row, v) + kw * behind(ns, row, v)) + mid * v
                    final = out * (-1.0 / 12.0) - at(us, row)
                    ds[pl.ds(row - 16, 8), :] = at(ds, row, -16) + c0 * v + c1 * final
                    vs[pl.ds(row - 16, 8), :] = at(vs, row, -16) + c2 * v + c3 * final
            return carry

        lax.fori_loop(0, rows // GROUP, step, 0)

    def slots(c, core):
        turn = lax.rem((1 - 2 * core) * (lax.rem(c, 4) - my_y) + 8, 4)
        side = lax.rem(c // 4 + my_z, 2)
        return turn * 2 + side, side * 4 + turn

    def stores(c, core, same):
        here = pl.ds((c * rows + core * half_rows) * 16, half_rows * 16)
        y_slot, z_slot = slots(c, core)
        return [
            pltpu.make_async_copy(ds.at[here], (d_same if same else d_other).at[y_slot], out_sem.at[0, core, c]),
            pltpu.make_async_copy(vs.at[here], (v_same if same else v_other).at[z_slot], out_sem.at[1, core, c]),
        ]

    def edge_stores(c, core, same):
        here = pl.ds((c * rows + core * half_rows) * 16, (half_rows + 2) * 16)
        y_slot, z_slot = slots(c, core)
        return [
            pltpu.make_async_copy(es.at[0, here], (low_same if same else low_other).at[y_slot], edge_sem.at[0, core, c]),
            pltpu.make_async_copy(es.at[1, here], (high_same if same else high_other).at[z_slot], edge_sem.at[1, core, c]),
        ]

    def send(copies, c, core):
        for same in (True, False):
            @pl.when((my_core == core) == same)
            def _():
                for copy in copies(c, core, same):
                    copy.start()

    def chunk(c, carry):
        @pl.when(c < CHIPS)
        def _():
            @pl.when(c == 0)
            def _():
                for copy in loads(c, (0, 1, 2)):
                    copy.wait()

            @pl.when(c + 1 < CHIPS)
            def _():
                for copy in loads(c + 1, (0, 1, 2)):
                    copy.wait()

            first_pass(c)
            moments(c)
            send(edge_stores, c, 0)

        @pl.when(c > 0)
        def _():
            send(edge_stores, c - 1, 1)
            for copy in loads(c - 1, (3, 4)):
                copy.wait()
            second_pass(c - 1)
            for core in (0, 1):
                send(stores, c - 1, core)

        return carry

    lax.fori_loop(0, CHIPS + 1, chunk, 0)

    def end(c, carry):
        for core in (0, 1):
            for copy in stores(c, core, True) + edge_stores(c, core, True):
                copy.wait()
        return carry

    lax.fori_loop(0, CHIPS, end, 0)


def mend_kernel(d, v, low, high, below, above, k, k_low, k_high, d_out, v_out, ds, vs):
    rows = d.shape[0]
    slab = lax.axis_index("gz")
    lower, upper = jnp.where(slab == 0, 1.0, 0.0), jnp.where(slab == SLABS - 1, 1.0, 0.0)
    wide = rows + 2
    z = places(wide)[1]
    factor = []
    for h in (0, 1):
        under = (1.0 - lower) * (k[:, h] + roll(k_low[:, h], -3))
        over = (1.0 - upper) * (k[:, h] + roll(k_high[:, h], 3))
        factor.append(jnp.where(z == 0, under, jnp.where(z == 3, -over, 0.0)) * (1.0 / 12.0))
    from_low = [low[:, h] - below[:, h] for h in (0, 1)]
    from_high = [above[:, h] - high[:, h] for h in (0, 1)]
    direct = []
    for field, slot in ((ds, 0), (vs, 2)):
        for h in (0, 1):
            a = jnp.where(z == 0, roll(from_low[h], -slot), roll(from_high[h], 3 - slot))
            b = jnp.where(z == 0, roll(from_low[h], -slot - 1), roll(from_high[h], 2 - slot))
            w = factor[h] * a
            field[:, h] = w
            direct.append((factor[h] * b + 2.0 * jnp.abs(factor[h]) * w)[1 : rows + 1])
    for field, given, out, direct_of in ((ds, d, d_out, direct[:2]), (vs, v, v_out, direct[2:])):
        w, outflow = spread(field, k, 0, rows, lower, upper)
        for h in (0, 1):
            out[:, h] = given[:, h] + direct_of[h] - outflow[h] * (1.0 / 12.0) - 2.0 * w[h]


ANYWHERE = pl.BlockSpec(memory_space=pl.ANY)
SMEM = pl.BlockSpec(memory_space=pltpu.SMEM)


def params(mib):
    return pltpu.CompilerParams(vmem_limit_bytes=mib * MIB)


def cost(mib):
    return pl.CostEstimate(flops=0, bytes_accessed=mib * MIB, transcendentals=0)


def flat(cells):
    return cells.reshape(-1, 128)


def series(coeffs, u, k, p, cos, sin):
    cells = u.shape[0] // 16
    share = pltpu.VMEM((CHIPS, cells, 128), F32)
    edge = pltpu.VMEM((CHIPS, (cells // COUNT + 2) * 16, 128), F32)
    ring = pltpu.VMEM((2 * cells // CHIPS * 16, 128), F32)
    wide = pltpu.VMEM(((cells + 2) * 16, 128), F32)
    exact = pltpu.VMEM((cells * 16, 128), F32)
    return pl.pallas_call(
        series_kernel,
        out_shape=(share,) * 4 + (edge,) * 4,
        in_specs=[SMEM] + [ANYWHERE] * 5,
        out_specs=(ANYWHERE,) * 8,
        scratch_shapes=[wide, wide, wide, exact, exact, ring, ring, ring, ring, ring]
        + [
            pltpu.VMEM((2, (cells + 2) * 16, 128), F32),
            pltpu.SemaphoreType.DMA((5, CHIPS)),
            pltpu.SemaphoreType.DMA((2, 2, CHIPS)),
            pltpu.SemaphoreType.DMA((2, 2, CHIPS)),
        ],
        compiler_params=params(36),
        cost_estimate=cost(45),
    )(coeffs, u, k, p, cos, sin)


def mend(d, v, low, high, below, above, k, k_low, k_high):
    shape = jax.ShapeDtypeStruct(d.shape, F32)
    whole = pl.BlockSpec(memory_space=pltpu.VMEM)
    return pl.pallas_call(
        mend_kernel,
        out_shape=(shape, shape),
        in_specs=[whole] * 9,
        out_specs=(whole, whole),
        scratch_shapes=[pltpu.VMEM(k.shape, F32)] * 2,
        compiler_params=params(16),
        cost_estimate=cost(4),
    )(d, v, low, high, below, above, k, k_low, k_high)


CELL = (2, 8, 128)


def along_y(sign):
    def goal(i):
        z, y, core = i // 8, (i // 2) % 4, i % 2
        return z * 8 + ((y + sign * (1 - 2 * core)) % 4) * 2 + core

    return [(i, goal(i)) for i in range(COUNT)]


FORTH, BACK = along_y(1), along_y(-1)
ACROSS = [(i, i ^ 8) for i in range(COUNT)]
SIBLING = [(i, i ^ 1) for i in range(COUNT)]
UP = [(i, i + 1) for i in range(SLABS - 1)]
DOWN = [(i + 1, i) for i in range(SLABS - 1)]


def to_sibling(other):
    return lax.ppermute(other, "tm", SIBLING)


def forth(cells):
    return lax.ppermute(cells, "tm", FORTH)


def back(cells):
    return lax.ppermute(cells, "tm", BACK)


def across(cells):
    return lax.ppermute(cells, "tm", ACROSS)


def after(first, then):
    return lax.optimization_barrier((first, then))


def local(prev_term, last_term, cos_sum, sin_sum, speed_sq, series_coeffs):
    u, p, k = flat(packed(last_term[0])), flat(packed(prev_term[0])), flat(packed(speed_sq))
    cos, sin = flat(packed(cos_sum[0])), flat(packed(sin_sum[0]))
    rows = last_term.shape[1] // COUNT
    me = lax.axis_index("tm")

    d_other, d_same, v_other, v_same, low_other, low_same, high_other, high_same = series(series_coeffs, u, k, p, cos, sin)

    def blocks(same, came, *at):
        return lax.slice_in_dim(same, *at) + lax.slice_in_dim(came, *at)

    high_came, low_came = to_sibling(high_other), to_sibling(low_other)
    (high_came, low_came), (d_other, v_other) = after((high_came, low_came), (d_other, v_other))
    d_came, v_came = to_sibling(d_other), to_sibling(v_other)

    high_far = across(blocks(high_same, high_came, 4, 8))
    low_two = forth(blocks(low_same, low_came, 4, 6))
    low_back = back(blocks(low_same, low_came, 6, 8))
    d_two = forth(blocks(d_same, d_came, 4, 6))
    d_back = back(blocks(d_same, d_came, 6, 8))

    start = me * rows * 16
    k_here = jnp.concatenate(
        [
            jnp.where(me > 0, lax.dynamic_slice_in_dim(k, jnp.maximum(start - 16, 0), 16), 0.0),
            lax.dynamic_slice_in_dim(k, start, rows * 16),
            jnp.where(me < COUNT - 1, lax.dynamic_slice_in_dim(k, jnp.minimum(start + rows * 16, k.shape[0] - 16), 16), 0.0),
        ]
    )
    k_low, k_high = lax.ppermute(k_here, "gz", UP), lax.ppermute(k_here, "gz", DOWN)

    low_rest = forth(blocks(low_same, low_came, 2, 4) + low_two)
    v_ends, v_rest = blocks(v_same, v_came, 6, 8), blocks(v_same, v_came, 4, 6)
    (d_two, v_ends, v_rest, k_low, k_high), high_far = after((d_two, v_ends, v_rest, k_low, k_high), high_far)
    v_far_ends = across(v_ends)
    d_rest = forth(blocks(d_same, d_came, 2, 4) + d_two)

    high = blocks(high_same, high_came, 0, 4) + high_far
    high_two, high_back = forth(high[2]), back(high[3])
    low = blocks(low_same, low_came, 0, 2) + low_back + low_rest
    v_far_ends, low_sent = after(v_far_ends, low[1])
    low_far = across(low_sent)
    v_far = across(v_rest)
    high_rest = forth(high[1] + high_two)
    low = low[0] + low_far
    high = high[0] + high_back + high_rest
    above, below = lax.ppermute(low, "gz", DOWN), lax.ppermute(high, "gz", UP)

    d = blocks(d_same, d_came, 0, 2) + d_back + d_rest
    d = d[0] + across(d[1])
    v_ends = blocks(v_same, v_came, 2, 4) + v_far_ends
    v_two, v_back = forth(v_ends[0]), back(v_ends[1])
    v = blocks(v_same, v_came, 0, 2) + v_far
    (above, below), v_two = after((above, below), v_two)
    v = v[0] + v_back + forth(v[1] + v_two)

    wide = (a.reshape(rows + 2, *CELL) for a in (low, high, below, above, k_here, k_low, k_high))
    d, v = mend(d.reshape(rows, *CELL), v.reshape(rows, *CELL), *wide)
    return unpacked(d), unpacked(v)


def solution(mesh):
    return jax.shard_map(
        local,
        mesh=mesh,
        in_specs=(
            P("tm", None, "gz", None),
            P("tm", None, "gz", None),
            P("tm", None, "gz", None),
            P("tm", None, "gz", None),
            P(None, "gz", None),
            P("tm", None),
        ),
        out_specs=(P("tm", "gz", None), P("tm", "gz", None)),
        check_vma=False,
    )
```

```python
import jax
import jax.numpy as jnp
from jax import lax
from jax.experimental import pallas as pl
from jax.experimental.pallas import tpu as pltpu
from jax.sharding import PartitionSpec as P

CHIPS = 8
COUNT = 16
SLABS = 8
GROUP = 16
MIB = 1024 * 1024
F32 = jnp.float32


def packed(cells):
    x = cells.shape[0]
    return cells.reshape(x, 4, 4, 128).transpose(0, 2, 1, 3).reshape(x, 2, 8, 128)


def unpacked(cells):
    x = cells.shape[0]
    return cells.reshape(x, 4, 4, 128).transpose(0, 2, 1, 3).reshape(x, 4, 512)


def roll(cells, shift):
    return pltpu.roll(cells, shift % 8, 1)


def places(n):
    sub = lax.broadcasted_iota(jnp.int32, (n, 8, 128), 1)
    return sub, lax.rem(sub, 4), lax.broadcasted_iota(jnp.int32, (n, 8, 128), 2)


def spread(field, speed, row, n, lower, upper):
    sub, z, lane = places(n)
    first, at_start, at_end = sub < 4, lane == 0, lane == 127
    v = [field[pl.ds(row + 1, n), h] for h in (0, 1)]
    k = [speed[pl.ds(row + 1, n), h] for h in (0, 1)]

    def ahead(a, b):
        ra, rb = pltpu.roll(a, 127, 2), pltpu.roll(b, 127, 2)
        qa, qb = roll(ra, 4), roll(rb, 4)
        return (
            jnp.where(at_end, jnp.where(first, qa, qb), ra),
            jnp.where(at_end, jnp.where(first, qb, 0.0), rb),
        )

    def behind(a, b, edge):
        ra, rb = pltpu.roll(a, 1, 2), pltpu.roll(b, 1, 2)
        qa, qb = roll(ra, 4), roll(rb, 4)
        return (
            jnp.where(at_start, jnp.where(first, edge, qa), ra),
            jnp.where(at_start, jnp.where(first, qa, qb), rb),
        )

    v_y, k_y = ahead(*v), ahead(*k)
    f_y = [(k[h] + k_y[h]) * (v_y[h] - v[h]) for h in (0, 1)]
    b_y = behind(*f_y, k[0] * v[0])
    out = []
    for h in (0, 1):
        kv = k[h] * v[h]
        f_z = jnp.where(z == 3, -upper * kv, (k[h] + roll(k[h], -1)) * (roll(v[h], -1) - v[h]))
        b_z = jnp.where(z == 0, lower * kv, roll(f_z, 1))
        f_x = (k[h] + speed[pl.ds(row + 2, n), h]) * (field[pl.ds(row + 2, n), h] - v[h])
        b_x = (k[h] + speed[pl.ds(row, n), h]) * (v[h] - field[pl.ds(row, n), h])
        out.append((f_x - b_x) + (f_y[h] - b_y[h]) + (f_z - b_z))
    return v, out


def widen(scratch, main, before, after, block, blocks):
    rows = main.shape[0]
    scratch[pl.ds(1, rows)] = main[...]
    scratch[pl.ds(0, 1)] = jnp.where(block > 0, before[...], 0.0)
    scratch[pl.ds(rows + 1, 1)] = jnp.where(block < blocks - 1, after[...], 0.0)


def where_am_i():
    me = lax.axis_index("tm")
    return me // 8, lax.rem(me // 2, 4), lax.rem(me, 2)


def series_kernel(coeffs, u, k, p, cos, sin, far_other, far_same, near_other, near_same, ends_other, ends_same, rest_other, rest_same,
                  us, ks, ns, ds, vs, fx, fy, fw, fz, fm, es, in_sem, out_sem, edge_sem):
    cells = u.shape[0] // 16
    rows = cells // CHIPS
    half_rows = rows // 2
    my_z, my_y, my_core = where_am_i()
    slab = lax.axis_index("gz")
    lower, upper = jnp.where(slab == 0, 1.0, 0.0), jnp.where(slab == SLABS - 1, 1.0, 0.0)
    c0, c1, c2, c3 = (coeffs[0, i] for i in range(4))
    sub = lax.broadcasted_iota(jnp.int32, (8, 128), 0)
    lane = lax.broadcasted_iota(jnp.int32, (8, 128), 1)
    z = lax.rem(sub, 4)
    first, at_start, at_end = sub < 4, lane == 0, lane == 127
    open_up, open_down = jnp.where(z == 3, 0.0, 1.0), jnp.where(z == 0, 0.0, 1.0)
    of_u = jnp.where(z == 0, c1, jnp.where(z == 1, c0, jnp.where(z == 2, c3, c2)))
    of_n = jnp.where(z == 1, c1, jnp.where(z == 3, c3, 0.0))
    y_first, y_last = jnp.logical_and(first, at_start), jnp.logical_and(jnp.logical_not(first), at_end)
    outer = jnp.where(z == 0, lower, 0.0) + jnp.where(z == 3, upper, 0.0)

    def arrays():
        return ((u, us, 16), (k, ks, 16), (p, ns, 16), (cos, ds, 0), (sin, vs, 0))

    def loads(c, which):
        return [
            pltpu.make_async_copy(a.at[pl.ds(c * rows * 16, rows * 16)], b.at[pl.ds(c * rows * 16 + off, rows * 16)], in_sem.at[i, c])
            for i, (a, b, off) in enumerate(arrays()) if i in which
        ]

    for c in range(CHIPS):
        for copy in loads(c, (0, 1, 2)):
            copy.start()
        if c:
            for copy in loads(c - 1, (3, 4)):
                copy.start()
    for copy in loads(CHIPS - 1, (3, 4)):
        copy.start()
    nothing = jnp.zeros((16, 128), F32)
    fx[0:16] = nothing
    fz[0:16] = nothing
    for side in (0, 1):
        es[side, 0:16] = nothing
        es[side, (cells + 1) * 16 : (cells + 2) * 16] = nothing
    for ref in (us, ks, ns):
        ref[0:16] = nothing
        ref[(cells + 1) * 16 : (cells + 2) * 16] = nothing

    def at(ref, row, by=0):
        return ref[pl.ds(row + by, 8), :]

    def ahead(ref, row, here):
        return pltpu.roll(jnp.where(at_start, at(ref, row, 4), here), 127, 1)

    def behind(ref, row, here):
        return pltpu.roll(jnp.where(at_end, at(ref, row, -4), here), 1, 1)

    def up(here):
        return pltpu.roll(here, 7, 0)

    def down(here):
        return pltpu.roll(here, 1, 0)

    def first_pass(c):
        def step(i, carry):
            start = (c * rows + i * GROUP + 1) * 16
            kk, uu, kx = {}, {}, {}

            def center(seen, ref, g, h):
                if (g, h) not in seen:
                    seen[g, h] = at(ref, start + g * 16 + h * 8)
                return seen[g, h]

            for h in (0, 1):
                kx[-1, h] = center(kk, ks, -1, h) + center(kk, ks, 0, h)
            for g in range(GROUP):
                for h in (0, 1):
                    row = start + g * 16 + h * 8
                    k0 = center(kk, ks, g, h)
                    kx[g, h] = k0 + center(kk, ks, g + 1, h)
                    ky, kw = k0 + ahead(ks, row, k0), k0 + behind(ks, row, k0)
                    if h == 0:
                        face_w = jnp.where(y_first, k0, kw)
                        face_y, kw = ky, jnp.where(y_first, 0.0, kw)
                    else:
                        face_y = jnp.where(y_last, k0, ky)
                        face_w, ky = kw, jnp.where(y_last, 0.0, ky)
                    kz, kv = (k0 + up(k0)) * open_up, (k0 + down(k0)) * open_down
                    mid = 24.0 - (((kx[g, h] + kx[g - 1, h]) + (face_y + face_w)) + ((kz + kv) + outer * k0))
                    for ref, value in ((fx, kx[g, h]), (fy, ky), (fw, kw), (fz, kz), (fm, mid)):
                        ref[pl.ds(row, 8), :] = value
                    v = center(uu, us, g, h)
                    out = (kx[g, h] * center(uu, us, g + 1, h) + kx[g - 1, h] * center(uu, us, g - 1, h)) + (kz * up(v) + kv * down(v))
                    out = out + (ky * ahead(us, row, v) + kw * behind(us, row, v)) + mid * v
                    ns[pl.ds(row, 8), :] = out * (-1.0 / 12.0) - at(ns, row)
            return carry

        lax.fori_loop(0, rows // GROUP, step, 0)

    def moments(c):
        def spread(ref, row, plane):
            return jnp.where(first, ref[pl.ds(row + plane, 1), :], ref[pl.ds(row + 4 + plane, 1), :])

        def step(i, carry):
            for g in range(2 * GROUP):
                row = (c * rows + 1) * 16 + (i * 2 * GROUP + g) * 8
                for side, plane in ((0, 0), (1, 3)):
                    es[side, pl.ds(row, 8), :] = of_u * spread(us, row, plane) + of_n * spread(ns, row, plane)
            return carry

        lax.fori_loop(0, rows // GROUP, step, 0)

    def second_pass(c):
        def step(i, carry):
            start = (c * rows + i * GROUP + 1) * 16
            nn, kx = {}, {}

            def center(seen, ref, g, h):
                if (g, h) not in seen:
                    seen[g, h] = at(ref, start + g * 16 + h * 8)
                return seen[g, h]

            for g in range(GROUP):
                for h in (0, 1):
                    row = start + g * 16 + h * 8
                    v = center(nn, ns, g, h)
                    kz = at(fz, row)
                    out = center(kx, fx, g, h) * center(nn, ns, g + 1, h) + center(kx, fx, g - 1, h) * center(nn, ns, g - 1, h)
                    out = out + (kz * up(v) + down(kz) * down(v))
                    out = out + (at(fy, row) * ahead(ns, row, v) + at(fw, row) * behind(ns, row, v)) + at(fm, row) * v
                    final = out * (-1.0 / 12.0) - at(us, row)
                    ds[pl.ds(row - 16, 8), :] = at(ds, row, -16) + c0 * v + c1 * final
                    vs[pl.ds(row - 16, 8), :] = at(vs, row, -16) + c2 * v + c3 * final
            return carry

        lax.fori_loop(0, rows // GROUP, step, 0)

    def place(c, core):
        return lax.rem((1 - 2 * core) * (lax.rem(c, 4) - my_y) + 8, 4), lax.rem(c // 4 + my_z, 2)

    def stores(c, core, same, far):
        turn, _ = place(c, core)
        here = pl.ds((c * rows + core * half_rows) * 16, half_rows * 16)
        to = ((far_other, far_same) if far else (near_other, near_same))[same]
        return [pltpu.make_async_copy(a.at[here], to.at[turn, i], out_sem.at[i, core, c]) for i, a in enumerate((ds, vs))]

    def edge_stores(c, core, same, is_end):
        turn, side = place(c, core)
        here = pl.ds((c * rows + core * half_rows) * 16, (half_rows + 2) * 16)
        to = ((ends_other, ends_same) if is_end else (rest_other, rest_same))[same]
        return [pltpu.make_async_copy(es.at[i, here], to.at[lax.rem(turn, 2), side, i], edge_sem.at[i, core, c]) for i in (0, 1)]

    def send(copies, c, core, test):
        for same in (0, 1):
            for kind in (0, 1):
                @pl.when(((my_core == core) == (same == 1)) & (test(*place(c, core)) == (kind == 1)))
                def _():
                    for copy in copies(c, core, same, kind):
                        copy.start()

    def send_edges(c, core):
        send(edge_stores, c, core, lambda turn, side: turn >= 2)

    def send_series(c, core):
        send(stores, c, core, lambda turn, side: side == 1)

    def chunk(c, carry):
        @pl.when(c < CHIPS)
        def _():
            @pl.when(c == 0)
            def _():
                for copy in loads(c, (0, 1, 2)):
                    copy.wait()

            @pl.when(c + 1 < CHIPS)
            def _():
                for copy in loads(c + 1, (0, 1, 2)):
                    copy.wait()

            first_pass(c)
            moments(c)
            send_edges(c, 0)

        @pl.when(c > 0)
        def _():
            send_edges(c - 1, 1)
            for copy in loads(c - 1, (3, 4)):
                copy.wait()
            second_pass(c - 1)
            for core in (0, 1):
                send_series(c - 1, core)

        return carry

    lax.fori_loop(0, CHIPS + 1, chunk, 0)

    def end(c, carry):
        for core in (0, 1):
            for copy in stores(c, core, 1, 1) + edge_stores(c, core, 1, 1):
                copy.wait()
        return carry

    lax.fori_loop(0, CHIPS, end, 0)


def mend_kernel(d, v, low, high, below, above, k, k_low, k_high, d_out, v_out, ds, vs):
    rows = d.shape[0]
    slab = lax.axis_index("gz")
    lower, upper = jnp.where(slab == 0, 1.0, 0.0), jnp.where(slab == SLABS - 1, 1.0, 0.0)
    wide = rows + 2
    z = places(wide)[1]
    factor = []
    for h in (0, 1):
        under = (1.0 - lower) * (k[:, h] + roll(k_low[:, h], -3))
        over = (1.0 - upper) * (k[:, h] + roll(k_high[:, h], 3))
        factor.append(jnp.where(z == 0, under, jnp.where(z == 3, -over, 0.0)) * (1.0 / 12.0))
    from_low = [low[:, h] - below[:, h] for h in (0, 1)]
    from_high = [above[:, h] - high[:, h] for h in (0, 1)]
    direct = []
    for field, slot in ((ds, 0), (vs, 2)):
        for h in (0, 1):
            a = jnp.where(z == 0, roll(from_low[h], -slot), roll(from_high[h], 3 - slot))
            b = jnp.where(z == 0, roll(from_low[h], -slot - 1), roll(from_high[h], 2 - slot))
            w = factor[h] * a
            field[:, h] = w
            direct.append((factor[h] * b + 2.0 * jnp.abs(factor[h]) * w)[1 : rows + 1])
    for field, given, out, direct_of in ((ds, d, d_out, direct[:2]), (vs, v, v_out, direct[2:])):
        w, outflow = spread(field, k, 0, rows, lower, upper)
        for h in (0, 1):
            out[:, h] = given[:, h] + direct_of[h] - outflow[h] * (1.0 / 12.0) - 2.0 * w[h]


ANYWHERE = pl.BlockSpec(memory_space=pl.ANY)
SMEM = pl.BlockSpec(memory_space=pltpu.SMEM)


def params(mib):
    return pltpu.CompilerParams(vmem_limit_bytes=mib * MIB)


def cost(mib):
    return pl.CostEstimate(flops=0, bytes_accessed=mib * MIB, transcendentals=0)


def flat(cells):
    return cells.reshape(-1, 128)


def series(coeffs, u, k, p, cos, sin):
    cells = u.shape[0] // 16
    share = jax.ShapeDtypeStruct((4, 2, cells // COUNT * 16, 128), F32)
    edge = jax.ShapeDtypeStruct((2, 2, 2, (cells // COUNT + 2) * 16, 128), F32)
    wide = pltpu.VMEM(((cells + 2) * 16, 128), F32)
    exact = pltpu.VMEM((cells * 16, 128), F32)
    return pl.pallas_call(
        series_kernel,
        out_shape=(share,) * 4 + (edge,) * 4,
        in_specs=[SMEM] + [ANYWHERE] * 5,
        out_specs=(ANYWHERE,) * 8,
        scratch_shapes=[wide, wide, wide, exact, exact, wide, wide, wide, wide, wide]
        + [
            pltpu.VMEM((2, (cells + 2) * 16, 128), F32),
            pltpu.SemaphoreType.DMA((5, CHIPS)),
            pltpu.SemaphoreType.DMA((2, 2, CHIPS)),
            pltpu.SemaphoreType.DMA((2, 2, CHIPS)),
        ],
        compiler_params=params(56),
        cost_estimate=cost(45),
    )(coeffs, u, k, p, cos, sin)


def mend(d, v, low, high, below, above, k, k_low, k_high):
    shape = jax.ShapeDtypeStruct(d.shape, F32)
    whole = pl.BlockSpec(memory_space=pltpu.VMEM)
    return pl.pallas_call(
        mend_kernel,
        out_shape=(shape, shape),
        in_specs=[whole] * 9,
        out_specs=(whole, whole),
        scratch_shapes=[pltpu.VMEM(k.shape, F32)] * 2,
        compiler_params=params(16),
        cost_estimate=cost(4),
    )(d, v, low, high, below, above, k, k_low, k_high)


CELL = (2, 8, 128)


def along_y(sign):
    def goal(i):
        z, y, core = i // 8, (i // 2) % 4, i % 2
        return z * 8 + ((y + sign * (1 - 2 * core)) % 4) * 2 + core

    return [(i, goal(i)) for i in range(COUNT)]


FORTH, BACK = along_y(1), along_y(-1)
ACROSS = [(i, i ^ 8) for i in range(COUNT)]
SIBLING = [(i, i ^ 1) for i in range(COUNT)]
UP = [(i, i + 1) for i in range(SLABS - 1)]
DOWN = [(i + 1, i) for i in range(SLABS - 1)]


def to_sibling(other):
    return lax.ppermute(other, "tm", SIBLING)


def forth(cells):
    return lax.ppermute(cells, "tm", FORTH)


def back(cells):
    return lax.ppermute(cells, "tm", BACK)


def across(cells):
    return lax.ppermute(cells, "tm", ACROSS)


def after(first, then):
    return lax.optimization_barrier((first, then))


def local(prev_term, last_term, cos_sum, sin_sum, speed_sq, series_coeffs):
    u, p, k = flat(packed(last_term[0])), flat(packed(prev_term[0])), flat(packed(speed_sq))
    cos, sin = flat(packed(cos_sum[0])), flat(packed(sin_sum[0]))
    rows = last_term.shape[1] // COUNT
    me = lax.axis_index("tm")

    outs = series(series_coeffs, u, k, p, cos, sin)
    far_other, far_same, near_other, near_same, ends_other, ends_same, rest_other, rest_same = outs

    far_came, ends_came = to_sibling(far_other), to_sibling(ends_other)
    rest_came, near_came = to_sibling(rest_other), to_sibling(near_other)
    far_came = across(far_same + far_came)
    ends_two = forth(ends_same[0] + ends_came[0])
    ends_back = back(ends_same[1] + ends_came[1])

    start = me * rows * 16
    k_here = jnp.concatenate(
        [
            jnp.where(me > 0, lax.dynamic_slice_in_dim(k, jnp.maximum(start - 16, 0), 16), 0.0),
            lax.dynamic_slice_in_dim(k, start, rows * 16),
            jnp.where(me < COUNT - 1, lax.dynamic_slice_in_dim(k, jnp.minimum(start + rows * 16, k.shape[0] - 16), 16), 0.0),
        ]
    )
    k_low, k_high = lax.ppermute(k_here, "gz", UP), lax.ppermute(k_here, "gz", DOWN)

    ring = forth(rest_same[1] + rest_came[1] + ends_two)
    (k_low, k_high, near_came), far_came = after((k_low, k_high, near_came), far_came)
    edge_far = across(rest_same[0, 1] + rest_came[0, 1] + ends_back[1] + ring[1])
    edge = rest_same[0, 0] + rest_came[0, 0] + ends_back[0] + ring[0] + edge_far
    low, high = edge[0], edge[1]
    above, below = lax.ppermute(low, "gz", DOWN), lax.ppermute(high, "gz", UP)

    def both(turn):
        return near_same[turn] + near_came[turn] + far_came[turn]

    two, direct = forth(both(2)), back(both(3))
    result = both(0) + direct + forth(both(1) + two)
    d, v = result[0], result[1]

    wide = (a.reshape(rows + 2, *CELL) for a in (low, high, below, above, k_here, k_low, k_high))
    d, v = mend(d.reshape(rows, *CELL), v.reshape(rows, *CELL), *wide)
    return unpacked(d), unpacked(v)


def solution(mesh):
    return jax.shard_map(
        local,
        mesh=mesh,
        in_specs=(
            P("tm", None, "gz", None),
            P("tm", None, "gz", None),
            P("tm", None, "gz", None),
            P("tm", None, "gz", None),
            P(None, "gz", None),
            P("tm", None),
        ),
        out_specs=(P("tm", "gz", None), P("tm", "gz", None)),
        check_vma=False,
    )
```

```python
import jax
import jax.numpy as jnp
from jax import lax
from jax.experimental import pallas as pl
from jax.experimental.pallas import tpu as pltpu
from jax.sharding import PartitionSpec as P

CHIPS = 8
COUNT = 16
SLABS = 8
GROUP = 16
MIB = 1024 * 1024
F32 = jnp.float32


def packed(cells):
    x = cells.shape[0]
    return cells.reshape(x, 4, 4, 128).transpose(0, 2, 1, 3).reshape(x, 2, 8, 128)


def unpacked(cells):
    x = cells.shape[0]
    return cells.reshape(x, 4, 4, 128).transpose(0, 2, 1, 3).reshape(x, 4, 512)


def roll(cells, shift):
    return pltpu.roll(cells, shift % 8, 1)


def places(n):
    sub = lax.broadcasted_iota(jnp.int32, (n, 8, 128), 1)
    return sub, lax.rem(sub, 4), lax.broadcasted_iota(jnp.int32, (n, 8, 128), 2)


def spread(field, speed, row, n, lower, upper):
    sub, z, lane = places(n)
    first, at_start, at_end = sub < 4, lane == 0, lane == 127
    v = [field[pl.ds(row + 1, n), h] for h in (0, 1)]
    k = [speed[pl.ds(row + 1, n), h] for h in (0, 1)]

    def ahead(a, b):
        ra, rb = pltpu.roll(a, 127, 2), pltpu.roll(b, 127, 2)
        qa, qb = roll(ra, 4), roll(rb, 4)
        return (
            jnp.where(at_end, jnp.where(first, qa, qb), ra),
            jnp.where(at_end, jnp.where(first, qb, 0.0), rb),
        )

    def behind(a, b, edge):
        ra, rb = pltpu.roll(a, 1, 2), pltpu.roll(b, 1, 2)
        qa, qb = roll(ra, 4), roll(rb, 4)
        return (
            jnp.where(at_start, jnp.where(first, edge, qa), ra),
            jnp.where(at_start, jnp.where(first, qa, qb), rb),
        )

    v_y, k_y = ahead(*v), ahead(*k)
    f_y = [(k[h] + k_y[h]) * (v_y[h] - v[h]) for h in (0, 1)]
    b_y = behind(*f_y, k[0] * v[0])
    out = []
    for h in (0, 1):
        kv = k[h] * v[h]
        f_z = jnp.where(z == 3, -upper * kv, (k[h] + roll(k[h], -1)) * (roll(v[h], -1) - v[h]))
        b_z = jnp.where(z == 0, lower * kv, roll(f_z, 1))
        f_x = (k[h] + speed[pl.ds(row + 2, n), h]) * (field[pl.ds(row + 2, n), h] - v[h])
        b_x = (k[h] + speed[pl.ds(row, n), h]) * (v[h] - field[pl.ds(row, n), h])
        out.append((f_x - b_x) + (f_y[h] - b_y[h]) + (f_z - b_z))
    return v, out


def widen(scratch, main, before, after, block, blocks):
    rows = main.shape[0]
    scratch[pl.ds(1, rows)] = main[...]
    scratch[pl.ds(0, 1)] = jnp.where(block > 0, before[...], 0.0)
    scratch[pl.ds(rows + 1, 1)] = jnp.where(block < blocks - 1, after[...], 0.0)


def where_am_i():
    me = lax.axis_index("tm")
    return me // 8, lax.rem(me // 2, 4), lax.rem(me, 2)


def series_kernel(coeffs, u, k, p, cos, sin, far_other, far_same, near_other, near_same, ends_other, ends_same, rest_other, rest_same,
                  us, ks, ns, ds, vs, fx, fy, fw, fz, fm, es, in_sem, out_sem, edge_sem):
    cells = u.shape[0] // 16
    rows = cells // CHIPS
    half_rows = rows // 2
    my_z, my_y, my_core = where_am_i()
    slab = lax.axis_index("gz")
    lower, upper = jnp.where(slab == 0, 1.0, 0.0), jnp.where(slab == SLABS - 1, 1.0, 0.0)
    c0, c1, c2, c3 = (coeffs[0, i] for i in range(4))
    sub = lax.broadcasted_iota(jnp.int32, (8, 128), 0)
    lane = lax.broadcasted_iota(jnp.int32, (8, 128), 1)
    z = lax.rem(sub, 4)
    first, at_start, at_end = sub < 4, lane == 0, lane == 127
    open_up, open_down = jnp.where(z == 3, 0.0, 1.0), jnp.where(z == 0, 0.0, 1.0)
    of_u = jnp.where(z == 0, c1, jnp.where(z == 1, c0, jnp.where(z == 2, c3, c2)))
    of_n = jnp.where(z == 1, c1, jnp.where(z == 3, c3, 0.0))
    y_first, y_last = jnp.logical_and(first, at_start), jnp.logical_and(jnp.logical_not(first), at_end)
    outer = jnp.where(z == 0, lower, 0.0) + jnp.where(z == 3, upper, 0.0)

    def arrays():
        return ((u, us, 16), (k, ks, 16), (p, ns, 16), (cos, ds, 0), (sin, vs, 0))

    def loads(c, which):
        return [
            pltpu.make_async_copy(a.at[pl.ds(c * rows * 16, rows * 16)], b.at[pl.ds(c * rows * 16 + off, rows * 16)], in_sem.at[i, c])
            for i, (a, b, off) in enumerate(arrays()) if i in which
        ]

    for c in range(CHIPS):
        for copy in loads(c, (0, 1, 2)):
            copy.start()
        if c:
            for copy in loads(c - 1, (3, 4)):
                copy.start()
    for copy in loads(CHIPS - 1, (3, 4)):
        copy.start()
    nothing = jnp.zeros((16, 128), F32)
    fx[0:16] = nothing
    fz[0:16] = nothing
    for side in (0, 1):
        es[side, 0:16] = nothing
        es[side, (cells + 1) * 16 : (cells + 2) * 16] = nothing
    for ref in (us, ks, ns):
        ref[0:16] = nothing
        ref[(cells + 1) * 16 : (cells + 2) * 16] = nothing

    def at(ref, row, by=0):
        return ref[pl.ds(row + by, 8), :]

    def ahead(ref, row, here):
        return pltpu.roll(jnp.where(at_start, at(ref, row, 4), here), 127, 1)

    def behind(ref, row, here):
        return pltpu.roll(jnp.where(at_end, at(ref, row, -4), here), 1, 1)

    def up(here):
        return pltpu.roll(here, 7, 0)

    def down(here):
        return pltpu.roll(here, 1, 0)

    def first_pass(c):
        def step(i, carry):
            start = (c * rows + i * GROUP + 1) * 16
            kk, uu, kx = {}, {}, {}

            def center(seen, ref, g, h):
                if (g, h) not in seen:
                    seen[g, h] = at(ref, start + g * 16 + h * 8)
                return seen[g, h]

            for h in (0, 1):
                kx[-1, h] = center(kk, ks, -1, h) + center(kk, ks, 0, h)
            for g in range(GROUP):
                for h in (0, 1):
                    row = start + g * 16 + h * 8
                    k0 = center(kk, ks, g, h)
                    kx[g, h] = k0 + center(kk, ks, g + 1, h)
                    ky, kw = k0 + ahead(ks, row, k0), k0 + behind(ks, row, k0)
                    if h == 0:
                        face_w = jnp.where(y_first, k0, kw)
                        face_y, kw = ky, jnp.where(y_first, 0.0, kw)
                    else:
                        face_y = jnp.where(y_last, k0, ky)
                        face_w, ky = kw, jnp.where(y_last, 0.0, ky)
                    kz, kv = (k0 + up(k0)) * open_up, (k0 + down(k0)) * open_down
                    mid = 24.0 - (((kx[g, h] + kx[g - 1, h]) + (face_y + face_w)) + ((kz + kv) + outer * k0))
                    for ref, value in ((fx, kx[g, h]), (fy, ky), (fw, kw), (fz, kz), (fm, mid)):
                        ref[pl.ds(row, 8), :] = value
                    v = center(uu, us, g, h)
                    out = (kx[g, h] * center(uu, us, g + 1, h) + kx[g - 1, h] * center(uu, us, g - 1, h)) + (kz * up(v) + kv * down(v))
                    out = out + (ky * ahead(us, row, v) + kw * behind(us, row, v)) + mid * v
                    ns[pl.ds(row, 8), :] = out * (-1.0 / 12.0) - at(ns, row)
            return carry

        lax.fori_loop(0, rows // GROUP, step, 0)

    def moments(c):
        def spread(ref, row, plane):
            return jnp.where(first, ref[pl.ds(row + plane, 1), :], ref[pl.ds(row + 4 + plane, 1), :])

        def step(i, carry):
            for g in range(2 * GROUP):
                row = (c * rows + 1) * 16 + (i * 2 * GROUP + g) * 8
                for side, plane in ((0, 0), (1, 3)):
                    es[side, pl.ds(row, 8), :] = of_u * spread(us, row, plane) + of_n * spread(ns, row, plane)
            return carry

        lax.fori_loop(0, rows // GROUP, step, 0)

    def second_pass(c):
        def step(i, carry):
            start = (c * rows + i * GROUP + 1) * 16
            nn, kx = {}, {}

            def center(seen, ref, g, h):
                if (g, h) not in seen:
                    seen[g, h] = at(ref, start + g * 16 + h * 8)
                return seen[g, h]

            for g in range(GROUP):
                for h in (0, 1):
                    row = start + g * 16 + h * 8
                    v = center(nn, ns, g, h)
                    kz = at(fz, row)
                    out = center(kx, fx, g, h) * center(nn, ns, g + 1, h) + center(kx, fx, g - 1, h) * center(nn, ns, g - 1, h)
                    out = out + (kz * up(v) + down(kz) * down(v))
                    out = out + (at(fy, row) * ahead(ns, row, v) + at(fw, row) * behind(ns, row, v)) + at(fm, row) * v
                    final = out * (-1.0 / 12.0) - at(us, row)
                    ds[pl.ds(row - 16, 8), :] = at(ds, row, -16) + c0 * v + c1 * final
                    vs[pl.ds(row - 16, 8), :] = at(vs, row, -16) + c2 * v + c3 * final
            return carry

        lax.fori_loop(0, rows // GROUP, step, 0)

    def place(c, core):
        return lax.rem((1 - 2 * core) * (lax.rem(c, 4) - my_y) + 8, 4), lax.rem(c // 4 + my_z, 2)

    def stores(c, core, same, far):
        turn, _ = place(c, core)
        here = pl.ds((c * rows + core * half_rows) * 16, half_rows * 16)
        to = ((far_other, far_same) if far else (near_other, near_same))[same]
        return [pltpu.make_async_copy(a.at[here], to.at[turn, i], out_sem.at[i, core, c]) for i, a in enumerate((ds, vs))]

    def edge_stores(c, core, same, is_end):
        turn, side = place(c, core)
        here = pl.ds((c * rows + core * half_rows) * 16, (half_rows + 2) * 16)
        to = ((ends_other, ends_same) if is_end else (rest_other, rest_same))[same]
        return [pltpu.make_async_copy(es.at[i, here], to.at[lax.rem(turn, 2), side, i], edge_sem.at[i, core, c]) for i in (0, 1)]

    def send(copies, c, core, test):
        for same in (0, 1):
            for kind in (0, 1):
                @pl.when(((my_core == core) == (same == 1)) & (test(*place(c, core)) == (kind == 1)))
                def _():
                    for copy in copies(c, core, same, kind):
                        copy.start()

    def send_edges(c, core):
        send(edge_stores, c, core, lambda turn, side: turn >= 2)

    def send_series(c, core):
        send(stores, c, core, lambda turn, side: side == 1)

    def chunk(c, carry):
        @pl.when(c < CHIPS)
        def _():
            @pl.when(c == 0)
            def _():
                for copy in loads(c, (0, 1, 2)):
                    copy.wait()

            @pl.when(c + 1 < CHIPS)
            def _():
                for copy in loads(c + 1, (0, 1, 2)):
                    copy.wait()

            first_pass(c)
            moments(c)
            send_edges(c, 0)

        @pl.when(c > 0)
        def _():
            send_edges(c - 1, 1)
            for copy in loads(c - 1, (3, 4)):
                copy.wait()
            second_pass(c - 1)
            for core in (0, 1):
                send_series(c - 1, core)

        return carry

    lax.fori_loop(0, CHIPS + 1, chunk, 0)

    def end(c, carry):
        for core in (0, 1):
            for copy in stores(c, core, 1, 1) + edge_stores(c, core, 1, 1):
                copy.wait()
        return carry

    lax.fori_loop(0, CHIPS, end, 0)


def mend_kernel(d, v, low, high, below, above, k, k_low, k_high, d_out, v_out, ds, vs):
    rows = d.shape[0]
    slab = lax.axis_index("gz")
    lower, upper = jnp.where(slab == 0, 1.0, 0.0), jnp.where(slab == SLABS - 1, 1.0, 0.0)
    wide = rows + 2
    z = places(wide)[1]
    factor = []
    for h in (0, 1):
        under = (1.0 - lower) * (k[:, h] + roll(k_low[:, h], -3))
        over = (1.0 - upper) * (k[:, h] + roll(k_high[:, h], 3))
        factor.append(jnp.where(z == 0, under, jnp.where(z == 3, -over, 0.0)) * (1.0 / 12.0))
    from_low = [low[:, h] - below[:, h] for h in (0, 1)]
    from_high = [above[:, h] - high[:, h] for h in (0, 1)]
    direct = []
    for field, slot in ((ds, 0), (vs, 2)):
        for h in (0, 1):
            a = jnp.where(z == 0, roll(from_low[h], -slot), roll(from_high[h], 3 - slot))
            b = jnp.where(z == 0, roll(from_low[h], -slot - 1), roll(from_high[h], 2 - slot))
            w = factor[h] * a
            field[:, h] = w
            direct.append((factor[h] * b + 2.0 * jnp.abs(factor[h]) * w)[1 : rows + 1])
    for field, given, out, direct_of in ((ds, d, d_out, direct[:2]), (vs, v, v_out, direct[2:])):
        w, outflow = spread(field, k, 0, rows, lower, upper)
        for h in (0, 1):
            out[:, h] = given[:, h] + direct_of[h] - outflow[h] * (1.0 / 12.0) - 2.0 * w[h]


ANYWHERE = pl.BlockSpec(memory_space=pl.ANY)
SMEM = pl.BlockSpec(memory_space=pltpu.SMEM)


def params(mib):
    return pltpu.CompilerParams(vmem_limit_bytes=mib * MIB)


def cost(mib):
    return pl.CostEstimate(flops=0, bytes_accessed=mib * MIB, transcendentals=0)


def flat(cells):
    return cells.reshape(-1, 128)


def series(coeffs, u, k, p, cos, sin):
    cells = u.shape[0] // 16
    share = jax.ShapeDtypeStruct((4, 2, cells // COUNT * 16, 128), F32)
    edge = jax.ShapeDtypeStruct((2, 2, 2, (cells // COUNT + 2) * 16, 128), F32)
    wide = pltpu.VMEM(((cells + 2) * 16, 128), F32)
    exact = pltpu.VMEM((cells * 16, 128), F32)
    return pl.pallas_call(
        series_kernel,
        out_shape=(share,) * 4 + (edge,) * 4,
        in_specs=[SMEM] + [ANYWHERE] * 5,
        out_specs=(ANYWHERE,) * 8,
        scratch_shapes=[wide, wide, wide, exact, exact, wide, wide, wide, wide, wide]
        + [
            pltpu.VMEM((2, (cells + 2) * 16, 128), F32),
            pltpu.SemaphoreType.DMA((5, CHIPS)),
            pltpu.SemaphoreType.DMA((2, 2, CHIPS)),
            pltpu.SemaphoreType.DMA((2, 2, CHIPS)),
        ],
        compiler_params=params(56),
        cost_estimate=cost(45),
    )(coeffs, u, k, p, cos, sin)


def mend(d, v, low, high, below, above, k, k_low, k_high):
    shape = jax.ShapeDtypeStruct(d.shape, F32)
    whole = pl.BlockSpec(memory_space=pltpu.VMEM)
    return pl.pallas_call(
        mend_kernel,
        out_shape=(shape, shape),
        in_specs=[whole] * 9,
        out_specs=(whole, whole),
        scratch_shapes=[pltpu.VMEM(k.shape, F32)] * 2,
        compiler_params=params(16),
        cost_estimate=cost(4),
    )(d, v, low, high, below, above, k, k_low, k_high)


CELL = (2, 8, 128)


def along_y(sign):
    def goal(i):
        z, y, core = i // 8, (i // 2) % 4, i % 2
        return z * 8 + ((y + sign * (1 - 2 * core)) % 4) * 2 + core

    return [(i, goal(i)) for i in range(COUNT)]


FORTH, BACK = along_y(1), along_y(-1)
ACROSS = [(i, i ^ 8) for i in range(COUNT)]
SIBLING = [(i, i ^ 1) for i in range(COUNT)]
UP = [(i, i + 1) for i in range(SLABS - 1)]
DOWN = [(i + 1, i) for i in range(SLABS - 1)]


def to_sibling(other):
    return lax.ppermute(other, "tm", SIBLING)


def forth(cells):
    return lax.ppermute(cells, "tm", FORTH)


def back(cells):
    return lax.ppermute(cells, "tm", BACK)


def across(cells):
    return lax.ppermute(cells, "tm", ACROSS)


def after(first, then):
    return lax.optimization_barrier((first, then))


def local(prev_term, last_term, cos_sum, sin_sum, speed_sq, series_coeffs):
    u, p, k = flat(packed(last_term[0])), flat(packed(prev_term[0])), flat(packed(speed_sq))
    cos, sin = flat(packed(cos_sum[0])), flat(packed(sin_sum[0]))
    rows = last_term.shape[1] // COUNT
    me = lax.axis_index("tm")

    outs = series(series_coeffs, u, k, p, cos, sin)
    far_other, far_same, near_other, near_same, ends_other, ends_same, rest_other, rest_same = outs

    ends_came, far_came = to_sibling(ends_other), to_sibling(far_other)
    rest_came, near_came = to_sibling(rest_other), to_sibling(near_other)
    ends_two = forth(ends_same[0] + ends_came[0])
    far_ends = far_same[2:] + far_came[2:]
    far_ends, ends_came = after(far_ends, ends_came)
    far_ends_came, far_rest_came = across(far_ends), across(far_same[:2] + far_came[:2])
    ends_back = back(ends_same[1] + ends_came[1])

    start = me * rows * 16
    k_here = jnp.concatenate(
        [
            jnp.where(me > 0, lax.dynamic_slice_in_dim(k, jnp.maximum(start - 16, 0), 16), 0.0),
            lax.dynamic_slice_in_dim(k, start, rows * 16),
            jnp.where(me < COUNT - 1, lax.dynamic_slice_in_dim(k, jnp.minimum(start + rows * 16, k.shape[0] - 16), 16), 0.0),
        ]
    )
    k_low, k_high = lax.ppermute(k_here, "gz", UP), lax.ppermute(k_here, "gz", DOWN)

    ring = forth(rest_same[1] + rest_came[1] + ends_two)
    two, direct = (near_same[t] + near_came[t] + far_ends_came[t - 2] for t in (2, 3))
    (two, direct, k_low, k_high), ring = after((two, direct, k_low, k_high), ring)
    two, direct = forth(two), back(direct)
    edge_far = rest_same[0, 1] + rest_came[0, 1] + ends_back[1] + ring[1]
    edge_far, far_rest_came = after(edge_far, far_rest_came)
    edge_far = across(edge_far)
    last = near_same[1] + near_came[1] + far_rest_came[1] + two
    last, edge_far = after(last, edge_far)
    last = forth(last)
    edge = rest_same[0, 0] + rest_came[0, 0] + ends_back[0] + ring[0] + edge_far
    low, high = edge[0], edge[1]
    above, below = lax.ppermute(low, "gz", DOWN), lax.ppermute(high, "gz", UP)
    result = near_same[0] + near_came[0] + far_rest_came[0] + direct + last
    d, v = result[0], result[1]

    wide = (a.reshape(rows + 2, *CELL) for a in (low, high, below, above, k_here, k_low, k_high))
    d, v = mend(d.reshape(rows, *CELL), v.reshape(rows, *CELL), *wide)
    return unpacked(d), unpacked(v)


def solution(mesh):
    return jax.shard_map(
        local,
        mesh=mesh,
        in_specs=(
            P("tm", None, "gz", None),
            P("tm", None, "gz", None),
            P("tm", None, "gz", None),
            P("tm", None, "gz", None),
            P(None, "gz", None),
            P("tm", None),
        ),
        out_specs=(P("tm", "gz", None), P("tm", "gz", None)),
        check_vma=False,
    )
```

```python
import jax
import jax.numpy as jnp
from jax import lax
from jax.experimental import pallas as pl
from jax.experimental.pallas import tpu as pltpu
from jax.sharding import PartitionSpec as P

CHIPS = 8
COUNT = 16
SLABS = 8
GROUP = 16
MIB = 1024 * 1024
F32 = jnp.float32


def packed(cells):
    x = cells.shape[0]
    return cells.reshape(x, 4, 4, 128).transpose(0, 2, 1, 3).reshape(x, 2, 8, 128)


def unpacked(cells):
    x = cells.shape[0]
    return cells.reshape(x, 4, 4, 128).transpose(0, 2, 1, 3).reshape(x, 4, 512)


def roll(cells, shift):
    return pltpu.roll(cells, shift % 8, 1)


def places(n):
    sub = lax.broadcasted_iota(jnp.int32, (n, 8, 128), 1)
    return sub, lax.rem(sub, 4), lax.broadcasted_iota(jnp.int32, (n, 8, 128), 2)


def spread(field, speed, row, n, lower, upper):
    sub, z, lane = places(n)
    first, at_start, at_end = sub < 4, lane == 0, lane == 127
    v = [field[pl.ds(row + 1, n), h] for h in (0, 1)]
    k = [speed[pl.ds(row + 1, n), h] for h in (0, 1)]

    def ahead(a, b):
        ra, rb = pltpu.roll(a, 127, 2), pltpu.roll(b, 127, 2)
        qa, qb = roll(ra, 4), roll(rb, 4)
        return (
            jnp.where(at_end, jnp.where(first, qa, qb), ra),
            jnp.where(at_end, jnp.where(first, qb, 0.0), rb),
        )

    def behind(a, b, edge):
        ra, rb = pltpu.roll(a, 1, 2), pltpu.roll(b, 1, 2)
        qa, qb = roll(ra, 4), roll(rb, 4)
        return (
            jnp.where(at_start, jnp.where(first, edge, qa), ra),
            jnp.where(at_start, jnp.where(first, qa, qb), rb),
        )

    v_y, k_y = ahead(*v), ahead(*k)
    f_y = [(k[h] + k_y[h]) * (v_y[h] - v[h]) for h in (0, 1)]
    b_y = behind(*f_y, k[0] * v[0])
    out = []
    for h in (0, 1):
        kv = k[h] * v[h]
        f_z = jnp.where(z == 3, -upper * kv, (k[h] + roll(k[h], -1)) * (roll(v[h], -1) - v[h]))
        b_z = jnp.where(z == 0, lower * kv, roll(f_z, 1))
        f_x = (k[h] + speed[pl.ds(row + 2, n), h]) * (field[pl.ds(row + 2, n), h] - v[h])
        b_x = (k[h] + speed[pl.ds(row, n), h]) * (v[h] - field[pl.ds(row, n), h])
        out.append((f_x - b_x) + (f_y[h] - b_y[h]) + (f_z - b_z))
    return v, out


def widen(scratch, main, before, after, block, blocks):
    rows = main.shape[0]
    scratch[pl.ds(1, rows)] = main[...]
    scratch[pl.ds(0, 1)] = jnp.where(block > 0, before[...], 0.0)
    scratch[pl.ds(rows + 1, 1)] = jnp.where(block < blocks - 1, after[...], 0.0)


def where_am_i():
    me = lax.axis_index("tm")
    return me // 8, lax.rem(me // 2, 4), lax.rem(me, 2)


def series_kernel(coeffs, u, k, p, cos, sin, far_other, far_same, near_other, near_same, ends_other, ends_same, rest_other, rest_same,
                  us, ks, ns, ds, vs, fx, fy, fw, fz, fm, es, in_sem, out_sem, edge_sem):
    cells = u.shape[0] // 16
    rows = cells // CHIPS
    half_rows = rows // 2
    my_z, my_y, my_core = where_am_i()
    slab = lax.axis_index("gz")
    lower, upper = jnp.where(slab == 0, 1.0, 0.0), jnp.where(slab == SLABS - 1, 1.0, 0.0)
    c0, c1, c2, c3 = (coeffs[0, i] for i in range(4))
    sub = lax.broadcasted_iota(jnp.int32, (8, 128), 0)
    lane = lax.broadcasted_iota(jnp.int32, (8, 128), 1)
    z = lax.rem(sub, 4)
    first, at_start, at_end = sub < 4, lane == 0, lane == 127
    open_up, open_down = jnp.where(z == 3, 0.0, 1.0), jnp.where(z == 0, 0.0, 1.0)
    of_u = jnp.where(z == 0, c1, jnp.where(z == 1, c0, jnp.where(z == 2, c3, c2)))
    of_n = jnp.where(z == 1, c1, jnp.where(z == 3, c3, 0.0))
    y_first, y_last = jnp.logical_and(first, at_start), jnp.logical_and(jnp.logical_not(first), at_end)
    outer = jnp.where(z == 0, lower, 0.0) + jnp.where(z == 3, upper, 0.0)

    def arrays():
        return ((u, us, 16), (k, ks, 16), (p, ns, 16), (cos, ds, 0), (sin, vs, 0))

    def loads(c, which):
        return [
            pltpu.make_async_copy(a.at[pl.ds(c * rows * 16, rows * 16)], b.at[pl.ds(c * rows * 16 + off, rows * 16)], in_sem.at[i, c])
            for i, (a, b, off) in enumerate(arrays()) if i in which
        ]

    for c in range(CHIPS):
        for copy in loads(c, (0, 1, 2)):
            copy.start()
        if c:
            for copy in loads(c - 1, (3, 4)):
                copy.start()
    for copy in loads(CHIPS - 1, (3, 4)):
        copy.start()
    nothing = jnp.zeros((16, 128), F32)
    fx[0:16] = nothing
    fz[0:16] = nothing
    for side in (0, 1):
        es[side, 0:16] = nothing
        es[side, (cells + 1) * 16 : (cells + 2) * 16] = nothing
    for ref in (us, ks, ns):
        ref[0:16] = nothing
        ref[(cells + 1) * 16 : (cells + 2) * 16] = nothing

    def at(ref, row, by=0):
        return ref[pl.ds(row + by, 8), :]

    def ahead(ref, row, here):
        return pltpu.roll(jnp.where(at_start, at(ref, row, 4), here), 127, 1)

    def behind(ref, row, here):
        return pltpu.roll(jnp.where(at_end, at(ref, row, -4), here), 1, 1)

    def up(here):
        return pltpu.roll(here, 7, 0)

    def down(here):
        return pltpu.roll(here, 1, 0)

    def first_pass(c):
        def step(i, carry):
            start = (c * rows + i * GROUP + 1) * 16
            kk, uu, kx = {}, {}, {}

            def center(seen, ref, g, h):
                if (g, h) not in seen:
                    seen[g, h] = at(ref, start + g * 16 + h * 8)
                return seen[g, h]

            for h in (0, 1):
                kx[-1, h] = center(kk, ks, -1, h) + center(kk, ks, 0, h)
            for g in range(GROUP):
                for h in (0, 1):
                    row = start + g * 16 + h * 8
                    k0 = center(kk, ks, g, h)
                    kx[g, h] = k0 + center(kk, ks, g + 1, h)
                    ky, kw = k0 + ahead(ks, row, k0), k0 + behind(ks, row, k0)
                    if h == 0:
                        face_w = jnp.where(y_first, k0, kw)
                        face_y, kw = ky, jnp.where(y_first, 0.0, kw)
                    else:
                        face_y = jnp.where(y_last, k0, ky)
                        face_w, ky = kw, jnp.where(y_last, 0.0, ky)
                    kz, kv = (k0 + up(k0)) * open_up, (k0 + down(k0)) * open_down
                    mid = 24.0 - (((kx[g, h] + kx[g - 1, h]) + (face_y + face_w)) + ((kz + kv) + outer * k0))
                    for ref, value in ((fx, kx[g, h]), (fy, ky), (fw, kw), (fz, kz), (fm, mid)):
                        ref[pl.ds(row, 8), :] = value
                    v = center(uu, us, g, h)
                    out = (kx[g, h] * center(uu, us, g + 1, h) + kx[g - 1, h] * center(uu, us, g - 1, h)) + (kz * up(v) + kv * down(v))
                    out = out + (ky * ahead(us, row, v) + kw * behind(us, row, v)) + mid * v
                    ns[pl.ds(row, 8), :] = out * (-1.0 / 12.0) - at(ns, row)
            return carry

        lax.fori_loop(0, rows // GROUP, step, 0)

    def moments(c):
        def spread(ref, row, plane):
            return jnp.where(first, ref[pl.ds(row + plane, 1), :], ref[pl.ds(row + 4 + plane, 1), :])

        def step(i, carry):
            for g in range(2 * GROUP):
                row = (c * rows + 1) * 16 + (i * 2 * GROUP + g) * 8
                for side, plane in ((0, 0), (1, 3)):
                    es[side, pl.ds(row, 8), :] = of_u * spread(us, row, plane) + of_n * spread(ns, row, plane)
            return carry

        lax.fori_loop(0, rows // GROUP, step, 0)

    def second_pass(c):
        def step(i, carry):
            start = (c * rows + i * GROUP + 1) * 16
            nn, kx = {}, {}

            def center(seen, ref, g, h):
                if (g, h) not in seen:
                    seen[g, h] = at(ref, start + g * 16 + h * 8)
                return seen[g, h]

            for g in range(GROUP):
                for h in (0, 1):
                    row = start + g * 16 + h * 8
                    v = center(nn, ns, g, h)
                    kz = at(fz, row)
                    out = center(kx, fx, g, h) * center(nn, ns, g + 1, h) + center(kx, fx, g - 1, h) * center(nn, ns, g - 1, h)
                    out = out + (kz * up(v) + down(kz) * down(v))
                    out = out + (at(fy, row) * ahead(ns, row, v) + at(fw, row) * behind(ns, row, v)) + at(fm, row) * v
                    final = out * (-1.0 / 12.0) - at(us, row)
                    ds[pl.ds(row - 16, 8), :] = at(ds, row, -16) + c0 * v + c1 * final
                    vs[pl.ds(row - 16, 8), :] = at(vs, row, -16) + c2 * v + c3 * final
            return carry

        lax.fori_loop(0, rows // GROUP, step, 0)

    def place(c, core):
        return lax.rem((1 - 2 * core) * (lax.rem(c, 4) - my_y) + 8, 4), lax.rem(c // 4 + my_z, 2)

    def stores(c, core, same, far):
        turn, _ = place(c, core)
        here = pl.ds((c * rows + core * half_rows) * 16, half_rows * 16)
        to = ((far_other, far_same) if far else (near_other, near_same))[same]
        return [pltpu.make_async_copy(a.at[here], to.at[turn, i], out_sem.at[i, core, c]) for i, a in enumerate((ds, vs))]

    def edge_stores(c, core, same, is_end):
        turn, side = place(c, core)
        here = pl.ds((c * rows + core * half_rows) * 16, (half_rows + 2) * 16)
        to = ((ends_other, ends_same) if is_end else (rest_other, rest_same))[same]
        return [pltpu.make_async_copy(es.at[i, here], to.at[lax.rem(turn, 2), side, i], edge_sem.at[i, core, c]) for i in (0, 1)]

    def send(copies, c, core, test):
        for same in (0, 1):
            for kind in (0, 1):
                @pl.when(((my_core == core) == (same == 1)) & (test(*place(c, core)) == (kind == 1)))
                def _():
                    for copy in copies(c, core, same, kind):
                        copy.start()

    def send_edges(c, core):
        send(edge_stores, c, core, lambda turn, side: turn >= 2)

    def send_series(c, core):
        send(stores, c, core, lambda turn, side: side == 1)

    def chunk(c, carry):
        @pl.when(c < CHIPS)
        def _():
            @pl.when(c == 0)
            def _():
                for copy in loads(c, (0, 1, 2)):
                    copy.wait()

            @pl.when(c + 1 < CHIPS)
            def _():
                for copy in loads(c + 1, (0, 1, 2)):
                    copy.wait()

            first_pass(c)
            moments(c)
            send_edges(c, 0)

        @pl.when(c > 0)
        def _():
            send_edges(c - 1, 1)
            for copy in loads(c - 1, (3, 4)):
                copy.wait()
            second_pass(c - 1)
            for core in (0, 1):
                send_series(c - 1, core)

        return carry

    lax.fori_loop(0, CHIPS + 1, chunk, 0)

    def end(c, carry):
        for core in (0, 1):
            for copy in stores(c, core, 1, 1) + edge_stores(c, core, 1, 1):
                copy.wait()
        return carry

    lax.fori_loop(0, CHIPS, end, 0)


def mend_kernel(d, v, low, high, below, above, k, k_low, k_high, d_out, v_out, ds, vs):
    rows = d.shape[0]
    slab = lax.axis_index("gz")
    lower, upper = jnp.where(slab == 0, 1.0, 0.0), jnp.where(slab == SLABS - 1, 1.0, 0.0)
    wide = rows + 2
    z = places(wide)[1]
    factor = []
    for h in (0, 1):
        under = (1.0 - lower) * (k[:, h] + roll(k_low[:, h], -3))
        over = (1.0 - upper) * (k[:, h] + roll(k_high[:, h], 3))
        factor.append(jnp.where(z == 0, under, jnp.where(z == 3, -over, 0.0)) * (1.0 / 12.0))
    from_low = [low[:, h] - below[:, h] for h in (0, 1)]
    from_high = [above[:, h] - high[:, h] for h in (0, 1)]
    direct = []
    for field, slot in ((ds, 0), (vs, 2)):
        for h in (0, 1):
            a = jnp.where(z == 0, roll(from_low[h], -slot), roll(from_high[h], 3 - slot))
            b = jnp.where(z == 0, roll(from_low[h], -slot - 1), roll(from_high[h], 2 - slot))
            w = factor[h] * a
            field[:, h] = w
            direct.append((factor[h] * b + 2.0 * jnp.abs(factor[h]) * w)[1 : rows + 1])
    for field, given, out, direct_of in ((ds, d, d_out, direct[:2]), (vs, v, v_out, direct[2:])):
        w, outflow = spread(field, k, 0, rows, lower, upper)
        for h in (0, 1):
            out[:, h] = given[:, h] + direct_of[h] - outflow[h] * (1.0 / 12.0) - 2.0 * w[h]


ANYWHERE = pl.BlockSpec(memory_space=pl.ANY)
SMEM = pl.BlockSpec(memory_space=pltpu.SMEM)


def params(mib):
    return pltpu.CompilerParams(vmem_limit_bytes=mib * MIB)


def cost(mib):
    return pl.CostEstimate(flops=0, bytes_accessed=mib * MIB, transcendentals=0)


def flat(cells):
    return cells.reshape(-1, 128)


def series(coeffs, u, k, p, cos, sin):
    cells = u.shape[0] // 16
    share = jax.ShapeDtypeStruct((4, 2, cells // COUNT * 16, 128), F32)
    edge = jax.ShapeDtypeStruct((2, 2, 2, (cells // COUNT + 2) * 16, 128), F32)
    wide = pltpu.VMEM(((cells + 2) * 16, 128), F32)
    exact = pltpu.VMEM((cells * 16, 128), F32)
    return pl.pallas_call(
        series_kernel,
        out_shape=(share,) * 4 + (edge,) * 4,
        in_specs=[SMEM] + [ANYWHERE] * 5,
        out_specs=(ANYWHERE,) * 8,
        scratch_shapes=[wide, wide, wide, exact, exact, wide, wide, wide, wide, wide]
        + [
            pltpu.VMEM((2, (cells + 2) * 16, 128), F32),
            pltpu.SemaphoreType.DMA((5, CHIPS)),
            pltpu.SemaphoreType.DMA((2, 2, CHIPS)),
            pltpu.SemaphoreType.DMA((2, 2, CHIPS)),
        ],
        compiler_params=params(56),
        cost_estimate=cost(45),
    )(coeffs, u, k, p, cos, sin)


def mend(d, v, low, high, below, above, k, k_low, k_high):
    shape = jax.ShapeDtypeStruct(d.shape, F32)
    whole = pl.BlockSpec(memory_space=pltpu.VMEM)
    return pl.pallas_call(
        mend_kernel,
        out_shape=(shape, shape),
        in_specs=[whole] * 9,
        out_specs=(whole, whole),
        scratch_shapes=[pltpu.VMEM(k.shape, F32)] * 2,
        compiler_params=params(16),
        cost_estimate=cost(4),
    )(d, v, low, high, below, above, k, k_low, k_high)


CELL = (2, 8, 128)


def along_y(sign):
    def goal(i):
        z, y, core = i // 8, (i // 2) % 4, i % 2
        return z * 8 + ((y + sign * (1 - 2 * core)) % 4) * 2 + core

    return [(i, goal(i)) for i in range(COUNT)]


FORTH, BACK = along_y(1), along_y(-1)
ACROSS = [(i, i ^ 8) for i in range(COUNT)]
SIBLING = [(i, i ^ 1) for i in range(COUNT)]
UP = [(i, i + 1) for i in range(SLABS - 1)]
DOWN = [(i + 1, i) for i in range(SLABS - 1)]


def to_sibling(other):
    return lax.ppermute(other, "tm", SIBLING)


def forth(cells):
    return lax.ppermute(cells, "tm", FORTH)


def back(cells):
    return lax.ppermute(cells, "tm", BACK)


def across(cells):
    return lax.ppermute(cells, "tm", ACROSS)


def after(first, then):
    return lax.optimization_barrier((first, then))


def local(prev_term, last_term, cos_sum, sin_sum, speed_sq, series_coeffs):
    u, p, k = flat(packed(last_term[0])), flat(packed(prev_term[0])), flat(packed(speed_sq))
    cos, sin = flat(packed(cos_sum[0])), flat(packed(sin_sum[0]))
    rows = last_term.shape[1] // COUNT
    me = lax.axis_index("tm")

    outs = series(series_coeffs, u, k, p, cos, sin)
    far_other, far_same, near_other, near_same, ends_other, ends_same, rest_other, rest_same = outs

    ends_came, far_came = to_sibling(ends_other), to_sibling(far_other)
    rest_came, near_came = to_sibling(rest_other), to_sibling(near_other)
    ends_two = forth(ends_same[0] + ends_came[0])
    far_ends = far_same[2:] + far_came[2:]
    far_ends, ends_came = after(far_ends, ends_came)
    far_ends_came = across(far_ends)
    ends_back = back(ends_same[1] + ends_came[1])

    start = me * rows * 16
    k_here = jnp.concatenate(
        [
            jnp.where(me > 0, lax.dynamic_slice_in_dim(k, jnp.maximum(start - 16, 0), 16), 0.0),
            lax.dynamic_slice_in_dim(k, start, rows * 16),
            jnp.where(me < COUNT - 1, lax.dynamic_slice_in_dim(k, jnp.minimum(start + rows * 16, k.shape[0] - 16), 16), 0.0),
        ]
    )
    k_low, k_high = lax.ppermute(k_here, "gz", UP), lax.ppermute(k_here, "gz", DOWN)

    (ends_two, ends_back), far_came = after((ends_two, ends_back), far_came)
    ring = forth(rest_same[1] + rest_came[1] + ends_two)
    far_next_came = across(far_same[1] + far_came[1])
    two, direct = (near_same[t] + near_came[t] + far_ends_came[t - 2] for t in (2, 3))
    (two, direct, k_low, k_high), ring = after((two, direct, k_low, k_high), ring)
    two, direct = forth(two), back(direct)
    edge_far = rest_same[0, 1] + rest_came[0, 1] + ends_back[1] + ring[1]
    edge_far, (far_came, far_next_came) = after(edge_far, (far_came, far_next_came))
    edge_far = across(edge_far)
    far_own_came = across(far_same[0] + far_came[0])
    last = near_same[1] + near_came[1] + far_next_came + two
    last, edge_far = after(last, edge_far)
    last = forth(last)
    edge = rest_same[0, 0] + rest_came[0, 0] + ends_back[0] + ring[0] + edge_far
    low, high = edge[0], edge[1]
    above, below = lax.ppermute(low, "gz", DOWN), lax.ppermute(high, "gz", UP)
    result = near_same[0] + near_came[0] + far_own_came + direct + last
    d, v = result[0], result[1]

    wide = (a.reshape(rows + 2, *CELL) for a in (low, high, below, above, k_here, k_low, k_high))
    d, v = mend(d.reshape(rows, *CELL), v.reshape(rows, *CELL), *wide)
    return unpacked(d), unpacked(v)


def solution(mesh):
    return jax.shard_map(
        local,
        mesh=mesh,
        in_specs=(
            P("tm", None, "gz", None),
            P("tm", None, "gz", None),
            P("tm", None, "gz", None),
            P("tm", None, "gz", None),
            P(None, "gz", None),
            P("tm", None),
        ),
        out_specs=(P("tm", "gz", None), P("tm", "gz", None)),
        check_vma=False,
    )
```

```python
import jax
import jax.numpy as jnp
from jax import lax
from jax.experimental import pallas as pl
from jax.experimental.pallas import tpu as pltpu
from jax.sharding import PartitionSpec as P

CHIPS = 8
COUNT = 16
SLABS = 8
GROUP = 16
MIB = 1024 * 1024
F32 = jnp.float32


def packed(cells):
    x = cells.shape[0]
    return cells.reshape(x, 4, 4, 128).transpose(0, 2, 1, 3).reshape(x, 2, 8, 128)


def unpacked(cells):
    x = cells.shape[0]
    return cells.reshape(x, 4, 4, 128).transpose(0, 2, 1, 3).reshape(x, 4, 512)


def roll(cells, shift):
    return pltpu.roll(cells, shift % 8, 1)


def places(n):
    sub = lax.broadcasted_iota(jnp.int32, (n, 8, 128), 1)
    return sub, lax.rem(sub, 4), lax.broadcasted_iota(jnp.int32, (n, 8, 128), 2)


def spread(field, speed, row, n, lower, upper):
    sub, z, lane = places(n)
    first, at_start, at_end = sub < 4, lane == 0, lane == 127
    v = [field[pl.ds(row + 1, n), h] for h in (0, 1)]
    k = [speed[pl.ds(row + 1, n), h] for h in (0, 1)]

    def ahead(a, b):
        ra, rb = pltpu.roll(a, 127, 2), pltpu.roll(b, 127, 2)
        qa, qb = roll(ra, 4), roll(rb, 4)
        return (
            jnp.where(at_end, jnp.where(first, qa, qb), ra),
            jnp.where(at_end, jnp.where(first, qb, 0.0), rb),
        )

    def behind(a, b, edge):
        ra, rb = pltpu.roll(a, 1, 2), pltpu.roll(b, 1, 2)
        qa, qb = roll(ra, 4), roll(rb, 4)
        return (
            jnp.where(at_start, jnp.where(first, edge, qa), ra),
            jnp.where(at_start, jnp.where(first, qa, qb), rb),
        )

    v_y, k_y = ahead(*v), ahead(*k)
    f_y = [(k[h] + k_y[h]) * (v_y[h] - v[h]) for h in (0, 1)]
    b_y = behind(*f_y, k[0] * v[0])
    out = []
    for h in (0, 1):
        kv = k[h] * v[h]
        f_z = jnp.where(z == 3, -upper * kv, (k[h] + roll(k[h], -1)) * (roll(v[h], -1) - v[h]))
        b_z = jnp.where(z == 0, lower * kv, roll(f_z, 1))
        f_x = (k[h] + speed[pl.ds(row + 2, n), h]) * (field[pl.ds(row + 2, n), h] - v[h])
        b_x = (k[h] + speed[pl.ds(row, n), h]) * (v[h] - field[pl.ds(row, n), h])
        out.append((f_x - b_x) + (f_y[h] - b_y[h]) + (f_z - b_z))
    return v, out


def widen(scratch, main, before, after, block, blocks):
    rows = main.shape[0]
    scratch[pl.ds(1, rows)] = main[...]
    scratch[pl.ds(0, 1)] = jnp.where(block > 0, before[...], 0.0)
    scratch[pl.ds(rows + 1, 1)] = jnp.where(block < blocks - 1, after[...], 0.0)


def where_am_i():
    me = lax.axis_index("tm")
    return me // 8, lax.rem(me // 2, 4), lax.rem(me, 2)


def series_kernel(coeffs, u, k, p, cos, sin, far_other, far_same, near_other, near_same, ends_other, ends_same, rest_other, rest_same,
                  us, ks, ns, ds, vs, fx, fy, fw, fz, fm, es, in_sem, out_sem, edge_sem):
    cells = u.shape[0] // 16
    rows = cells // CHIPS
    half_rows = rows // 2
    my_z, my_y, my_core = where_am_i()
    slab = lax.axis_index("gz")
    lower, upper = jnp.where(slab == 0, 1.0, 0.0), jnp.where(slab == SLABS - 1, 1.0, 0.0)
    c0, c1, c2, c3 = (coeffs[0, i] for i in range(4))
    sub = lax.broadcasted_iota(jnp.int32, (8, 128), 0)
    lane = lax.broadcasted_iota(jnp.int32, (8, 128), 1)
    z = lax.rem(sub, 4)
    first, at_start, at_end = sub < 4, lane == 0, lane == 127
    open_up, open_down = jnp.where(z == 3, 0.0, 1.0), jnp.where(z == 0, 0.0, 1.0)
    of_u = jnp.where(z == 0, c1, jnp.where(z == 1, c0, jnp.where(z == 2, c3, c2)))
    of_n = jnp.where(z == 1, c1, jnp.where(z == 3, c3, 0.0))
    y_first, y_last = jnp.logical_and(first, at_start), jnp.logical_and(jnp.logical_not(first), at_end)
    outer = jnp.where(z == 0, lower, 0.0) + jnp.where(z == 3, upper, 0.0)

    def arrays():
        return ((u, us, 16), (k, ks, 16), (p, ns, 16), (cos, ds, 0), (sin, vs, 0))

    def loads(c, which):
        return [
            pltpu.make_async_copy(a.at[pl.ds(c * rows * 16, rows * 16)], b.at[pl.ds(c * rows * 16 + off, rows * 16)], in_sem.at[i, c])
            for i, (a, b, off) in enumerate(arrays()) if i in which
        ]

    for c in range(CHIPS):
        for copy in loads(c, (0, 1, 2)):
            copy.start()
        if c:
            for copy in loads(c - 1, (3, 4)):
                copy.start()
    for copy in loads(CHIPS - 1, (3, 4)):
        copy.start()
    nothing = jnp.zeros((16, 128), F32)
    fx[0:16] = nothing
    fz[0:16] = nothing
    for side in (0, 1):
        es[side, 0:16] = nothing
        es[side, (cells + 1) * 16 : (cells + 2) * 16] = nothing
    for ref in (us, ks, ns):
        ref[0:16] = nothing
        ref[(cells + 1) * 16 : (cells + 2) * 16] = nothing

    def at(ref, row, by=0):
        return ref[pl.ds(row + by, 8), :]

    def ahead(ref, row, here):
        return pltpu.roll(jnp.where(at_start, at(ref, row, 4), here), 127, 1)

    def behind(ref, row, here):
        return pltpu.roll(jnp.where(at_end, at(ref, row, -4), here), 1, 1)

    def up(here):
        return pltpu.roll(here, 7, 0)

    def down(here):
        return pltpu.roll(here, 1, 0)

    def first_pass(c):
        def step(i, carry):
            start = (c * rows + i * GROUP + 1) * 16
            kk, uu, kx = {}, {}, {}

            def center(seen, ref, g, h):
                if (g, h) not in seen:
                    seen[g, h] = at(ref, start + g * 16 + h * 8)
                return seen[g, h]

            for h in (0, 1):
                kx[-1, h] = center(kk, ks, -1, h) + center(kk, ks, 0, h)
            for g in range(GROUP):
                for h in (0, 1):
                    row = start + g * 16 + h * 8
                    k0 = center(kk, ks, g, h)
                    kx[g, h] = k0 + center(kk, ks, g + 1, h)
                    ky, kw = k0 + ahead(ks, row, k0), k0 + behind(ks, row, k0)
                    if h == 0:
                        face_w = jnp.where(y_first, k0, kw)
                        face_y, kw = ky, jnp.where(y_first, 0.0, kw)
                    else:
                        face_y = jnp.where(y_last, k0, ky)
                        face_w, ky = kw, jnp.where(y_last, 0.0, ky)
                    kz, kv = (k0 + up(k0)) * open_up, (k0 + down(k0)) * open_down
                    mid = 24.0 - (((kx[g, h] + kx[g - 1, h]) + (face_y + face_w)) + ((kz + kv) + outer * k0))
                    for ref, value in ((fx, kx[g, h]), (fy, ky), (fw, kw), (fz, kz), (fm, mid)):
                        ref[pl.ds(row, 8), :] = value
                    v = center(uu, us, g, h)
                    out = (kx[g, h] * center(uu, us, g + 1, h) + kx[g - 1, h] * center(uu, us, g - 1, h)) + (kz * up(v) + kv * down(v))
                    out = out + (ky * ahead(us, row, v) + kw * behind(us, row, v)) + mid * v
                    ns[pl.ds(row, 8), :] = out * (-1.0 / 12.0) - at(ns, row)
            return carry

        lax.fori_loop(0, rows // GROUP, step, 0)

    def moments(c):
        def spread(ref, row, plane):
            return jnp.where(first, ref[pl.ds(row + plane, 1), :], ref[pl.ds(row + 4 + plane, 1), :])

        def step(i, carry):
            for g in range(2 * GROUP):
                row = (c * rows + 1) * 16 + (i * 2 * GROUP + g) * 8
                for side, plane in ((0, 0), (1, 3)):
                    es[side, pl.ds(row, 8), :] = of_u * spread(us, row, plane) + of_n * spread(ns, row, plane)
            return carry

        lax.fori_loop(0, rows // GROUP, step, 0)

    def second_pass(c):
        def step(i, carry):
            start = (c * rows + i * GROUP + 1) * 16
            nn, kx = {}, {}

            def center(seen, ref, g, h):
                if (g, h) not in seen:
                    seen[g, h] = at(ref, start + g * 16 + h * 8)
                return seen[g, h]

            for g in range(GROUP):
                for h in (0, 1):
                    row = start + g * 16 + h * 8
                    v = center(nn, ns, g, h)
                    kz = at(fz, row)
                    out = center(kx, fx, g, h) * center(nn, ns, g + 1, h) + center(kx, fx, g - 1, h) * center(nn, ns, g - 1, h)
                    out = out + (kz * up(v) + down(kz) * down(v))
                    out = out + (at(fy, row) * ahead(ns, row, v) + at(fw, row) * behind(ns, row, v)) + at(fm, row) * v
                    final = out * (-1.0 / 12.0) - at(us, row)
                    ds[pl.ds(row - 16, 8), :] = at(ds, row, -16) + c0 * v + c1 * final
                    vs[pl.ds(row - 16, 8), :] = at(vs, row, -16) + c2 * v + c3 * final
            return carry

        lax.fori_loop(0, rows // GROUP, step, 0)

    def place(c, core):
        return lax.rem((1 - 2 * core) * (lax.rem(c, 4) - my_y) + 8, 4), lax.rem(c // 4 + my_z, 2)

    def stores(c, core, same, far):
        turn, _ = place(c, core)
        here = pl.ds((c * rows + core * half_rows) * 16, half_rows * 16)
        to = ((far_other, far_same) if far else (near_other, near_same))[same]
        return [pltpu.make_async_copy(a.at[here], to.at[turn, i], out_sem.at[i, core, c]) for i, a in enumerate((ds, vs))]

    def edge_stores(c, core, same, is_end):
        turn, side = place(c, core)
        here = pl.ds((c * rows + core * half_rows) * 16, (half_rows + 2) * 16)
        to = ((ends_other, ends_same) if is_end else (rest_other, rest_same))[same]
        return [pltpu.make_async_copy(es.at[i, here], to.at[lax.rem(turn, 2), side, i], edge_sem.at[i, core, c]) for i in (0, 1)]

    def send(copies, c, core, test):
        for same in (0, 1):
            for kind in (0, 1):
                @pl.when(((my_core == core) == (same == 1)) & (test(*place(c, core)) == (kind == 1)))
                def _():
                    for copy in copies(c, core, same, kind):
                        copy.start()

    def send_edges(c, core):
        send(edge_stores, c, core, lambda turn, side: turn >= 2)

    def send_series(c, core):
        send(stores, c, core, lambda turn, side: side == 1)

    def chunk(c, carry):
        @pl.when(c < CHIPS)
        def _():
            @pl.when(c == 0)
            def _():
                for copy in loads(c, (0, 1, 2)):
                    copy.wait()

            @pl.when(c + 1 < CHIPS)
            def _():
                for copy in loads(c + 1, (0, 1, 2)):
                    copy.wait()

            first_pass(c)
            moments(c)
            send_edges(c, 0)

        @pl.when(c > 0)
        def _():
            send_edges(c - 1, 1)
            for copy in loads(c - 1, (3, 4)):
                copy.wait()
            second_pass(c - 1)
            for core in (0, 1):
                send_series(c - 1, core)

        return carry

    lax.fori_loop(0, CHIPS + 1, chunk, 0)

    def end(c, carry):
        for core in (0, 1):
            for copy in stores(c, core, 1, 1) + edge_stores(c, core, 1, 1):
                copy.wait()
        return carry

    lax.fori_loop(0, CHIPS, end, 0)


def mend_kernel(d, v, low, high, below, above, k, k_low, k_high, d_out, v_out, ds, vs):
    rows = d.shape[0]
    slab = lax.axis_index("gz")
    lower, upper = jnp.where(slab == 0, 1.0, 0.0), jnp.where(slab == SLABS - 1, 1.0, 0.0)
    wide = rows + 2
    z = places(wide)[1]
    factor = []
    for h in (0, 1):
        under = (1.0 - lower) * (k[:, h] + roll(k_low[:, h], -3))
        over = (1.0 - upper) * (k[:, h] + roll(k_high[:, h], 3))
        factor.append(jnp.where(z == 0, under, jnp.where(z == 3, -over, 0.0)) * (1.0 / 12.0))
    from_low = [low[:, h] - below[:, h] for h in (0, 1)]
    from_high = [above[:, h] - high[:, h] for h in (0, 1)]
    direct = []
    for field, slot in ((ds, 0), (vs, 2)):
        for h in (0, 1):
            a = jnp.where(z == 0, roll(from_low[h], -slot), roll(from_high[h], 3 - slot))
            b = jnp.where(z == 0, roll(from_low[h], -slot - 1), roll(from_high[h], 2 - slot))
            w = factor[h] * a
            field[:, h] = w
            direct.append((factor[h] * b + 2.0 * jnp.abs(factor[h]) * w)[1 : rows + 1])
    for field, given, out, direct_of in ((ds, d, d_out, direct[:2]), (vs, v, v_out, direct[2:])):
        w, outflow = spread(field, k, 0, rows, lower, upper)
        for h in (0, 1):
            out[:, h] = given[:, h] + direct_of[h] - outflow[h] * (1.0 / 12.0) - 2.0 * w[h]


ANYWHERE = pl.BlockSpec(memory_space=pl.ANY)
SMEM = pl.BlockSpec(memory_space=pltpu.SMEM)


def params(mib):
    return pltpu.CompilerParams(vmem_limit_bytes=mib * MIB)


def cost(mib):
    return pl.CostEstimate(flops=0, bytes_accessed=mib * MIB, transcendentals=0)


def flat(cells):
    return cells.reshape(-1, 128)


def series(coeffs, u, k, p, cos, sin):
    cells = u.shape[0] // 16
    share = jax.ShapeDtypeStruct((4, 2, cells // COUNT * 16, 128), F32)
    edge = jax.ShapeDtypeStruct((2, 2, 2, (cells // COUNT + 2) * 16, 128), F32)
    wide = pltpu.VMEM(((cells + 2) * 16, 128), F32)
    exact = pltpu.VMEM((cells * 16, 128), F32)
    return pl.pallas_call(
        series_kernel,
        out_shape=(share,) * 4 + (edge,) * 4,
        in_specs=[SMEM] + [ANYWHERE] * 5,
        out_specs=(ANYWHERE,) * 8,
        scratch_shapes=[wide, wide, wide, exact, exact, wide, wide, wide, wide, wide]
        + [
            pltpu.VMEM((2, (cells + 2) * 16, 128), F32),
            pltpu.SemaphoreType.DMA((5, CHIPS)),
            pltpu.SemaphoreType.DMA((2, 2, CHIPS)),
            pltpu.SemaphoreType.DMA((2, 2, CHIPS)),
        ],
        compiler_params=params(56),
        cost_estimate=cost(45),
    )(coeffs, u, k, p, cos, sin)


def mend(d, v, low, high, below, above, k, k_low, k_high):
    shape = jax.ShapeDtypeStruct(d.shape, F32)
    whole = pl.BlockSpec(memory_space=pltpu.VMEM)
    return pl.pallas_call(
        mend_kernel,
        out_shape=(shape, shape),
        in_specs=[whole] * 9,
        out_specs=(whole, whole),
        scratch_shapes=[pltpu.VMEM(k.shape, F32)] * 2,
        compiler_params=params(16),
        cost_estimate=cost(4),
    )(d, v, low, high, below, above, k, k_low, k_high)


CELL = (2, 8, 128)


def along_y(sign):
    def goal(i):
        z, y, core = i // 8, (i // 2) % 4, i % 2
        return z * 8 + ((y + sign * (1 - 2 * core)) % 4) * 2 + core

    return [(i, goal(i)) for i in range(COUNT)]


FORTH, BACK = along_y(1), along_y(-1)
ACROSS = [(i, i ^ 8) for i in range(COUNT)]
SIBLING = [(i, i ^ 1) for i in range(COUNT)]
UP = [(i, i + 1) for i in range(SLABS - 1)]
DOWN = [(i + 1, i) for i in range(SLABS - 1)]


def to_sibling(other):
    return lax.ppermute(other, "tm", SIBLING)


def forth(cells):
    return lax.ppermute(cells, "tm", FORTH)


def back(cells):
    return lax.ppermute(cells, "tm", BACK)


def across(cells):
    return lax.ppermute(cells, "tm", ACROSS)


def after(first, then):
    return lax.optimization_barrier((first, then))


def local(prev_term, last_term, cos_sum, sin_sum, speed_sq, series_coeffs):
    u, p, k = flat(packed(last_term[0])), flat(packed(prev_term[0])), flat(packed(speed_sq))
    cos, sin = flat(packed(cos_sum[0])), flat(packed(sin_sum[0]))
    rows = last_term.shape[1] // COUNT
    me = lax.axis_index("tm")

    outs = series(series_coeffs, u, k, p, cos, sin)
    far_other, far_same, near_other, near_same, ends_other, ends_same, rest_other, rest_same = outs

    ends_came, far_came = to_sibling(ends_other), to_sibling(far_other)
    rest_came, near_came = to_sibling(rest_other), to_sibling(near_other)
    ends_two = forth(ends_same[0] + ends_came[0])
    far_ends = far_same[2:] + far_came[2:]
    far_ends, ends_came = after(far_ends, ends_came)
    far_ends_came = across(far_ends)
    ends_back = back(ends_same[1] + ends_came[1])

    start = me * rows * 16
    k_here = jnp.concatenate(
        [
            jnp.where(me > 0, lax.dynamic_slice_in_dim(k, jnp.maximum(start - 16, 0), 16), 0.0),
            lax.dynamic_slice_in_dim(k, start, rows * 16),
            jnp.where(me < COUNT - 1, lax.dynamic_slice_in_dim(k, jnp.minimum(start + rows * 16, k.shape[0] - 16), 16), 0.0),
        ]
    )
    k_low, k_high = lax.ppermute(k_here, "gz", UP), lax.ppermute(k_here, "gz", DOWN)

    ends_two, far_came = after(ends_two, far_came)
    ring = forth(rest_same[1] + rest_came[1] + ends_two)
    far_next_came = across(far_same[1] + far_came[1])
    two, direct = (near_same[t] + near_came[t] + far_ends_came[t - 2] for t in (2, 3))
    (two, direct, k_low, k_high), ring = after((two, direct, k_low, k_high), ring)
    two, direct = forth(two), back(direct)
    edge_far = rest_same[0, 1] + rest_came[0, 1] + ends_back[1] + ring[1]
    edge_far, (far_came, far_next_came) = after(edge_far, (far_came, far_next_came))
    edge_far = across(edge_far)
    far_own_came = across(far_same[0] + far_came[0])
    last = near_same[1] + near_came[1] + far_next_came + two
    last, edge_far = after(last, edge_far)
    last = forth(last)
    edge = rest_same[0, 0] + rest_came[0, 0] + ends_back[0] + ring[0] + edge_far
    low, high = edge[0], edge[1]
    above, below = lax.ppermute(low, "gz", DOWN), lax.ppermute(high, "gz", UP)
    result = near_same[0] + near_came[0] + far_own_came + direct + last
    d, v = result[0], result[1]

    wide = (a.reshape(rows + 2, *CELL) for a in (low, high, below, above, k_here, k_low, k_high))
    d, v = mend(d.reshape(rows, *CELL), v.reshape(rows, *CELL), *wide)
    return unpacked(d), unpacked(v)


def solution(mesh):
    return jax.shard_map(
        local,
        mesh=mesh,
        in_specs=(
            P("tm", None, "gz", None),
            P("tm", None, "gz", None),
            P("tm", None, "gz", None),
            P("tm", None, "gz", None),
            P(None, "gz", None),
            P("tm", None),
        ),
        out_specs=(P("tm", "gz", None), P("tm", "gz", None)),
        check_vma=False,
    )
```

```python
import jax
import jax.numpy as jnp
from jax import lax
from jax.experimental import pallas as pl
from jax.experimental.pallas import tpu as pltpu
from jax.sharding import PartitionSpec as P

CHIPS = 8
COUNT = 16
SLABS = 8
GROUP = 16
MIB = 1024 * 1024
F32 = jnp.float32


def packed(cells):
    x = cells.shape[0]
    return cells.reshape(x, 4, 4, 128).transpose(0, 2, 1, 3).reshape(x, 2, 8, 128)


def unpacked(cells):
    x = cells.shape[0]
    return cells.reshape(x, 4, 4, 128).transpose(0, 2, 1, 3).reshape(x, 4, 512)


def roll(cells, shift):
    return pltpu.roll(cells, shift % 8, 1)


def places(n):
    sub = lax.broadcasted_iota(jnp.int32, (n, 8, 128), 1)
    return sub, lax.rem(sub, 4), lax.broadcasted_iota(jnp.int32, (n, 8, 128), 2)


def spread(field, speed, row, n, lower, upper):
    sub, z, lane = places(n)
    first, at_start, at_end = sub < 4, lane == 0, lane == 127
    v = [field[pl.ds(row + 1, n), h] for h in (0, 1)]
    k = [speed[pl.ds(row + 1, n), h] for h in (0, 1)]

    def ahead(a, b):
        ra, rb = pltpu.roll(a, 127, 2), pltpu.roll(b, 127, 2)
        qa, qb = roll(ra, 4), roll(rb, 4)
        return (
            jnp.where(at_end, jnp.where(first, qa, qb), ra),
            jnp.where(at_end, jnp.where(first, qb, 0.0), rb),
        )

    def behind(a, b, edge):
        ra, rb = pltpu.roll(a, 1, 2), pltpu.roll(b, 1, 2)
        qa, qb = roll(ra, 4), roll(rb, 4)
        return (
            jnp.where(at_start, jnp.where(first, edge, qa), ra),
            jnp.where(at_start, jnp.where(first, qa, qb), rb),
        )

    v_y, k_y = ahead(*v), ahead(*k)
    f_y = [(k[h] + k_y[h]) * (v_y[h] - v[h]) for h in (0, 1)]
    b_y = behind(*f_y, k[0] * v[0])
    out = []
    for h in (0, 1):
        kv = k[h] * v[h]
        f_z = jnp.where(z == 3, -upper * kv, (k[h] + roll(k[h], -1)) * (roll(v[h], -1) - v[h]))
        b_z = jnp.where(z == 0, lower * kv, roll(f_z, 1))
        f_x = (k[h] + speed[pl.ds(row + 2, n), h]) * (field[pl.ds(row + 2, n), h] - v[h])
        b_x = (k[h] + speed[pl.ds(row, n), h]) * (v[h] - field[pl.ds(row, n), h])
        out.append((f_x - b_x) + (f_y[h] - b_y[h]) + (f_z - b_z))
    return v, out


def widen(scratch, main, before, after, block, blocks):
    rows = main.shape[0]
    scratch[pl.ds(1, rows)] = main[...]
    scratch[pl.ds(0, 1)] = jnp.where(block > 0, before[...], 0.0)
    scratch[pl.ds(rows + 1, 1)] = jnp.where(block < blocks - 1, after[...], 0.0)


def where_am_i():
    me = lax.axis_index("tm")
    return me // 8, lax.rem(me // 2, 4), lax.rem(me, 2)


def series_kernel(coeffs, u, k, p, cos, sin, *refs):
    near, far_rest, far_ends, rest, two, three = (refs[2 * i : 2 * i + 2] for i in range(6))
    us, ks, ns, ds, vs, fx, fy, fw, fz, fm, es, in_sem, out_sem, edge_sem = refs[12:]
    cells = u.shape[0] // 16
    rows = cells // CHIPS
    half_rows = rows // 2
    my_z, my_y, my_core = where_am_i()
    slab = lax.axis_index("gz")
    lower, upper = jnp.where(slab == 0, 1.0, 0.0), jnp.where(slab == SLABS - 1, 1.0, 0.0)
    c0, c1, c2, c3 = (coeffs[0, i] for i in range(4))
    sub = lax.broadcasted_iota(jnp.int32, (8, 128), 0)
    lane = lax.broadcasted_iota(jnp.int32, (8, 128), 1)
    z = lax.rem(sub, 4)
    first, at_start, at_end = sub < 4, lane == 0, lane == 127
    open_up, open_down = jnp.where(z == 3, 0.0, 1.0), jnp.where(z == 0, 0.0, 1.0)
    of_u = jnp.where(z == 0, c1, jnp.where(z == 1, c0, jnp.where(z == 2, c3, c2)))
    of_n = jnp.where(z == 1, c1, jnp.where(z == 3, c3, 0.0))
    y_first, y_last = jnp.logical_and(first, at_start), jnp.logical_and(jnp.logical_not(first), at_end)
    outer = jnp.where(z == 0, lower, 0.0) + jnp.where(z == 3, upper, 0.0)

    def arrays():
        return ((u, us, 16), (k, ks, 16), (p, ns, 16), (cos, ds, 0), (sin, vs, 0))

    def loads(c, which):
        return [
            pltpu.make_async_copy(a.at[pl.ds(c * rows * 16, rows * 16)], b.at[pl.ds(c * rows * 16 + off, rows * 16)], in_sem.at[i, c])
            for i, (a, b, off) in enumerate(arrays()) if i in which
        ]

    for c in range(CHIPS):
        for copy in loads(c, (0, 1, 2)):
            copy.start()
        if c:
            for copy in loads(c - 1, (3, 4)):
                copy.start()
    for copy in loads(CHIPS - 1, (3, 4)):
        copy.start()
    nothing = jnp.zeros((16, 128), F32)
    fx[0:16] = nothing
    fz[0:16] = nothing
    for side in (0, 1):
        es[side, 0:16] = nothing
        es[side, (cells + 1) * 16 : (cells + 2) * 16] = nothing
    for ref in (us, ks, ns):
        ref[0:16] = nothing
        ref[(cells + 1) * 16 : (cells + 2) * 16] = nothing

    def at(ref, row, by=0):
        return ref[pl.ds(row + by, 8), :]

    def ahead(ref, row, here):
        return pltpu.roll(jnp.where(at_start, at(ref, row, 4), here), 127, 1)

    def behind(ref, row, here):
        return pltpu.roll(jnp.where(at_end, at(ref, row, -4), here), 1, 1)

    def up(here):
        return pltpu.roll(here, 7, 0)

    def down(here):
        return pltpu.roll(here, 1, 0)

    def first_pass(c):
        def step(i, carry):
            start = (c * rows + i * GROUP + 1) * 16
            kk, uu, kx = {}, {}, {}

            def center(seen, ref, g, h):
                if (g, h) not in seen:
                    seen[g, h] = at(ref, start + g * 16 + h * 8)
                return seen[g, h]

            for h in (0, 1):
                kx[-1, h] = center(kk, ks, -1, h) + center(kk, ks, 0, h)
            for g in range(GROUP):
                for h in (0, 1):
                    row = start + g * 16 + h * 8
                    k0 = center(kk, ks, g, h)
                    kx[g, h] = k0 + center(kk, ks, g + 1, h)
                    ky, kw = k0 + ahead(ks, row, k0), k0 + behind(ks, row, k0)
                    if h == 0:
                        face_w = jnp.where(y_first, k0, kw)
                        face_y, kw = ky, jnp.where(y_first, 0.0, kw)
                    else:
                        face_y = jnp.where(y_last, k0, ky)
                        face_w, ky = kw, jnp.where(y_last, 0.0, ky)
                    kz, kv = (k0 + up(k0)) * open_up, (k0 + down(k0)) * open_down
                    mid = 24.0 - (((kx[g, h] + kx[g - 1, h]) + (face_y + face_w)) + ((kz + kv) + outer * k0))
                    for ref, value in ((fx, kx[g, h]), (fy, ky), (fw, kw), (fz, kz), (fm, mid)):
                        ref[pl.ds(row, 8), :] = value
                    v = center(uu, us, g, h)
                    out = (kx[g, h] * center(uu, us, g + 1, h) + kx[g - 1, h] * center(uu, us, g - 1, h)) + (kz * up(v) + kv * down(v))
                    out = out + (ky * ahead(us, row, v) + kw * behind(us, row, v)) + mid * v
                    ns[pl.ds(row, 8), :] = out * (-1.0 / 12.0) - at(ns, row)
            return carry

        lax.fori_loop(0, rows // GROUP, step, 0)

    def moments(c):
        def spread(ref, row, plane):
            return jnp.where(first, ref[pl.ds(row + plane, 1), :], ref[pl.ds(row + 4 + plane, 1), :])

        def step(i, carry):
            for g in range(2 * GROUP):
                row = (c * rows + 1) * 16 + (i * 2 * GROUP + g) * 8
                for side, plane in ((0, 0), (1, 3)):
                    es[side, pl.ds(row, 8), :] = of_u * spread(us, row, plane) + of_n * spread(ns, row, plane)
            return carry

        lax.fori_loop(0, rows // GROUP, step, 0)

    def second_pass(c):
        def step(i, carry):
            start = (c * rows + i * GROUP + 1) * 16
            nn, kx = {}, {}

            def center(seen, ref, g, h):
                if (g, h) not in seen:
                    seen[g, h] = at(ref, start + g * 16 + h * 8)
                return seen[g, h]

            for g in range(GROUP):
                for h in (0, 1):
                    row = start + g * 16 + h * 8
                    v = center(nn, ns, g, h)
                    kz = at(fz, row)
                    out = center(kx, fx, g, h) * center(nn, ns, g + 1, h) + center(kx, fx, g - 1, h) * center(nn, ns, g - 1, h)
                    out = out + (kz * up(v) + down(kz) * down(v))
                    out = out + (at(fy, row) * ahead(ns, row, v) + at(fw, row) * behind(ns, row, v)) + at(fm, row) * v
                    final = out * (-1.0 / 12.0) - at(us, row)
                    ds[pl.ds(row - 16, 8), :] = at(ds, row, -16) + c0 * v + c1 * final
                    vs[pl.ds(row - 16, 8), :] = at(vs, row, -16) + c2 * v + c3 * final
            return carry

        lax.fori_loop(0, rows // GROUP, step, 0)

    def place(c, core):
        return lax.rem((1 - 2 * core) * (lax.rem(c, 4) - my_y) + 8, 4), lax.rem(c // 4 + my_z, 2)

    def stores(c, core, same, kind):
        turn, _ = place(c, core)
        here = pl.ds((c * rows + core * half_rows) * 16, half_rows * 16)
        to = (near, far_rest, far_ends)[kind][same].at[turn - 2 if kind == 2 else turn]
        return [pltpu.make_async_copy(a.at[here], to.at[i], out_sem.at[i, core, c]) for i, a in enumerate((ds, vs))]

    def edge_stores(c, core, same, kind):
        turn, side = place(c, core)
        here = pl.ds((c * rows + core * half_rows) * 16, (half_rows + 2) * 16)
        to = (rest[same].at[turn, side], two[same].at[side], three[same].at[side])[kind]
        return [pltpu.make_async_copy(es.at[i, here], to.at[i], edge_sem.at[i, core, c]) for i in (0, 1)]

    def send(copies, c, core, kind_of):
        for same in (0, 1):
            for kind in (0, 1, 2):
                @pl.when(((my_core == core) == (same == 1)) & (kind_of(*place(c, core)) == kind))
                def _():
                    for copy in copies(c, core, same, kind):
                        copy.start()

    def send_edges(c, core):
        send(edge_stores, c, core, lambda turn, side: jnp.maximum(turn - 1, 0))

    def send_series(c, core):
        send(stores, c, core, lambda turn, side: side * (1 + turn // 2))

    def chunk(c, carry):
        @pl.when(c < CHIPS)
        def _():
            @pl.when(c == 0)
            def _():
                for copy in loads(c, (0, 1, 2)):
                    copy.wait()

            @pl.when(c + 1 < CHIPS)
            def _():
                for copy in loads(c + 1, (0, 1, 2)):
                    copy.wait()

            first_pass(c)
            moments(c)
            send_edges(c, 0)

        @pl.when(c > 0)
        def _():
            send_edges(c - 1, 1)
            for copy in loads(c - 1, (3, 4)):
                copy.wait()
            second_pass(c - 1)
            for core in (0, 1):
                send_series(c - 1, core)

        return carry

    lax.fori_loop(0, CHIPS + 1, chunk, 0)

    def end(c, carry):
        for core in (0, 1):
            for copy in stores(c, core, 1, 0) + edge_stores(c, core, 1, 1):
                copy.wait()
        return carry

    lax.fori_loop(0, CHIPS, end, 0)


def mend_kernel(d, v, low, high, below, above, k, k_low, k_high, d_out, v_out, ds, vs):
    rows = d.shape[0]
    slab = lax.axis_index("gz")
    lower, upper = jnp.where(slab == 0, 1.0, 0.0), jnp.where(slab == SLABS - 1, 1.0, 0.0)
    wide = rows + 2
    z = places(wide)[1]
    factor = []
    for h in (0, 1):
        under = (1.0 - lower) * (k[:, h] + roll(k_low[:, h], -3))
        over = (1.0 - upper) * (k[:, h] + roll(k_high[:, h], 3))
        factor.append(jnp.where(z == 0, under, jnp.where(z == 3, -over, 0.0)) * (1.0 / 12.0))
    from_low = [low[:, h] - below[:, h] for h in (0, 1)]
    from_high = [above[:, h] - high[:, h] for h in (0, 1)]
    direct = []
    for field, slot in ((ds, 0), (vs, 2)):
        for h in (0, 1):
            a = jnp.where(z == 0, roll(from_low[h], -slot), roll(from_high[h], 3 - slot))
            b = jnp.where(z == 0, roll(from_low[h], -slot - 1), roll(from_high[h], 2 - slot))
            w = factor[h] * a
            field[:, h] = w
            direct.append((factor[h] * b + 2.0 * jnp.abs(factor[h]) * w)[1 : rows + 1])
    for field, given, out, direct_of in ((ds, d, d_out, direct[:2]), (vs, v, v_out, direct[2:])):
        w, outflow = spread(field, k, 0, rows, lower, upper)
        for h in (0, 1):
            out[:, h] = given[:, h] + direct_of[h] - outflow[h] * (1.0 / 12.0) - 2.0 * w[h]


ANYWHERE = pl.BlockSpec(memory_space=pl.ANY)
SMEM = pl.BlockSpec(memory_space=pltpu.SMEM)


def params(mib):
    return pltpu.CompilerParams(vmem_limit_bytes=mib * MIB)


def cost(mib):
    return pl.CostEstimate(flops=0, bytes_accessed=mib * MIB, transcendentals=0)


def flat(cells):
    return cells.reshape(-1, 128)


def series(coeffs, u, k, p, cos, sin):
    cells = u.shape[0] // 16
    share, edge = (2, cells // COUNT * 16, 128), (2, (cells // COUNT + 2) * 16, 128)
    shapes = ((4, *share), (2, *share), (2, *share), (2, 2, *edge), (2, *edge), (2, *edge))
    wide = pltpu.VMEM(((cells + 2) * 16, 128), F32)
    exact = pltpu.VMEM((cells * 16, 128), F32)
    return pl.pallas_call(
        series_kernel,
        out_shape=[jax.ShapeDtypeStruct(shape, F32) for shape in shapes for _ in range(2)],
        in_specs=[SMEM] + [ANYWHERE] * 5,
        out_specs=[ANYWHERE] * 12,
        scratch_shapes=[wide, wide, wide, exact, exact, wide, wide, wide, wide, wide]
        + [
            pltpu.VMEM((2, (cells + 2) * 16, 128), F32),
            pltpu.SemaphoreType.DMA((5, CHIPS)),
            pltpu.SemaphoreType.DMA((2, 2, CHIPS)),
            pltpu.SemaphoreType.DMA((2, 2, CHIPS)),
        ],
        compiler_params=params(56),
        cost_estimate=cost(45),
    )(coeffs, u, k, p, cos, sin)


def mend(d, v, low, high, below, above, k, k_low, k_high):
    shape = jax.ShapeDtypeStruct(d.shape, F32)
    whole = pl.BlockSpec(memory_space=pltpu.VMEM)
    return pl.pallas_call(
        mend_kernel,
        out_shape=(shape, shape),
        in_specs=[whole] * 9,
        out_specs=(whole, whole),
        scratch_shapes=[pltpu.VMEM(k.shape, F32)] * 2,
        compiler_params=params(16),
        cost_estimate=cost(4),
    )(d, v, low, high, below, above, k, k_low, k_high)


CELL = (2, 8, 128)


def along_y(sign):
    def goal(i):
        z, y, core = i // 8, (i // 2) % 4, i % 2
        return z * 8 + ((y + sign * (1 - 2 * core)) % 4) * 2 + core

    return [(i, goal(i)) for i in range(COUNT)]


FORTH, BACK = along_y(1), along_y(-1)
ACROSS = [(i, i ^ 8) for i in range(COUNT)]
SIBLING = [(i, i ^ 1) for i in range(COUNT)]
UP = [(i, i + 1) for i in range(SLABS - 1)]
DOWN = [(i + 1, i) for i in range(SLABS - 1)]


def to_sibling(other):
    return lax.ppermute(other, "tm", SIBLING)


def forth(cells):
    return lax.ppermute(cells, "tm", FORTH)


def back(cells):
    return lax.ppermute(cells, "tm", BACK)


def across(cells):
    return lax.ppermute(cells, "tm", ACROSS)


def after(first, then):
    return lax.optimization_barrier((first, then))


def local(prev_term, last_term, cos_sum, sin_sum, speed_sq, series_coeffs):
    u, p, k = flat(packed(last_term[0])), flat(packed(prev_term[0])), flat(packed(speed_sq))
    cos, sin = flat(packed(cos_sum[0])), flat(packed(sin_sum[0]))
    rows = last_term.shape[1] // COUNT
    me = lax.axis_index("tm")

    outs = series(series_coeffs, u, k, p, cos, sin)
    near, far_rest, far_ends, rest, two, three = (outs[2 * i : 2 * i + 2] for i in range(6))

    two_came, far_came, three_came = to_sibling(two[0]), to_sibling(far_ends[0]), to_sibling(three[0])
    two_came, others = after(two_came, (rest[0], near[0], far_rest[0]))
    rest_came, near_came, far_rest_came = (to_sibling(other) for other in others)
    two, far_came = after(two[1] + two_came, far_came)
    two = forth(two)
    far_ends = across(far_ends[1] + far_came)
    three = back(three[1] + three_came)

    start = me * rows * 16
    k_here = jnp.concatenate(
        [
            jnp.where(me > 0, lax.dynamic_slice_in_dim(k, jnp.maximum(start - 16, 0), 16), 0.0),
            lax.dynamic_slice_in_dim(k, start, rows * 16),
            jnp.where(me < COUNT - 1, lax.dynamic_slice_in_dim(k, jnp.minimum(start + rows * 16, k.shape[0] - 16), 16), 0.0),
        ]
    )
    k_low, k_high = lax.ppermute(k_here, "gz", UP), lax.ppermute(k_here, "gz", DOWN)

    ring = forth(rest[1][1] + rest_came[1] + two)
    two, far_rest_came = after(two, far_rest_came)
    far_next = across(far_rest[1][1] + far_rest_came[1])
    relay, direct = (near[1][t] + near_came[t] + far_ends[t - 2] for t in (2, 3))
    far_own = far_rest[1][0] + far_rest_came[0]
    (relay, direct, far_own, k_low, k_high), ring = after((relay, direct, far_own, k_low, k_high), ring)
    relay, direct, far_own = forth(relay), back(direct), across(far_own)
    edge_far = rest[1][0, 1] + rest_came[0, 1] + three[1] + ring[1]
    edge_far, far_next = after(edge_far, far_next)
    edge_far = across(edge_far)
    last = near[1][1] + near_came[1] + far_next + relay
    last, edge_far = after(last, edge_far)
    last = forth(last)
    edge = rest[1][0, 0] + rest_came[0, 0] + three[0] + ring[0] + edge_far
    low, high = edge[0], edge[1]
    above, below = lax.ppermute(low, "gz", DOWN), lax.ppermute(high, "gz", UP)
    result = near[1][0] + near_came[0] + far_own + direct + last
    d, v = result[0], result[1]

    wide = (a.reshape(rows + 2, *CELL) for a in (low, high, below, above, k_here, k_low, k_high))
    d, v = mend(d.reshape(rows, *CELL), v.reshape(rows, *CELL), *wide)
    return unpacked(d), unpacked(v)


def solution(mesh):
    return jax.shard_map(
        local,
        mesh=mesh,
        in_specs=(
            P("tm", None, "gz", None),
            P("tm", None, "gz", None),
            P("tm", None, "gz", None),
            P("tm", None, "gz", None),
            P(None, "gz", None),
            P("tm", None),
        ),
        out_specs=(P("tm", "gz", None), P("tm", "gz", None)),
        check_vma=False,
    )
```

```python
import jax
import jax.numpy as jnp
from jax import lax
from jax.experimental import pallas as pl
from jax.experimental.pallas import tpu as pltpu
from jax.sharding import PartitionSpec as P

CHIPS = 8
COUNT = 16
SLABS = 8
GROUP = 16
MIB = 1024 * 1024
F32 = jnp.float32


def packed(cells):
    x = cells.shape[0]
    return cells.reshape(x, 4, 4, 128).transpose(0, 2, 1, 3).reshape(x, 2, 8, 128)


def unpacked(cells):
    x = cells.shape[0]
    return cells.reshape(x, 4, 4, 128).transpose(0, 2, 1, 3).reshape(x, 4, 512)


def roll(cells, shift):
    return pltpu.roll(cells, shift % 8, 1)


def places(n):
    sub = lax.broadcasted_iota(jnp.int32, (n, 8, 128), 1)
    return sub, lax.rem(sub, 4), lax.broadcasted_iota(jnp.int32, (n, 8, 128), 2)


def spread(field, speed, row, n, lower, upper):
    sub, z, lane = places(n)
    first, at_start, at_end = sub < 4, lane == 0, lane == 127
    v = [field[pl.ds(row + 1, n), h] for h in (0, 1)]
    k = [speed[pl.ds(row + 1, n), h] for h in (0, 1)]

    def ahead(a, b):
        ra, rb = pltpu.roll(a, 127, 2), pltpu.roll(b, 127, 2)
        qa, qb = roll(ra, 4), roll(rb, 4)
        return (
            jnp.where(at_end, jnp.where(first, qa, qb), ra),
            jnp.where(at_end, jnp.where(first, qb, 0.0), rb),
        )

    def behind(a, b, edge):
        ra, rb = pltpu.roll(a, 1, 2), pltpu.roll(b, 1, 2)
        qa, qb = roll(ra, 4), roll(rb, 4)
        return (
            jnp.where(at_start, jnp.where(first, edge, qa), ra),
            jnp.where(at_start, jnp.where(first, qa, qb), rb),
        )

    v_y, k_y = ahead(*v), ahead(*k)
    f_y = [(k[h] + k_y[h]) * (v_y[h] - v[h]) for h in (0, 1)]
    b_y = behind(*f_y, k[0] * v[0])
    out = []
    for h in (0, 1):
        kv = k[h] * v[h]
        f_z = jnp.where(z == 3, -upper * kv, (k[h] + roll(k[h], -1)) * (roll(v[h], -1) - v[h]))
        b_z = jnp.where(z == 0, lower * kv, roll(f_z, 1))
        f_x = (k[h] + speed[pl.ds(row + 2, n), h]) * (field[pl.ds(row + 2, n), h] - v[h])
        b_x = (k[h] + speed[pl.ds(row, n), h]) * (v[h] - field[pl.ds(row, n), h])
        out.append((f_x - b_x) + (f_y[h] - b_y[h]) + (f_z - b_z))
    return v, out


def widen(scratch, main, before, after, block, blocks):
    rows = main.shape[0]
    scratch[pl.ds(1, rows)] = main[...]
    scratch[pl.ds(0, 1)] = jnp.where(block > 0, before[...], 0.0)
    scratch[pl.ds(rows + 1, 1)] = jnp.where(block < blocks - 1, after[...], 0.0)


def where_am_i():
    me = lax.axis_index("tm")
    return me // 8, lax.rem(me // 2, 4), lax.rem(me, 2)


def series_kernel(coeffs, u, k, p, cos, sin, far_other, far_same, near_other, near_same, ends_other, ends_same, rest_other, rest_same,
                  us, ks, ns, ds, vs, fx, fy, fw, fz, fm, es, in_sem, out_sem, edge_sem):
    cells = u.shape[0] // 16
    rows = cells // CHIPS
    half_rows = rows // 2
    my_z, my_y, my_core = where_am_i()
    slab = lax.axis_index("gz")
    lower, upper = jnp.where(slab == 0, 1.0, 0.0), jnp.where(slab == SLABS - 1, 1.0, 0.0)
    c0, c1, c2, c3 = (coeffs[0, i] for i in range(4))
    sub = lax.broadcasted_iota(jnp.int32, (8, 128), 0)
    lane = lax.broadcasted_iota(jnp.int32, (8, 128), 1)
    z = lax.rem(sub, 4)
    first, at_start, at_end = sub < 4, lane == 0, lane == 127
    open_up, open_down = jnp.where(z == 3, 0.0, 1.0), jnp.where(z == 0, 0.0, 1.0)
    of_u = jnp.where(z == 0, c1, jnp.where(z == 1, c0, jnp.where(z == 2, c3, c2)))
    of_n = jnp.where(z == 1, c1, jnp.where(z == 3, c3, 0.0))
    y_first, y_last = jnp.logical_and(first, at_start), jnp.logical_and(jnp.logical_not(first), at_end)
    outer = jnp.where(z == 0, lower, 0.0) + jnp.where(z == 3, upper, 0.0)

    def arrays():
        return ((u, us, 16), (k, ks, 16), (p, ns, 16), (cos, ds, 0), (sin, vs, 0))

    def loads(c, which):
        return [
            pltpu.make_async_copy(a.at[pl.ds(c * rows * 16, rows * 16)], b.at[pl.ds(c * rows * 16 + off, rows * 16)], in_sem.at[i, c])
            for i, (a, b, off) in enumerate(arrays()) if i in which
        ]

    for c in range(CHIPS):
        for copy in loads(c, (0, 1, 2)):
            copy.start()
        if c:
            for copy in loads(c - 1, (3, 4)):
                copy.start()
    for copy in loads(CHIPS - 1, (3, 4)):
        copy.start()
    nothing = jnp.zeros((16, 128), F32)
    fx[0:16] = nothing
    fz[0:16] = nothing
    for side in (0, 1):
        es[side, 0:16] = nothing
        es[side, (cells + 1) * 16 : (cells + 2) * 16] = nothing
    for ref in (us, ks, ns):
        ref[0:16] = nothing
        ref[(cells + 1) * 16 : (cells + 2) * 16] = nothing

    def at(ref, row, by=0):
        return ref[pl.ds(row + by, 8), :]

    def ahead(ref, row, here):
        return pltpu.roll(jnp.where(at_start, at(ref, row, 4), here), 127, 1)

    def behind(ref, row, here):
        return pltpu.roll(jnp.where(at_end, at(ref, row, -4), here), 1, 1)

    def up(here):
        return pltpu.roll(here, 7, 0)

    def down(here):
        return pltpu.roll(here, 1, 0)

    def first_pass(c):
        def step(i, carry):
            start = (c * rows + i * GROUP + 1) * 16
            kk, uu, kx = {}, {}, {}

            def center(seen, ref, g, h):
                if (g, h) not in seen:
                    seen[g, h] = at(ref, start + g * 16 + h * 8)
                return seen[g, h]

            for h in (0, 1):
                kx[-1, h] = center(kk, ks, -1, h) + center(kk, ks, 0, h)
            for g in range(GROUP):
                for h in (0, 1):
                    row = start + g * 16 + h * 8
                    k0 = center(kk, ks, g, h)
                    kx[g, h] = k0 + center(kk, ks, g + 1, h)
                    ky, kw = k0 + ahead(ks, row, k0), k0 + behind(ks, row, k0)
                    if h == 0:
                        face_w = jnp.where(y_first, k0, kw)
                        face_y, kw = ky, jnp.where(y_first, 0.0, kw)
                    else:
                        face_y = jnp.where(y_last, k0, ky)
                        face_w, ky = kw, jnp.where(y_last, 0.0, ky)
                    kz, kv = (k0 + up(k0)) * open_up, (k0 + down(k0)) * open_down
                    mid = 24.0 - (((kx[g, h] + kx[g - 1, h]) + (face_y + face_w)) + ((kz + kv) + outer * k0))
                    for ref, value in ((fx, kx[g, h]), (fy, ky), (fw, kw), (fz, kz), (fm, mid)):
                        ref[pl.ds(row, 8), :] = value
                    v = center(uu, us, g, h)
                    out = (kx[g, h] * center(uu, us, g + 1, h) + kx[g - 1, h] * center(uu, us, g - 1, h)) + (kz * up(v) + kv * down(v))
                    out = out + (ky * ahead(us, row, v) + kw * behind(us, row, v)) + mid * v
                    ns[pl.ds(row, 8), :] = out * (-1.0 / 12.0) - at(ns, row)
            return carry

        lax.fori_loop(0, rows // GROUP, step, 0)

    def moments(c):
        def spread(ref, row, plane):
            return jnp.where(first, ref[pl.ds(row + plane, 1), :], ref[pl.ds(row + 4 + plane, 1), :])

        def step(i, carry):
            for g in range(2 * GROUP):
                row = (c * rows + 1) * 16 + (i * 2 * GROUP + g) * 8
                for side, plane in ((0, 0), (1, 3)):
                    es[side, pl.ds(row, 8), :] = of_u * spread(us, row, plane) + of_n * spread(ns, row, plane)
            return carry

        lax.fori_loop(0, rows // GROUP, step, 0)

    def second_pass(c):
        def step(i, carry):
            start = (c * rows + i * GROUP + 1) * 16
            nn, kx = {}, {}

            def center(seen, ref, g, h):
                if (g, h) not in seen:
                    seen[g, h] = at(ref, start + g * 16 + h * 8)
                return seen[g, h]

            for g in range(GROUP):
                for h in (0, 1):
                    row = start + g * 16 + h * 8
                    v = center(nn, ns, g, h)
                    kz = at(fz, row)
                    out = center(kx, fx, g, h) * center(nn, ns, g + 1, h) + center(kx, fx, g - 1, h) * center(nn, ns, g - 1, h)
                    out = out + (kz * up(v) + down(kz) * down(v))
                    out = out + (at(fy, row) * ahead(ns, row, v) + at(fw, row) * behind(ns, row, v)) + at(fm, row) * v
                    final = out * (-1.0 / 12.0) - at(us, row)
                    ds[pl.ds(row - 16, 8), :] = at(ds, row, -16) + c0 * v + c1 * final
                    vs[pl.ds(row - 16, 8), :] = at(vs, row, -16) + c2 * v + c3 * final
            return carry

        lax.fori_loop(0, rows // GROUP, step, 0)

    def place(c, core):
        return lax.rem((1 - 2 * core) * (lax.rem(c, 4) - my_y) + 8, 4), lax.rem(c // 4 + my_z, 2)

    def stores(c, core, same, far):
        turn, _ = place(c, core)
        here = pl.ds((c * rows + core * half_rows) * 16, half_rows * 16)
        to = ((far_other, far_same) if far else (near_other, near_same))[same]
        return [pltpu.make_async_copy(a.at[here], to.at[turn, i], out_sem.at[i, core, c]) for i, a in enumerate((ds, vs))]

    def edge_stores(c, core, same, is_end):
        turn, side = place(c, core)
        here = pl.ds((c * rows + core * half_rows) * 16, (half_rows + 2) * 16)
        to = ((ends_other, ends_same) if is_end else (rest_other, rest_same))[same]
        return [pltpu.make_async_copy(es.at[i, here], to.at[lax.rem(turn, 2), side, i], edge_sem.at[i, core, c]) for i in (0, 1)]

    def send(copies, c, core, test):
        for same in (0, 1):
            for kind in (0, 1):
                @pl.when(((my_core == core) == (same == 1)) & (test(*place(c, core)) == (kind == 1)))
                def _():
                    for copy in copies(c, core, same, kind):
                        copy.start()

    def send_edges(c, core):
        send(edge_stores, c, core, lambda turn, side: turn >= 2)

    def send_series(c, core):
        send(stores, c, core, lambda turn, side: side == 1)

    def chunk(c, carry):
        @pl.when(c < CHIPS)
        def _():
            @pl.when(c == 0)
            def _():
                for copy in loads(c, (0, 1, 2)):
                    copy.wait()

            @pl.when(c + 1 < CHIPS)
            def _():
                for copy in loads(c + 1, (0, 1, 2)):
                    copy.wait()

            first_pass(c)
            moments(c)
            send_edges(c, 0)

        @pl.when(c > 0)
        def _():
            send_edges(c - 1, 1)
            for copy in loads(c - 1, (3, 4)):
                copy.wait()
            second_pass(c - 1)
            for core in (0, 1):
                send_series(c - 1, core)

        return carry

    lax.fori_loop(0, CHIPS + 1, chunk, 0)

    def end(c, carry):
        for core in (0, 1):
            for copy in stores(c, core, 1, 1) + edge_stores(c, core, 1, 1):
                copy.wait()
        return carry

    lax.fori_loop(0, CHIPS, end, 0)


def mend_kernel(d, v, low, high, below, above, k, k_low, k_high, d_out, v_out, ds, vs):
    rows = d.shape[0]
    slab = lax.axis_index("gz")
    lower, upper = jnp.where(slab == 0, 1.0, 0.0), jnp.where(slab == SLABS - 1, 1.0, 0.0)
    wide = rows + 2
    z = places(wide)[1]
    factor = []
    for h in (0, 1):
        under = (1.0 - lower) * (k[:, h] + roll(k_low[:, h], -3))
        over = (1.0 - upper) * (k[:, h] + roll(k_high[:, h], 3))
        factor.append(jnp.where(z == 0, under, jnp.where(z == 3, -over, 0.0)) * (1.0 / 12.0))
    from_low = [low[:, h] - below[:, h] for h in (0, 1)]
    from_high = [above[:, h] - high[:, h] for h in (0, 1)]
    direct = []
    for field, slot in ((ds, 0), (vs, 2)):
        for h in (0, 1):
            a = jnp.where(z == 0, roll(from_low[h], -slot), roll(from_high[h], 3 - slot))
            b = jnp.where(z == 0, roll(from_low[h], -slot - 1), roll(from_high[h], 2 - slot))
            w = factor[h] * a
            field[:, h] = w
            direct.append((factor[h] * b + 2.0 * jnp.abs(factor[h]) * w)[1 : rows + 1])
    for field, given, out, direct_of in ((ds, d, d_out, direct[:2]), (vs, v, v_out, direct[2:])):
        w, outflow = spread(field, k, 0, rows, lower, upper)
        for h in (0, 1):
            out[:, h] = given[:, h] + direct_of[h] - outflow[h] * (1.0 / 12.0) - 2.0 * w[h]


ANYWHERE = pl.BlockSpec(memory_space=pl.ANY)
SMEM = pl.BlockSpec(memory_space=pltpu.SMEM)


def params(mib):
    return pltpu.CompilerParams(vmem_limit_bytes=mib * MIB)


def cost(mib):
    return pl.CostEstimate(flops=0, bytes_accessed=mib * MIB, transcendentals=0)


def flat(cells):
    return cells.reshape(-1, 128)


def series(coeffs, u, k, p, cos, sin):
    cells = u.shape[0] // 16
    share = jax.ShapeDtypeStruct((4, 2, cells // COUNT * 16, 128), F32)
    edge = jax.ShapeDtypeStruct((2, 2, 2, (cells // COUNT + 2) * 16, 128), F32)
    wide = pltpu.VMEM(((cells + 2) * 16, 128), F32)
    exact = pltpu.VMEM((cells * 16, 128), F32)
    return pl.pallas_call(
        series_kernel,
        out_shape=(share,) * 4 + (edge,) * 4,
        in_specs=[SMEM] + [ANYWHERE] * 5,
        out_specs=(ANYWHERE,) * 8,
        scratch_shapes=[wide, wide, wide, exact, exact, wide, wide, wide, wide, wide]
        + [
            pltpu.VMEM((2, (cells + 2) * 16, 128), F32),
            pltpu.SemaphoreType.DMA((5, CHIPS)),
            pltpu.SemaphoreType.DMA((2, 2, CHIPS)),
            pltpu.SemaphoreType.DMA((2, 2, CHIPS)),
        ],
        compiler_params=params(56),
        cost_estimate=cost(45),
    )(coeffs, u, k, p, cos, sin)


def mend(d, v, low, high, below, above, k, k_low, k_high):
    shape = jax.ShapeDtypeStruct(d.shape, F32)
    whole = pl.BlockSpec(memory_space=pltpu.VMEM)
    return pl.pallas_call(
        mend_kernel,
        out_shape=(shape, shape),
        in_specs=[whole] * 9,
        out_specs=(whole, whole),
        scratch_shapes=[pltpu.VMEM(k.shape, F32)] * 2,
        compiler_params=params(16),
        cost_estimate=cost(4),
    )(d, v, low, high, below, above, k, k_low, k_high)


CELL = (2, 8, 128)


def along_y(sign):
    def goal(i):
        z, y, core = i // 8, (i // 2) % 4, i % 2
        return z * 8 + ((y + sign * (1 - 2 * core)) % 4) * 2 + core

    return [(i, goal(i)) for i in range(COUNT)]


FORTH, BACK = along_y(1), along_y(-1)
ACROSS = [(i, i ^ 8) for i in range(COUNT)]
SIBLING = [(i, i ^ 1) for i in range(COUNT)]
UP = [(i, i + 1) for i in range(SLABS - 1)]
DOWN = [(i + 1, i) for i in range(SLABS - 1)]


def to_sibling(other):
    return lax.ppermute(other, "tm", SIBLING)


def forth(cells):
    return lax.ppermute(cells, "tm", FORTH)


def back(cells):
    return lax.ppermute(cells, "tm", BACK)


def across(cells):
    return lax.ppermute(cells, "tm", ACROSS)


def after(first, then):
    return lax.optimization_barrier((first, then))


def local(prev_term, last_term, cos_sum, sin_sum, speed_sq, series_coeffs):
    u, p, k = flat(packed(last_term[0])), flat(packed(prev_term[0])), flat(packed(speed_sq))
    cos, sin = flat(packed(cos_sum[0])), flat(packed(sin_sum[0]))
    rows = last_term.shape[1] // COUNT
    me = lax.axis_index("tm")

    outs = series(series_coeffs, u, k, p, cos, sin)
    far_other, far_same, near_other, near_same, ends_other, ends_same, rest_other, rest_same = outs

    ends_came, far_came = to_sibling(ends_other), to_sibling(far_other)
    rest_came = to_sibling(rest_other)
    ends_two = forth(ends_same[0] + ends_came[0])
    far_two, ends_came = after(far_same[2] + far_came[2], ends_came)
    far_two_came = across(far_two)
    ends_back = back(ends_same[1] + ends_came[1])

    rest_came, k = after(rest_came, k)
    start = me * rows * 16
    k_here = jnp.concatenate(
        [
            jnp.where(me > 0, lax.dynamic_slice_in_dim(k, jnp.maximum(start - 16, 0), 16), 0.0),
            lax.dynamic_slice_in_dim(k, start, rows * 16),
            jnp.where(me < COUNT - 1, lax.dynamic_slice_in_dim(k, jnp.minimum(start + rows * 16, k.shape[0] - 16), 16), 0.0),
        ]
    )
    k_low, k_high = lax.ppermute(k_here, "gz", UP), lax.ppermute(k_here, "gz", DOWN)

    (far_two_came, k_low, k_high), ends_two = after((far_two_came, k_low, k_high), ends_two)
    ends_two, (far_came, near_other) = after(ends_two, (far_came, near_other))
    near_came = to_sibling(near_other)
    ring = forth(rest_same[1] + rest_came[1] + ends_two)
    far_back_came = across(far_same[3] + far_came[3])
    far_next_came = across(far_same[1] + far_came[1])
    two, direct = near_same[2] + near_came[2] + far_two_came, near_same[3] + near_came[3] + far_back_came
    (two, direct), ring = after((two, direct), ring)
    two, direct = forth(two), back(direct)
    edge_far = rest_same[0, 1] + rest_came[0, 1] + ends_back[1] + ring[1]
    edge_far, (far_came, far_next_came) = after(edge_far, (far_came, far_next_came))
    edge_far = across(edge_far)
    far_own_came = across(far_same[0] + far_came[0])
    last = near_same[1] + near_came[1] + far_next_came + two
    last, edge_far = after(last, edge_far)
    last = forth(last)
    edge = rest_same[0, 0] + rest_came[0, 0] + ends_back[0] + ring[0] + edge_far
    low, high = edge[0], edge[1]
    above, below = lax.ppermute(low, "gz", DOWN), lax.ppermute(high, "gz", UP)
    result = near_same[0] + near_came[0] + far_own_came + direct + last
    d, v = result[0], result[1]

    wide = (a.reshape(rows + 2, *CELL) for a in (low, high, below, above, k_here, k_low, k_high))
    d, v = mend(d.reshape(rows, *CELL), v.reshape(rows, *CELL), *wide)
    return unpacked(d), unpacked(v)


def solution(mesh):
    return jax.shard_map(
        local,
        mesh=mesh,
        in_specs=(
            P("tm", None, "gz", None),
            P("tm", None, "gz", None),
            P("tm", None, "gz", None),
            P("tm", None, "gz", None),
            P(None, "gz", None),
            P("tm", None),
        ),
        out_specs=(P("tm", "gz", None), P("tm", "gz", None)),
        check_vma=False,
    )
```

```python
import jax
import jax.numpy as jnp
from jax import lax
from jax.experimental import pallas as pl
from jax.experimental.pallas import tpu as pltpu
from jax.sharding import PartitionSpec as P

CHIPS = 8
COUNT = 16
SLABS = 8
GROUP = 16
MIB = 1024 * 1024
F32 = jnp.float32


def packed(cells):
    x = cells.shape[0]
    return cells.reshape(x, 4, 4, 128).transpose(0, 2, 1, 3).reshape(x, 2, 8, 128)


def unpacked(cells):
    x = cells.shape[0]
    return cells.reshape(x, 4, 4, 128).transpose(0, 2, 1, 3).reshape(x, 4, 512)


def roll(cells, shift):
    return pltpu.roll(cells, shift % 8, 1)


def places(n):
    sub = lax.broadcasted_iota(jnp.int32, (n, 8, 128), 1)
    return sub, lax.rem(sub, 4), lax.broadcasted_iota(jnp.int32, (n, 8, 128), 2)


def spread(field, speed, row, n, lower, upper):
    sub, z, lane = places(n)
    first, at_start, at_end = sub < 4, lane == 0, lane == 127
    v = [field[pl.ds(row + 1, n), h] for h in (0, 1)]
    k = [speed[pl.ds(row + 1, n), h] for h in (0, 1)]

    def ahead(a, b):
        ra, rb = pltpu.roll(a, 127, 2), pltpu.roll(b, 127, 2)
        qa, qb = roll(ra, 4), roll(rb, 4)
        return (
            jnp.where(at_end, jnp.where(first, qa, qb), ra),
            jnp.where(at_end, jnp.where(first, qb, 0.0), rb),
        )

    def behind(a, b, edge):
        ra, rb = pltpu.roll(a, 1, 2), pltpu.roll(b, 1, 2)
        qa, qb = roll(ra, 4), roll(rb, 4)
        return (
            jnp.where(at_start, jnp.where(first, edge, qa), ra),
            jnp.where(at_start, jnp.where(first, qa, qb), rb),
        )

    v_y, k_y = ahead(*v), ahead(*k)
    f_y = [(k[h] + k_y[h]) * (v_y[h] - v[h]) for h in (0, 1)]
    b_y = behind(*f_y, k[0] * v[0])
    out = []
    for h in (0, 1):
        kv = k[h] * v[h]
        f_z = jnp.where(z == 3, -upper * kv, (k[h] + roll(k[h], -1)) * (roll(v[h], -1) - v[h]))
        b_z = jnp.where(z == 0, lower * kv, roll(f_z, 1))
        f_x = (k[h] + speed[pl.ds(row + 2, n), h]) * (field[pl.ds(row + 2, n), h] - v[h])
        b_x = (k[h] + speed[pl.ds(row, n), h]) * (v[h] - field[pl.ds(row, n), h])
        out.append((f_x - b_x) + (f_y[h] - b_y[h]) + (f_z - b_z))
    return v, out


def widen(scratch, main, before, after, block, blocks):
    rows = main.shape[0]
    scratch[pl.ds(1, rows)] = main[...]
    scratch[pl.ds(0, 1)] = jnp.where(block > 0, before[...], 0.0)
    scratch[pl.ds(rows + 1, 1)] = jnp.where(block < blocks - 1, after[...], 0.0)


def where_am_i():
    me = lax.axis_index("tm")
    return me // 8, lax.rem(me // 2, 4), lax.rem(me, 2)


def series_kernel(coeffs, u, k, p, cos, sin, far_other, far_same, near_other, near_same, ends_other, ends_same, rest_other, rest_same,
                  us, ks, ns, ds, vs, fx, fy, fw, fz, fm, es, in_sem, out_sem, edge_sem):
    cells = u.shape[0] // 16
    rows = cells // CHIPS
    half_rows = rows // 2
    my_z, my_y, my_core = where_am_i()
    slab = lax.axis_index("gz")
    lower, upper = jnp.where(slab == 0, 1.0, 0.0), jnp.where(slab == SLABS - 1, 1.0, 0.0)
    c0, c1, c2, c3 = (coeffs[0, i] for i in range(4))
    sub = lax.broadcasted_iota(jnp.int32, (8, 128), 0)
    lane = lax.broadcasted_iota(jnp.int32, (8, 128), 1)
    z = lax.rem(sub, 4)
    first, at_start, at_end = sub < 4, lane == 0, lane == 127
    open_up, open_down = jnp.where(z == 3, 0.0, 1.0), jnp.where(z == 0, 0.0, 1.0)
    of_u = jnp.where(z == 0, c1, jnp.where(z == 1, c0, jnp.where(z == 2, c3, c2)))
    of_n = jnp.where(z == 1, c1, jnp.where(z == 3, c3, 0.0))
    y_first, y_last = jnp.logical_and(first, at_start), jnp.logical_and(jnp.logical_not(first), at_end)
    outer = jnp.where(z == 0, lower, 0.0) + jnp.where(z == 3, upper, 0.0)

    def arrays():
        return ((u, us, 16), (k, ks, 16), (p, ns, 16), (cos, ds, 0), (sin, vs, 0))

    def loads(c, which):
        return [
            pltpu.make_async_copy(a.at[pl.ds(c * rows * 16, rows * 16)], b.at[pl.ds(c * rows * 16 + off, rows * 16)], in_sem.at[i, c])
            for i, (a, b, off) in enumerate(arrays()) if i in which
        ]

    for c in range(CHIPS):
        for copy in loads(c, (0, 1, 2)):
            copy.start()
        if c:
            for copy in loads(c - 1, (3, 4)):
                copy.start()
    for copy in loads(CHIPS - 1, (3, 4)):
        copy.start()
    nothing = jnp.zeros((16, 128), F32)
    fx[0:16] = nothing
    fz[0:16] = nothing
    for side in (0, 1):
        es[side, 0:16] = nothing
        es[side, (cells + 1) * 16 : (cells + 2) * 16] = nothing
    for ref in (us, ks, ns):
        ref[0:16] = nothing
        ref[(cells + 1) * 16 : (cells + 2) * 16] = nothing

    def at(ref, row, by=0):
        return ref[pl.ds(row + by, 8), :]

    def ahead(ref, row, here):
        return pltpu.roll(jnp.where(at_start, at(ref, row, 4), here), 127, 1)

    def behind(ref, row, here):
        return pltpu.roll(jnp.where(at_end, at(ref, row, -4), here), 1, 1)

    def up(here):
        return pltpu.roll(here, 7, 0)

    def down(here):
        return pltpu.roll(here, 1, 0)

    def first_pass(c):
        def step(i, carry):
            start = (c * rows + i * GROUP + 1) * 16
            kk, uu, kx = {}, {}, {}

            def center(seen, ref, g, h):
                if (g, h) not in seen:
                    seen[g, h] = at(ref, start + g * 16 + h * 8)
                return seen[g, h]

            for h in (0, 1):
                kx[-1, h] = center(kk, ks, -1, h) + center(kk, ks, 0, h)
            for g in range(GROUP):
                for h in (0, 1):
                    row = start + g * 16 + h * 8
                    k0 = center(kk, ks, g, h)
                    kx[g, h] = k0 + center(kk, ks, g + 1, h)
                    ky, kw = k0 + ahead(ks, row, k0), k0 + behind(ks, row, k0)
                    if h == 0:
                        face_w = jnp.where(y_first, k0, kw)
                        face_y, kw = ky, jnp.where(y_first, 0.0, kw)
                    else:
                        face_y = jnp.where(y_last, k0, ky)
                        face_w, ky = kw, jnp.where(y_last, 0.0, ky)
                    kz, kv = (k0 + up(k0)) * open_up, (k0 + down(k0)) * open_down
                    mid = 24.0 - (((kx[g, h] + kx[g - 1, h]) + (face_y + face_w)) + ((kz + kv) + outer * k0))
                    for ref, value in ((fx, kx[g, h]), (fy, ky), (fw, kw), (fz, kz), (fm, mid)):
                        ref[pl.ds(row, 8), :] = value
                    v = center(uu, us, g, h)
                    out = (kx[g, h] * center(uu, us, g + 1, h) + kx[g - 1, h] * center(uu, us, g - 1, h)) + (kz * up(v) + kv * down(v))
                    out = out + (ky * ahead(us, row, v) + kw * behind(us, row, v)) + mid * v
                    ns[pl.ds(row, 8), :] = out * (-1.0 / 12.0) - at(ns, row)
            return carry

        lax.fori_loop(0, rows // GROUP, step, 0)

    def moments(c):
        def spread(ref, row, plane):
            return jnp.where(first, ref[pl.ds(row + plane, 1), :], ref[pl.ds(row + 4 + plane, 1), :])

        def step(i, carry):
            for g in range(2 * GROUP):
                row = (c * rows + 1) * 16 + (i * 2 * GROUP + g) * 8
                for side, plane in ((0, 0), (1, 3)):
                    es[side, pl.ds(row, 8), :] = of_u * spread(us, row, plane) + of_n * spread(ns, row, plane)
            return carry

        lax.fori_loop(0, rows // GROUP, step, 0)

    def second_pass(c):
        def step(i, carry):
            start = (c * rows + i * GROUP + 1) * 16
            nn, kx = {}, {}

            def center(seen, ref, g, h):
                if (g, h) not in seen:
                    seen[g, h] = at(ref, start + g * 16 + h * 8)
                return seen[g, h]

            for g in range(GROUP):
                for h in (0, 1):
                    row = start + g * 16 + h * 8
                    v = center(nn, ns, g, h)
                    kz = at(fz, row)
                    out = center(kx, fx, g, h) * center(nn, ns, g + 1, h) + center(kx, fx, g - 1, h) * center(nn, ns, g - 1, h)
                    out = out + (kz * up(v) + down(kz) * down(v))
                    out = out + (at(fy, row) * ahead(ns, row, v) + at(fw, row) * behind(ns, row, v)) + at(fm, row) * v
                    final = out * (-1.0 / 12.0) - at(us, row)
                    ds[pl.ds(row - 16, 8), :] = at(ds, row, -16) + c0 * v + c1 * final
                    vs[pl.ds(row - 16, 8), :] = at(vs, row, -16) + c2 * v + c3 * final
            return carry

        lax.fori_loop(0, rows // GROUP, step, 0)

    def place(c, core):
        return lax.rem((1 - 2 * core) * (lax.rem(c, 4) - my_y) + 8, 4), lax.rem(c // 4 + my_z, 2)

    def stores(c, core, same, far):
        turn, _ = place(c, core)
        here = pl.ds((c * rows + core * half_rows) * 16, half_rows * 16)
        to = ((far_other, far_same) if far else (near_other, near_same))[same]
        return [pltpu.make_async_copy(a.at[here], to.at[turn, i], out_sem.at[i, core, c]) for i, a in enumerate((ds, vs))]

    def edge_stores(c, core, same, is_end):
        turn, side = place(c, core)
        here = pl.ds((c * rows + core * half_rows) * 16, (half_rows + 2) * 16)
        to = ((ends_other, ends_same) if is_end else (rest_other, rest_same))[same]
        return [pltpu.make_async_copy(es.at[i, here], to.at[lax.rem(turn, 2), side, i], edge_sem.at[i, core, c]) for i in (0, 1)]

    def send(copies, c, core, test):
        for same in (0, 1):
            for kind in (0, 1):
                @pl.when(((my_core == core) == (same == 1)) & (test(*place(c, core)) == (kind == 1)))
                def _():
                    for copy in copies(c, core, same, kind):
                        copy.start()

    def send_edges(c, core):
        send(edge_stores, c, core, lambda turn, side: turn >= 2)

    def send_series(c, core):
        send(stores, c, core, lambda turn, side: side == 1)

    def chunk(c, carry):
        @pl.when(c < CHIPS)
        def _():
            @pl.when(c == 0)
            def _():
                for copy in loads(c, (0, 1, 2)):
                    copy.wait()

            @pl.when(c + 1 < CHIPS)
            def _():
                for copy in loads(c + 1, (0, 1, 2)):
                    copy.wait()

            first_pass(c)
            moments(c)
            send_edges(c, 0)

        @pl.when(c > 0)
        def _():
            send_edges(c - 1, 1)
            for copy in loads(c - 1, (3, 4)):
                copy.wait()
            second_pass(c - 1)
            for core in (0, 1):
                send_series(c - 1, core)

        return carry

    lax.fori_loop(0, CHIPS + 1, chunk, 0)

    def end(c, carry):
        for core in (0, 1):
            for copy in stores(c, core, 1, 1) + edge_stores(c, core, 1, 1):
                copy.wait()
        return carry

    lax.fori_loop(0, CHIPS, end, 0)


def mend_kernel(d, v, low, high, below, above, k, k_low, k_high, d_out, v_out, ds, vs):
    rows = d.shape[0]
    slab = lax.axis_index("gz")
    lower, upper = jnp.where(slab == 0, 1.0, 0.0), jnp.where(slab == SLABS - 1, 1.0, 0.0)
    wide = rows + 2
    z = places(wide)[1]
    factor = []
    for h in (0, 1):
        under = (1.0 - lower) * (k[:, h] + roll(k_low[:, h], -3))
        over = (1.0 - upper) * (k[:, h] + roll(k_high[:, h], 3))
        factor.append(jnp.where(z == 0, under, jnp.where(z == 3, -over, 0.0)) * (1.0 / 12.0))
    from_low = [low[:, h] - below[:, h] for h in (0, 1)]
    from_high = [above[:, h] - high[:, h] for h in (0, 1)]
    direct = []
    for field, slot in ((ds, 0), (vs, 2)):
        for h in (0, 1):
            a = jnp.where(z == 0, roll(from_low[h], -slot), roll(from_high[h], 3 - slot))
            b = jnp.where(z == 0, roll(from_low[h], -slot - 1), roll(from_high[h], 2 - slot))
            w = factor[h] * a
            field[:, h] = w
            direct.append((factor[h] * b + 2.0 * jnp.abs(factor[h]) * w)[1 : rows + 1])
    for field, given, out, direct_of in ((ds, d, d_out, direct[:2]), (vs, v, v_out, direct[2:])):
        w, outflow = spread(field, k, 0, rows, lower, upper)
        for h in (0, 1):
            out[:, h] = given[:, h] + direct_of[h] - outflow[h] * (1.0 / 12.0) - 2.0 * w[h]


ANYWHERE = pl.BlockSpec(memory_space=pl.ANY)
SMEM = pl.BlockSpec(memory_space=pltpu.SMEM)


def params(mib):
    return pltpu.CompilerParams(vmem_limit_bytes=mib * MIB)


def cost(mib):
    return pl.CostEstimate(flops=0, bytes_accessed=mib * MIB, transcendentals=0)


def flat(cells):
    return cells.reshape(-1, 128)


def series(coeffs, u, k, p, cos, sin):
    cells = u.shape[0] // 16
    share = jax.ShapeDtypeStruct((4, 2, cells // COUNT * 16, 128), F32)
    edge = jax.ShapeDtypeStruct((2, 2, 2, (cells // COUNT + 2) * 16, 128), F32)
    wide = pltpu.VMEM(((cells + 2) * 16, 128), F32)
    exact = pltpu.VMEM((cells * 16, 128), F32)
    return pl.pallas_call(
        series_kernel,
        out_shape=(share,) * 4 + (edge,) * 4,
        in_specs=[SMEM] + [ANYWHERE] * 5,
        out_specs=(ANYWHERE,) * 8,
        scratch_shapes=[wide, wide, wide, exact, exact, wide, wide, wide, wide, wide]
        + [
            pltpu.VMEM((2, (cells + 2) * 16, 128), F32),
            pltpu.SemaphoreType.DMA((5, CHIPS)),
            pltpu.SemaphoreType.DMA((2, 2, CHIPS)),
            pltpu.SemaphoreType.DMA((2, 2, CHIPS)),
        ],
        compiler_params=params(56),
        cost_estimate=cost(45),
    )(coeffs, u, k, p, cos, sin)


def mend(d, v, low, high, below, above, k, k_low, k_high):
    shape = jax.ShapeDtypeStruct(d.shape, F32)
    whole = pl.BlockSpec(memory_space=pltpu.VMEM)
    return pl.pallas_call(
        mend_kernel,
        out_shape=(shape, shape),
        in_specs=[whole] * 9,
        out_specs=(whole, whole),
        scratch_shapes=[pltpu.VMEM(k.shape, F32)] * 2,
        compiler_params=params(16),
        cost_estimate=cost(4),
    )(d, v, low, high, below, above, k, k_low, k_high)


CELL = (2, 8, 128)


def along_y(sign):
    def goal(i):
        z, y, core = i // 8, (i // 2) % 4, i % 2
        return z * 8 + ((y + sign * (1 - 2 * core)) % 4) * 2 + core

    return [(i, goal(i)) for i in range(COUNT)]


FORTH, BACK = along_y(1), along_y(-1)
ACROSS = [(i, i ^ 8) for i in range(COUNT)]
SIBLING = [(i, i ^ 1) for i in range(COUNT)]
UP = [(i, i + 1) for i in range(SLABS - 1)]
DOWN = [(i + 1, i) for i in range(SLABS - 1)]


def to_sibling(other):
    return lax.ppermute(other, "tm", SIBLING)


def forth(cells):
    return lax.ppermute(cells, "tm", FORTH)


def back(cells):
    return lax.ppermute(cells, "tm", BACK)


def across(cells):
    return lax.ppermute(cells, "tm", ACROSS)


def after(first, then):
    return lax.optimization_barrier((first, then))[1]


def local(prev_term, last_term, cos_sum, sin_sum, speed_sq, series_coeffs):
    u, p, k = flat(packed(last_term[0])), flat(packed(prev_term[0])), flat(packed(speed_sq))
    cos, sin = flat(packed(cos_sum[0])), flat(packed(sin_sum[0]))
    rows = last_term.shape[1] // COUNT
    me = lax.axis_index("tm")

    outs = series(series_coeffs, u, k, p, cos, sin)
    far_other, far_same, near_other, near_same, ends_other, ends_same, rest_other, rest_same = outs

    ends_came, far_came = to_sibling(ends_other), to_sibling(far_other)
    rest_came, near_came = to_sibling(rest_other), to_sibling(near_other)
    ends_two = forth(ends_same[0] + ends_came[0])
    far_ends = far_same[2:] + far_came[2:]
    ends_came = after(far_ends, ends_came)
    far_ends_came, far_rest_came = across(far_ends), across(far_same[:2] + far_came[:2])
    ends_back = back(ends_same[1] + ends_came[1])

    start = me * rows * 16
    k_here = jnp.concatenate(
        [
            jnp.where(me > 0, lax.dynamic_slice_in_dim(k, jnp.maximum(start - 16, 0), 16), 0.0),
            lax.dynamic_slice_in_dim(k, start, rows * 16),
            jnp.where(me < COUNT - 1, lax.dynamic_slice_in_dim(k, jnp.minimum(start + rows * 16, k.shape[0] - 16), 16), 0.0),
        ]
    )
    k_low, k_high = lax.ppermute(k_here, "gz", UP), lax.ppermute(k_here, "gz", DOWN)

    ring = forth(rest_same[1] + rest_came[1] + ends_two)
    two, direct = (near_same[t] + near_came[t] + far_ends_came[t - 2] for t in (2, 3))
    ring = after((two, direct, k_low, k_high), ring)
    two, direct = forth(two), back(direct)
    edge_far = rest_same[0, 1] + rest_came[0, 1] + ends_back[1] + ring[1]
    far_rest_came = after(edge_far, far_rest_came)
    edge_far = across(edge_far)
    last = near_same[1] + near_came[1] + far_rest_came[1] + two
    edge_far = after(last, edge_far)
    last = forth(last)
    edge = rest_same[0, 0] + rest_came[0, 0] + ends_back[0] + ring[0] + edge_far
    low, high = edge[0], edge[1]
    above, below = lax.ppermute(low, "gz", DOWN), lax.ppermute(high, "gz", UP)
    result = near_same[0] + near_came[0] + far_rest_came[0] + direct + last
    d, v = result[0], result[1]

    wide = (a.reshape(rows + 2, *CELL) for a in (low, high, below, above, k_here, k_low, k_high))
    d, v = mend(d.reshape(rows, *CELL), v.reshape(rows, *CELL), *wide)
    return unpacked(d), unpacked(v)


def solution(mesh):
    return jax.shard_map(
        local,
        mesh=mesh,
        in_specs=(
            P("tm", None, "gz", None),
            P("tm", None, "gz", None),
            P("tm", None, "gz", None),
            P("tm", None, "gz", None),
            P(None, "gz", None),
            P("tm", None),
        ),
        out_specs=(P("tm", "gz", None), P("tm", "gz", None)),
        check_vma=False,
    )
```

```python
import jax
import jax.numpy as jnp
from jax import lax
from jax.experimental import pallas as pl
from jax.experimental.pallas import tpu as pltpu
from jax.sharding import PartitionSpec as P

CHIPS = 8
COUNT = 16
SLABS = 8
GROUP = 16
MIB = 1024 * 1024
F32 = jnp.float32


def packed(cells):
    x = cells.shape[0]
    return cells.reshape(x, 4, 4, 128).transpose(0, 2, 1, 3).reshape(x, 2, 8, 128)


def unpacked(cells):
    x = cells.shape[0]
    return cells.reshape(x, 4, 4, 128).transpose(0, 2, 1, 3).reshape(x, 4, 512)


def roll(cells, shift):
    return pltpu.roll(cells, shift % 8, 1)


def places(n):
    sub = lax.broadcasted_iota(jnp.int32, (n, 8, 128), 1)
    return sub, lax.rem(sub, 4), lax.broadcasted_iota(jnp.int32, (n, 8, 128), 2)


def spread(field, speed, row, n, lower, upper):
    sub, z, lane = places(n)
    first, at_start, at_end = sub < 4, lane == 0, lane == 127
    v = [field[pl.ds(row + 1, n), h] for h in (0, 1)]
    k = [speed[pl.ds(row + 1, n), h] for h in (0, 1)]

    def ahead(a, b):
        ra, rb = pltpu.roll(a, 127, 2), pltpu.roll(b, 127, 2)
        qa, qb = roll(ra, 4), roll(rb, 4)
        return (
            jnp.where(at_end, jnp.where(first, qa, qb), ra),
            jnp.where(at_end, jnp.where(first, qb, 0.0), rb),
        )

    def behind(a, b, edge):
        ra, rb = pltpu.roll(a, 1, 2), pltpu.roll(b, 1, 2)
        qa, qb = roll(ra, 4), roll(rb, 4)
        return (
            jnp.where(at_start, jnp.where(first, edge, qa), ra),
            jnp.where(at_start, jnp.where(first, qa, qb), rb),
        )

    v_y, k_y = ahead(*v), ahead(*k)
    f_y = [(k[h] + k_y[h]) * (v_y[h] - v[h]) for h in (0, 1)]
    b_y = behind(*f_y, k[0] * v[0])
    out = []
    for h in (0, 1):
        kv = k[h] * v[h]
        f_z = jnp.where(z == 3, -upper * kv, (k[h] + roll(k[h], -1)) * (roll(v[h], -1) - v[h]))
        b_z = jnp.where(z == 0, lower * kv, roll(f_z, 1))
        f_x = (k[h] + speed[pl.ds(row + 2, n), h]) * (field[pl.ds(row + 2, n), h] - v[h])
        b_x = (k[h] + speed[pl.ds(row, n), h]) * (v[h] - field[pl.ds(row, n), h])
        out.append((f_x - b_x) + (f_y[h] - b_y[h]) + (f_z - b_z))
    return v, out


def widen(scratch, main, before, after, block, blocks):
    rows = main.shape[0]
    scratch[pl.ds(1, rows)] = main[...]
    scratch[pl.ds(0, 1)] = jnp.where(block > 0, before[...], 0.0)
    scratch[pl.ds(rows + 1, 1)] = jnp.where(block < blocks - 1, after[...], 0.0)


def where_am_i():
    me = lax.axis_index("tm")
    return me // 8, lax.rem(me // 2, 4), lax.rem(me, 2)


def series_kernel(coeffs, u, k, p, cos, sin, far_other, far_same, near_other, near_same, ends_other, ends_same, rest_other, rest_same,
                  us, ks, ns, ds, vs, fx, fy, fw, fz, fm, es, in_sem, out_sem, edge_sem):
    cells = u.shape[0] // 16
    rows = cells // CHIPS
    half_rows = rows // 2
    my_z, my_y, my_core = where_am_i()
    slab = lax.axis_index("gz")
    lower, upper = jnp.where(slab == 0, 1.0, 0.0), jnp.where(slab == SLABS - 1, 1.0, 0.0)
    c0, c1, c2, c3 = (coeffs[0, i] for i in range(4))
    sub = lax.broadcasted_iota(jnp.int32, (8, 128), 0)
    lane = lax.broadcasted_iota(jnp.int32, (8, 128), 1)
    z = lax.rem(sub, 4)
    first, at_start, at_end = sub < 4, lane == 0, lane == 127
    open_up, open_down = jnp.where(z == 3, 0.0, 1.0), jnp.where(z == 0, 0.0, 1.0)
    of_u = jnp.where(z == 0, c1, jnp.where(z == 1, c0, jnp.where(z == 2, c3, c2)))
    of_n = jnp.where(z == 1, c1, jnp.where(z == 3, c3, 0.0))
    y_first, y_last = jnp.logical_and(first, at_start), jnp.logical_and(jnp.logical_not(first), at_end)
    outer = jnp.where(z == 0, lower, 0.0) + jnp.where(z == 3, upper, 0.0)

    def arrays():
        return ((u, us, 16), (k, ks, 16), (p, ns, 16), (cos, ds, 0), (sin, vs, 0))

    def loads(c, which):
        return [
            pltpu.make_async_copy(a.at[pl.ds(c * rows * 16, rows * 16)], b.at[pl.ds(c * rows * 16 + off, rows * 16)], in_sem.at[i, c])
            for i, (a, b, off) in enumerate(arrays()) if i in which
        ]

    for c in range(CHIPS):
        for copy in loads(c, (0, 1, 2)):
            copy.start()
        if c:
            for copy in loads(c - 1, (3, 4)):
                copy.start()
    for copy in loads(CHIPS - 1, (3, 4)):
        copy.start()
    nothing = jnp.zeros((16, 128), F32)
    fx[0:16] = nothing
    fz[0:16] = nothing
    for side in (0, 1):
        es[side, 0:16] = nothing
        es[side, (cells + 1) * 16 : (cells + 2) * 16] = nothing
    for ref in (us, ks, ns):
        ref[0:16] = nothing
        ref[(cells + 1) * 16 : (cells + 2) * 16] = nothing

    def at(ref, row, by=0):
        return ref[pl.ds(row + by, 8), :]

    def ahead(ref, row, here):
        return pltpu.roll(jnp.where(at_start, at(ref, row, 4), here), 127, 1)

    def behind(ref, row, here):
        return pltpu.roll(jnp.where(at_end, at(ref, row, -4), here), 1, 1)

    def up(here):
        return pltpu.roll(here, 7, 0)

    def down(here):
        return pltpu.roll(here, 1, 0)

    def first_pass(c):
        def step(i, carry):
            start = (c * rows + i * GROUP + 1) * 16
            kk, uu, kx = {}, {}, {}

            def center(seen, ref, g, h):
                if (g, h) not in seen:
                    seen[g, h] = at(ref, start + g * 16 + h * 8)
                return seen[g, h]

            for h in (0, 1):
                kx[-1, h] = center(kk, ks, -1, h) + center(kk, ks, 0, h)
            for g in range(GROUP):
                for h in (0, 1):
                    row = start + g * 16 + h * 8
                    k0 = center(kk, ks, g, h)
                    kx[g, h] = k0 + center(kk, ks, g + 1, h)
                    ky, kw = k0 + ahead(ks, row, k0), k0 + behind(ks, row, k0)
                    if h == 0:
                        face_w = jnp.where(y_first, k0, kw)
                        face_y, kw = ky, jnp.where(y_first, 0.0, kw)
                    else:
                        face_y = jnp.where(y_last, k0, ky)
                        face_w, ky = kw, jnp.where(y_last, 0.0, ky)
                    kz, kv = (k0 + up(k0)) * open_up, (k0 + down(k0)) * open_down
                    mid = 24.0 - (((kx[g, h] + kx[g - 1, h]) + (face_y + face_w)) + ((kz + kv) + outer * k0))
                    for ref, value in ((fx, kx[g, h]), (fy, ky), (fw, kw), (fz, kz), (fm, mid)):
                        ref[pl.ds(row, 8), :] = value
                    v = center(uu, us, g, h)
                    out = (kx[g, h] * center(uu, us, g + 1, h) + kx[g - 1, h] * center(uu, us, g - 1, h)) + (kz * up(v) + kv * down(v))
                    out = out + (ky * ahead(us, row, v) + kw * behind(us, row, v)) + mid * v
                    ns[pl.ds(row, 8), :] = out * (-1.0 / 12.0) - at(ns, row)
            return carry

        lax.fori_loop(0, rows // GROUP, step, 0)

    def moments(c):
        def spread(ref, row, plane):
            return jnp.where(first, ref[pl.ds(row + plane, 1), :], ref[pl.ds(row + 4 + plane, 1), :])

        def step(i, carry):
            for g in range(2 * GROUP):
                row = (c * rows + 1) * 16 + (i * 2 * GROUP + g) * 8
                for side, plane in ((0, 0), (1, 3)):
                    es[side, pl.ds(row, 8), :] = of_u * spread(us, row, plane) + of_n * spread(ns, row, plane)
            return carry

        lax.fori_loop(0, rows // GROUP, step, 0)

    def second_pass(c):
        def step(i, carry):
            start = (c * rows + i * GROUP + 1) * 16
            nn, kx = {}, {}

            def center(seen, ref, g, h):
                if (g, h) not in seen:
                    seen[g, h] = at(ref, start + g * 16 + h * 8)
                return seen[g, h]

            for g in range(GROUP):
                for h in (0, 1):
                    row = start + g * 16 + h * 8
                    v = center(nn, ns, g, h)
                    kz = at(fz, row)
                    out = center(kx, fx, g, h) * center(nn, ns, g + 1, h) + center(kx, fx, g - 1, h) * center(nn, ns, g - 1, h)
                    out = out + (kz * up(v) + down(kz) * down(v))
                    out = out + (at(fy, row) * ahead(ns, row, v) + at(fw, row) * behind(ns, row, v)) + at(fm, row) * v
                    final = out * (-1.0 / 12.0) - at(us, row)
                    ds[pl.ds(row - 16, 8), :] = at(ds, row, -16) + c0 * v + c1 * final
                    vs[pl.ds(row - 16, 8), :] = at(vs, row, -16) + c2 * v + c3 * final
            return carry

        lax.fori_loop(0, rows // GROUP, step, 0)

    def place(c, core):
        return lax.rem((1 - 2 * core) * (lax.rem(c, 4) - my_y) + 8, 4), lax.rem(c // 4 + my_z, 2)

    def stores(c, core, same, far):
        turn, _ = place(c, core)
        here = pl.ds((c * rows + core * half_rows) * 16, half_rows * 16)
        to = ((far_other, far_same) if far else (near_other, near_same))[same]
        return [pltpu.make_async_copy(a.at[here], to.at[turn, i], out_sem.at[i, core, c]) for i, a in enumerate((ds, vs))]

    def edge_stores(c, core, same, is_end):
        turn, side = place(c, core)
        here = pl.ds((c * rows + core * half_rows) * 16, (half_rows + 2) * 16)
        to = ((ends_other, ends_same) if is_end else (rest_other, rest_same))[same]
        return [pltpu.make_async_copy(es.at[i, here], to.at[lax.rem(turn, 2), side, i], edge_sem.at[i, core, c]) for i in (0, 1)]

    def send(copies, c, core, test):
        for same in (0, 1):
            for kind in (0, 1):
                @pl.when(((my_core == core) == (same == 1)) & (test(*place(c, core)) == (kind == 1)))
                def _():
                    for copy in copies(c, core, same, kind):
                        copy.start()

    def send_edges(c, core):
        send(edge_stores, c, core, lambda turn, side: turn >= 2)

    def send_series(c, core):
        send(stores, c, core, lambda turn, side: side == 1)

    def chunk(c, carry):
        @pl.when(c < CHIPS)
        def _():
            @pl.when(c == 0)
            def _():
                for copy in loads(c, (0, 1, 2)):
                    copy.wait()

            @pl.when(c + 1 < CHIPS)
            def _():
                for copy in loads(c + 1, (0, 1, 2)):
                    copy.wait()

            first_pass(c)
            moments(c)
            send_edges(c, 0)

        @pl.when(c > 0)
        def _():
            send_edges(c - 1, 1)
            for copy in loads(c - 1, (3, 4)):
                copy.wait()
            second_pass(c - 1)
            for core in (0, 1):
                send_series(c - 1, core)

        return carry

    lax.fori_loop(0, CHIPS + 1, chunk, 0)

    def end(c, carry):
        for core in (0, 1):
            for copy in stores(c, core, 1, 1) + edge_stores(c, core, 1, 1):
                copy.wait()
        return carry

    lax.fori_loop(0, CHIPS, end, 0)


def mend_kernel(d, v, low, high, below, above, k, k_low, k_high, d_out, v_out, ds, vs):
    rows = d.shape[0]
    slab = lax.axis_index("gz")
    lower, upper = jnp.where(slab == 0, 1.0, 0.0), jnp.where(slab == SLABS - 1, 1.0, 0.0)
    wide = rows + 2
    z = places(wide)[1]
    factor = []
    for h in (0, 1):
        under = (1.0 - lower) * (k[:, h] + roll(k_low[:, h], -3))
        over = (1.0 - upper) * (k[:, h] + roll(k_high[:, h], 3))
        factor.append(jnp.where(z == 0, under, jnp.where(z == 3, -over, 0.0)) * (1.0 / 12.0))
    from_low = [low[:, h] - below[:, h] for h in (0, 1)]
    from_high = [above[:, h] - high[:, h] for h in (0, 1)]
    direct = []
    for field, slot in ((ds, 0), (vs, 2)):
        for h in (0, 1):
            a = jnp.where(z == 0, roll(from_low[h], -slot), roll(from_high[h], 3 - slot))
            b = jnp.where(z == 0, roll(from_low[h], -slot - 1), roll(from_high[h], 2 - slot))
            w = factor[h] * a
            field[:, h] = w
            direct.append((factor[h] * b + 2.0 * jnp.abs(factor[h]) * w)[1 : rows + 1])
    for field, given, out, direct_of in ((ds, d, d_out, direct[:2]), (vs, v, v_out, direct[2:])):
        w, outflow = spread(field, k, 0, rows, lower, upper)
        for h in (0, 1):
            out[:, h] = given[:, h] + direct_of[h] - outflow[h] * (1.0 / 12.0) - 2.0 * w[h]


ANYWHERE = pl.BlockSpec(memory_space=pl.ANY)
SMEM = pl.BlockSpec(memory_space=pltpu.SMEM)


def params(mib):
    return pltpu.CompilerParams(vmem_limit_bytes=mib * MIB)


def cost(mib):
    return pl.CostEstimate(flops=0, bytes_accessed=mib * MIB, transcendentals=0)


def flat(cells):
    return cells.reshape(-1, 128)


def series(coeffs, u, k, p, cos, sin):
    cells = u.shape[0] // 16
    share = jax.ShapeDtypeStruct((4, 2, cells // COUNT * 16, 128), F32)
    edge = jax.ShapeDtypeStruct((2, 2, 2, (cells // COUNT + 2) * 16, 128), F32)
    wide = pltpu.VMEM(((cells + 2) * 16, 128), F32)
    exact = pltpu.VMEM((cells * 16, 128), F32)
    return pl.pallas_call(
        series_kernel,
        out_shape=(share,) * 4 + (edge,) * 4,
        in_specs=[SMEM] + [ANYWHERE] * 5,
        out_specs=(ANYWHERE,) * 8,
        scratch_shapes=[wide, wide, wide, exact, exact, wide, wide, wide, wide, wide]
        + [
            pltpu.VMEM((2, (cells + 2) * 16, 128), F32),
            pltpu.SemaphoreType.DMA((5, CHIPS)),
            pltpu.SemaphoreType.DMA((2, 2, CHIPS)),
            pltpu.SemaphoreType.DMA((2, 2, CHIPS)),
        ],
        compiler_params=params(56),
        cost_estimate=cost(45),
    )(coeffs, u, k, p, cos, sin)


def mend(d, v, low, high, below, above, k, k_low, k_high):
    shape = jax.ShapeDtypeStruct(d.shape, F32)
    whole = pl.BlockSpec(memory_space=pltpu.VMEM)
    return pl.pallas_call(
        mend_kernel,
        out_shape=(shape, shape),
        in_specs=[whole] * 9,
        out_specs=(whole, whole),
        scratch_shapes=[pltpu.VMEM(k.shape, F32)] * 2,
        compiler_params=params(16),
        cost_estimate=cost(4),
    )(d, v, low, high, below, above, k, k_low, k_high)


CELL = (2, 8, 128)


def along_y(sign):
    def goal(i):
        z, y, core = i // 8, (i // 2) % 4, i % 2
        return z * 8 + ((y + sign * (1 - 2 * core)) % 4) * 2 + core

    return [(i, goal(i)) for i in range(COUNT)]


FORTH, BACK = along_y(1), along_y(-1)
ACROSS = [(i, i ^ 8) for i in range(COUNT)]
SIBLING = [(i, i ^ 1) for i in range(COUNT)]
UP = [(i, i + 1) for i in range(SLABS - 1)]
DOWN = [(i + 1, i) for i in range(SLABS - 1)]


def to_sibling(other):
    return lax.ppermute(other, "tm", SIBLING)


def forth(cells):
    return lax.ppermute(cells, "tm", FORTH)


def back(cells):
    return lax.ppermute(cells, "tm", BACK)


def across(cells):
    return lax.ppermute(cells, "tm", ACROSS)


def after(first, then):
    return lax.optimization_barrier((first, then))[1]


def local(prev_term, last_term, cos_sum, sin_sum, speed_sq, series_coeffs):
    u, p, k = flat(packed(last_term[0])), flat(packed(prev_term[0])), flat(packed(speed_sq))
    cos, sin = flat(packed(cos_sum[0])), flat(packed(sin_sum[0]))
    rows = last_term.shape[1] // COUNT
    me = lax.axis_index("tm")

    outs = series(series_coeffs, u, k, p, cos, sin)
    far_other, far_same, near_other, near_same, ends_other, ends_same, rest_other, rest_same = outs

    ends_came, far_came = to_sibling(ends_other), to_sibling(far_other)
    rest_came, near_came = to_sibling(rest_other), to_sibling(near_other)
    ends_two = forth(ends_same[0] + ends_came[0])
    far_ends = far_same[2:] + far_came[2:]
    ends_came = after(far_ends, ends_came)
    far_ends_came, far_rest_came = across(far_ends), across(far_same[:2] + far_came[:2])
    ends_back = back(ends_same[1] + ends_came[1])

    start = me * rows * 16
    k_here = jnp.concatenate(
        [
            jnp.where(me > 0, lax.dynamic_slice_in_dim(k, jnp.maximum(start - 16, 0), 16), 0.0),
            lax.dynamic_slice_in_dim(k, start, rows * 16),
            jnp.where(me < COUNT - 1, lax.dynamic_slice_in_dim(k, jnp.minimum(start + rows * 16, k.shape[0] - 16), 16), 0.0),
        ]
    )
    k_low, k_high = lax.ppermute(k_here, "gz", UP), lax.ppermute(k_here, "gz", DOWN)

    ring = forth(rest_same[1] + rest_came[1] + ends_two)
    two, direct = (near_same[t] + near_came[t] + far_ends_came[t - 2] for t in (2, 3))
    ring = after((two, direct, k_low, k_high), ring)
    two, direct = forth(two), back(direct)
    edge_far = rest_same[0, 1] + rest_came[0, 1] + ends_back[1] + ring[1]
    edge = rest_same[0, 0] + rest_came[0, 0] + ends_back[0] + ring[0]
    far_rest_came = after(edge_far, far_rest_came)
    edge_came = across(edge_far)
    last = near_same[1] + near_came[1] + far_rest_came[1] + two
    edge_came = after((last, edge), edge_came)
    last = forth(last)
    low, high = edge[0] + edge_came[0], edge[1] + edge_came[1]
    above, below = lax.ppermute(low, "gz", DOWN), lax.ppermute(high, "gz", UP)
    result = near_same[0] + near_came[0] + far_rest_came[0] + direct + last
    d, v = result[0], result[1]

    wide = (a.reshape(rows + 2, *CELL) for a in (low, high, below, above, k_here, k_low, k_high))
    d, v = mend(d.reshape(rows, *CELL), v.reshape(rows, *CELL), *wide)
    return unpacked(d), unpacked(v)


def solution(mesh):
    return jax.shard_map(
        local,
        mesh=mesh,
        in_specs=(
            P("tm", None, "gz", None),
            P("tm", None, "gz", None),
            P("tm", None, "gz", None),
            P("tm", None, "gz", None),
            P(None, "gz", None),
            P("tm", None),
        ),
        out_specs=(P("tm", "gz", None), P("tm", "gz", None)),
        check_vma=False,
    )
```

```python
import jax
import jax.numpy as jnp
from jax import lax
from jax.experimental import pallas as pl
from jax.experimental.pallas import tpu as pltpu
from jax.sharding import PartitionSpec as P

CHIPS = 8
COUNT = 16
SLABS = 8
GROUP = 16
MIB = 1024 * 1024
F32 = jnp.float32


def packed(cells):
    x = cells.shape[0]
    return cells.reshape(x, 4, 4, 128).transpose(0, 2, 1, 3).reshape(x, 2, 8, 128)


def unpacked(cells):
    x = cells.shape[0]
    return cells.reshape(x, 4, 4, 128).transpose(0, 2, 1, 3).reshape(x, 4, 512)


def roll(cells, shift):
    return pltpu.roll(cells, shift % 8, 1)


def places(n):
    sub = lax.broadcasted_iota(jnp.int32, (n, 8, 128), 1)
    return sub, lax.rem(sub, 4), lax.broadcasted_iota(jnp.int32, (n, 8, 128), 2)


def spread(field, speed, row, n, lower, upper):
    sub, z, lane = places(n)
    first, at_start, at_end = sub < 4, lane == 0, lane == 127
    v = [field[pl.ds(row + 1, n), h] for h in (0, 1)]
    k = [speed[pl.ds(row + 1, n), h] for h in (0, 1)]

    def ahead(a, b):
        ra, rb = pltpu.roll(a, 127, 2), pltpu.roll(b, 127, 2)
        qa, qb = roll(ra, 4), roll(rb, 4)
        return (
            jnp.where(at_end, jnp.where(first, qa, qb), ra),
            jnp.where(at_end, jnp.where(first, qb, 0.0), rb),
        )

    def behind(a, b, edge):
        ra, rb = pltpu.roll(a, 1, 2), pltpu.roll(b, 1, 2)
        qa, qb = roll(ra, 4), roll(rb, 4)
        return (
            jnp.where(at_start, jnp.where(first, edge, qa), ra),
            jnp.where(at_start, jnp.where(first, qa, qb), rb),
        )

    v_y, k_y = ahead(*v), ahead(*k)
    f_y = [(k[h] + k_y[h]) * (v_y[h] - v[h]) for h in (0, 1)]
    b_y = behind(*f_y, k[0] * v[0])
    out = []
    for h in (0, 1):
        kv = k[h] * v[h]
        f_z = jnp.where(z == 3, -upper * kv, (k[h] + roll(k[h], -1)) * (roll(v[h], -1) - v[h]))
        b_z = jnp.where(z == 0, lower * kv, roll(f_z, 1))
        f_x = (k[h] + speed[pl.ds(row + 2, n), h]) * (field[pl.ds(row + 2, n), h] - v[h])
        b_x = (k[h] + speed[pl.ds(row, n), h]) * (v[h] - field[pl.ds(row, n), h])
        out.append((f_x - b_x) + (f_y[h] - b_y[h]) + (f_z - b_z))
    return v, out


def widen(scratch, main, before, after, block, blocks):
    rows = main.shape[0]
    scratch[pl.ds(1, rows)] = main[...]
    scratch[pl.ds(0, 1)] = jnp.where(block > 0, before[...], 0.0)
    scratch[pl.ds(rows + 1, 1)] = jnp.where(block < blocks - 1, after[...], 0.0)


def where_am_i():
    me = lax.axis_index("tm")
    return me // 8, lax.rem(me // 2, 4), lax.rem(me, 2)


def series_kernel(coeffs, u, k, p, cos, sin, far_other, far_same, near_other, near_same, ends_other, ends_same, rest_other, rest_same,
                  us, ks, ns, ds, vs, fx, fy, fw, fz, fm, es, in_sem, out_sem, edge_sem):
    cells = u.shape[0] // 16
    rows = cells // CHIPS
    half_rows = rows // 2
    my_z, my_y, my_core = where_am_i()
    slab = lax.axis_index("gz")
    lower, upper = jnp.where(slab == 0, 1.0, 0.0), jnp.where(slab == SLABS - 1, 1.0, 0.0)
    c0, c1, c2, c3 = (coeffs[0, i] for i in range(4))
    sub = lax.broadcasted_iota(jnp.int32, (8, 128), 0)
    lane = lax.broadcasted_iota(jnp.int32, (8, 128), 1)
    z = lax.rem(sub, 4)
    first, at_start, at_end = sub < 4, lane == 0, lane == 127
    open_up, open_down = jnp.where(z == 3, 0.0, 1.0), jnp.where(z == 0, 0.0, 1.0)
    of_u = jnp.where(z == 0, c1, jnp.where(z == 1, c0, jnp.where(z == 2, c3, c2)))
    of_n = jnp.where(z == 1, c1, jnp.where(z == 3, c3, 0.0))
    y_first, y_last = jnp.logical_and(first, at_start), jnp.logical_and(jnp.logical_not(first), at_end)
    outer = jnp.where(z == 0, lower, 0.0) + jnp.where(z == 3, upper, 0.0)

    def arrays():
        return ((u, us, 16), (k, ks, 16), (p, ns, 16), (cos, ds, 0), (sin, vs, 0))

    def loads(c, which):
        return [
            pltpu.make_async_copy(a.at[pl.ds(c * rows * 16, rows * 16)], b.at[pl.ds(c * rows * 16 + off, rows * 16)], in_sem.at[i, c])
            for i, (a, b, off) in enumerate(arrays()) if i in which
        ]

    for c in range(CHIPS):
        for copy in loads(c, (0, 1, 2)):
            copy.start()
        if c:
            for copy in loads(c - 1, (3, 4)):
                copy.start()
    for copy in loads(CHIPS - 1, (3, 4)):
        copy.start()
    nothing = jnp.zeros((16, 128), F32)
    fx[0:16] = nothing
    fz[0:16] = nothing
    for side in (0, 1):
        es[side, 0:16] = nothing
        es[side, (cells + 1) * 16 : (cells + 2) * 16] = nothing
    for ref in (us, ks, ns):
        ref[0:16] = nothing
        ref[(cells + 1) * 16 : (cells + 2) * 16] = nothing

    def at(ref, row, by=0):
        return ref[pl.ds(row + by, 8), :]

    def ahead(ref, row, here):
        return pltpu.roll(jnp.where(at_start, at(ref, row, 4), here), 127, 1)

    def behind(ref, row, here):
        return pltpu.roll(jnp.where(at_end, at(ref, row, -4), here), 1, 1)

    def up(here):
        return pltpu.roll(here, 7, 0)

    def down(here):
        return pltpu.roll(here, 1, 0)

    def first_pass(c):
        def step(i, carry):
            start = (c * rows + i * GROUP + 1) * 16
            kk, uu, kx = {}, {}, {}

            def center(seen, ref, g, h):
                if (g, h) not in seen:
                    seen[g, h] = at(ref, start + g * 16 + h * 8)
                return seen[g, h]

            for h in (0, 1):
                kx[-1, h] = center(kk, ks, -1, h) + center(kk, ks, 0, h)
            for g in range(GROUP):
                for h in (0, 1):
                    row = start + g * 16 + h * 8
                    k0 = center(kk, ks, g, h)
                    kx[g, h] = k0 + center(kk, ks, g + 1, h)
                    ky, kw = k0 + ahead(ks, row, k0), k0 + behind(ks, row, k0)
                    if h == 0:
                        face_w = jnp.where(y_first, k0, kw)
                        face_y, kw = ky, jnp.where(y_first, 0.0, kw)
                    else:
                        face_y = jnp.where(y_last, k0, ky)
                        face_w, ky = kw, jnp.where(y_last, 0.0, ky)
                    kz, kv = (k0 + up(k0)) * open_up, (k0 + down(k0)) * open_down
                    mid = 24.0 - (((kx[g, h] + kx[g - 1, h]) + (face_y + face_w)) + ((kz + kv) + outer * k0))
                    for ref, value in ((fx, kx[g, h]), (fy, ky), (fw, kw), (fz, kz), (fm, mid)):
                        ref[pl.ds(row, 8), :] = value
                    v = center(uu, us, g, h)
                    out = (kx[g, h] * center(uu, us, g + 1, h) + kx[g - 1, h] * center(uu, us, g - 1, h)) + (kz * up(v) + kv * down(v))
                    out = out + (ky * ahead(us, row, v) + kw * behind(us, row, v)) + mid * v
                    ns[pl.ds(row, 8), :] = out * (-1.0 / 12.0) - at(ns, row)
            return carry

        lax.fori_loop(0, rows // GROUP, step, 0)

    def moments(c):
        def spread(ref, row, plane):
            return jnp.where(first, ref[pl.ds(row + plane, 1), :], ref[pl.ds(row + 4 + plane, 1), :])

        def step(i, carry):
            for g in range(2 * GROUP):
                row = (c * rows + 1) * 16 + (i * 2 * GROUP + g) * 8
                for side, plane in ((0, 0), (1, 3)):
                    es[side, pl.ds(row, 8), :] = of_u * spread(us, row, plane) + of_n * spread(ns, row, plane)
            return carry

        lax.fori_loop(0, rows // GROUP, step, 0)

    def second_pass(c):
        def step(i, carry):
            start = (c * rows + i * GROUP + 1) * 16
            nn, kx = {}, {}

            def center(seen, ref, g, h):
                if (g, h) not in seen:
                    seen[g, h] = at(ref, start + g * 16 + h * 8)
                return seen[g, h]

            for g in range(GROUP):
                for h in (0, 1):
                    row = start + g * 16 + h * 8
                    v = center(nn, ns, g, h)
                    kz = at(fz, row)
                    out = center(kx, fx, g, h) * center(nn, ns, g + 1, h) + center(kx, fx, g - 1, h) * center(nn, ns, g - 1, h)
                    out = out + (kz * up(v) + down(kz) * down(v))
                    out = out + (at(fy, row) * ahead(ns, row, v) + at(fw, row) * behind(ns, row, v)) + at(fm, row) * v
                    final = out * (-1.0 / 12.0) - at(us, row)
                    ds[pl.ds(row - 16, 8), :] = at(ds, row, -16) + c0 * v + c1 * final
                    vs[pl.ds(row - 16, 8), :] = at(vs, row, -16) + c2 * v + c3 * final
            return carry

        lax.fori_loop(0, rows // GROUP, step, 0)

    def place(c, core):
        return lax.rem((1 - 2 * core) * (lax.rem(c, 4) - my_y) + 8, 4), lax.rem(c // 4 + my_z, 2)

    def stores(c, core, same, far):
        turn, _ = place(c, core)
        here = pl.ds((c * rows + core * half_rows) * 16, half_rows * 16)
        to = ((far_other, far_same) if far else (near_other, near_same))[same]
        return [pltpu.make_async_copy(a.at[here], to.at[turn, i], out_sem.at[i, core, c]) for i, a in enumerate((ds, vs))]

    def edge_stores(c, core, same, is_end):
        turn, side = place(c, core)
        here = pl.ds((c * rows + core * half_rows) * 16, (half_rows + 2) * 16)
        to = ((ends_other, ends_same) if is_end else (rest_other, rest_same))[same]
        return [pltpu.make_async_copy(es.at[i, here], to.at[lax.rem(turn, 2), side, i], edge_sem.at[i, core, c]) for i in (0, 1)]

    def send(copies, c, core, test):
        for same in (0, 1):
            for kind in (0, 1):
                @pl.when(((my_core == core) == (same == 1)) & (test(*place(c, core)) == (kind == 1)))
                def _():
                    for copy in copies(c, core, same, kind):
                        copy.start()

    def send_edges(c, core):
        send(edge_stores, c, core, lambda turn, side: turn >= 2)

    def send_series(c, core):
        send(stores, c, core, lambda turn, side: side == 1)

    def chunk(c, carry):
        @pl.when(c < CHIPS)
        def _():
            @pl.when(c == 0)
            def _():
                for copy in loads(c, (0, 1, 2)):
                    copy.wait()

            @pl.when(c + 1 < CHIPS)
            def _():
                for copy in loads(c + 1, (0, 1, 2)):
                    copy.wait()

            first_pass(c)
            moments(c)
            send_edges(c, 0)

        @pl.when(c > 0)
        def _():
            send_edges(c - 1, 1)
            for copy in loads(c - 1, (3, 4)):
                copy.wait()
            second_pass(c - 1)
            for core in (0, 1):
                send_series(c - 1, core)

        return carry

    lax.fori_loop(0, CHIPS + 1, chunk, 0)

    def end(c, carry):
        for core in (0, 1):
            for copy in stores(c, core, 1, 1) + edge_stores(c, core, 1, 1):
                copy.wait()
        return carry

    lax.fori_loop(0, CHIPS, end, 0)


def mend_kernel(d, v, low, high, below, above, k, k_low, k_high, d_out, v_out, ds, vs):
    rows = d.shape[0]
    slab = lax.axis_index("gz")
    lower, upper = jnp.where(slab == 0, 1.0, 0.0), jnp.where(slab == SLABS - 1, 1.0, 0.0)
    wide = rows + 2
    z = places(wide)[1]
    factor = []
    for h in (0, 1):
        under = (1.0 - lower) * (k[:, h] + roll(k_low[:, h], -3))
        over = (1.0 - upper) * (k[:, h] + roll(k_high[:, h], 3))
        factor.append(jnp.where(z == 0, under, jnp.where(z == 3, -over, 0.0)) * (1.0 / 12.0))
    from_low = [low[:, h] - below[:, h] for h in (0, 1)]
    from_high = [above[:, h] - high[:, h] for h in (0, 1)]
    direct = []
    for field, slot in ((ds, 0), (vs, 2)):
        for h in (0, 1):
            a = jnp.where(z == 0, roll(from_low[h], -slot), roll(from_high[h], 3 - slot))
            b = jnp.where(z == 0, roll(from_low[h], -slot - 1), roll(from_high[h], 2 - slot))
            w = factor[h] * a
            field[:, h] = w
            direct.append((factor[h] * b + 2.0 * jnp.abs(factor[h]) * w)[1 : rows + 1])
    for field, given, out, direct_of in ((ds, d, d_out, direct[:2]), (vs, v, v_out, direct[2:])):
        w, outflow = spread(field, k, 0, rows, lower, upper)
        for h in (0, 1):
            out[:, h] = given[:, h] + direct_of[h] - outflow[h] * (1.0 / 12.0) - 2.0 * w[h]


ANYWHERE = pl.BlockSpec(memory_space=pl.ANY)
SMEM = pl.BlockSpec(memory_space=pltpu.SMEM)


def params(mib):
    return pltpu.CompilerParams(vmem_limit_bytes=mib * MIB)


def cost(mib):
    return pl.CostEstimate(flops=0, bytes_accessed=mib * MIB, transcendentals=0)


def flat(cells):
    return cells.reshape(-1, 128)


def series(coeffs, u, k, p, cos, sin):
    cells = u.shape[0] // 16
    share = jax.ShapeDtypeStruct((4, 2, cells // COUNT * 16, 128), F32)
    edge = jax.ShapeDtypeStruct((2, 2, 2, (cells // COUNT + 2) * 16, 128), F32)
    wide = pltpu.VMEM(((cells + 2) * 16, 128), F32)
    exact = pltpu.VMEM((cells * 16, 128), F32)
    return pl.pallas_call(
        series_kernel,
        out_shape=(share,) * 4 + (edge,) * 4,
        in_specs=[SMEM] + [ANYWHERE] * 5,
        out_specs=(ANYWHERE,) * 8,
        scratch_shapes=[wide, wide, wide, exact, exact, wide, wide, wide, wide, wide]
        + [
            pltpu.VMEM((2, (cells + 2) * 16, 128), F32),
            pltpu.SemaphoreType.DMA((5, CHIPS)),
            pltpu.SemaphoreType.DMA((2, 2, CHIPS)),
            pltpu.SemaphoreType.DMA((2, 2, CHIPS)),
        ],
        compiler_params=params(56),
        cost_estimate=cost(45),
    )(coeffs, u, k, p, cos, sin)


def mend(d, v, low, high, below, above, k, k_low, k_high):
    shape = jax.ShapeDtypeStruct(d.shape, F32)
    whole = pl.BlockSpec(memory_space=pltpu.VMEM)
    return pl.pallas_call(
        mend_kernel,
        out_shape=(shape, shape),
        in_specs=[whole] * 9,
        out_specs=(whole, whole),
        scratch_shapes=[pltpu.VMEM(k.shape, F32)] * 2,
        compiler_params=params(16),
        cost_estimate=cost(4),
    )(d, v, low, high, below, above, k, k_low, k_high)


CELL = (2, 8, 128)


def along_y(sign):
    def goal(i):
        z, y, core = i // 8, (i // 2) % 4, i % 2
        return z * 8 + ((y + sign * (1 - 2 * core)) % 4) * 2 + core

    return [(i, goal(i)) for i in range(COUNT)]


FORTH, BACK = along_y(1), along_y(-1)
ACROSS = [(i, i ^ 8) for i in range(COUNT)]
SIBLING = [(i, i ^ 1) for i in range(COUNT)]
UP = [(i, i + 1) for i in range(SLABS - 1)]
DOWN = [(i + 1, i) for i in range(SLABS - 1)]


def to_sibling(other):
    return lax.ppermute(other, "tm", SIBLING)


def forth(cells):
    return lax.ppermute(cells, "tm", FORTH)


def back(cells):
    return lax.ppermute(cells, "tm", BACK)


def across(cells):
    return lax.ppermute(cells, "tm", ACROSS)


def after(first, then):
    return lax.optimization_barrier((first, then))[1]


def local(prev_term, last_term, cos_sum, sin_sum, speed_sq, series_coeffs):
    u, p, k = flat(packed(last_term[0])), flat(packed(prev_term[0])), flat(packed(speed_sq))
    cos, sin = flat(packed(cos_sum[0])), flat(packed(sin_sum[0]))
    rows = last_term.shape[1] // COUNT
    me = lax.axis_index("tm")

    outs = series(series_coeffs, u, k, p, cos, sin)
    far_other, far_same, near_other, near_same, ends_other, ends_same, rest_other, rest_same = outs

    ends_came, far_came = to_sibling(ends_other), to_sibling(far_other)
    rest_came = to_sibling(rest_other)
    ends_two = ends_same[0] + ends_came[0]
    near_came = to_sibling(after(ends_two, near_other))
    ends_two = forth(ends_two)
    far_ends = far_same[2:] + far_came[2:]
    ends_came = after(far_ends, ends_came)
    far_ends_came, far_rest_came = across(far_ends), across(far_same[:2] + far_came[:2])
    ends_back = back(ends_same[1] + ends_came[1])

    start = me * rows * 16
    k_here = jnp.concatenate(
        [
            jnp.where(me > 0, lax.dynamic_slice_in_dim(k, jnp.maximum(start - 16, 0), 16), 0.0),
            lax.dynamic_slice_in_dim(k, start, rows * 16),
            jnp.where(me < COUNT - 1, lax.dynamic_slice_in_dim(k, jnp.minimum(start + rows * 16, k.shape[0] - 16), 16), 0.0),
        ]
    )
    k_low, k_high = lax.ppermute(k_here, "gz", UP), lax.ppermute(k_here, "gz", DOWN)

    ring = forth(rest_same[1] + rest_came[1] + ends_two)
    two, direct = (near_same[t] + near_came[t] + far_ends_came[t - 2] for t in (2, 3))
    ring = after((two, direct, k_low, k_high), ring)
    two, direct = forth(two), back(direct)
    edge_far = rest_same[0, 1] + rest_came[0, 1] + ends_back[1] + ring[1]
    edge = rest_same[0, 0] + rest_came[0, 0] + ends_back[0] + ring[0]
    far_rest_came = after(edge_far, far_rest_came)
    edge_came = across(edge_far)
    last = near_same[1] + near_came[1] + far_rest_came[1] + two
    edge_came = after((last, edge), edge_came)
    last = forth(last)
    low, high = edge[0] + edge_came[0], edge[1] + edge_came[1]
    above, below = lax.ppermute(low, "gz", DOWN), lax.ppermute(high, "gz", UP)
    result = near_same[0] + near_came[0] + far_rest_came[0] + direct + last
    d, v = result[0], result[1]

    wide = (a.reshape(rows + 2, *CELL) for a in (low, high, below, above, k_here, k_low, k_high))
    d, v = mend(d.reshape(rows, *CELL), v.reshape(rows, *CELL), *wide)
    return unpacked(d), unpacked(v)


def solution(mesh):
    return jax.shard_map(
        local,
        mesh=mesh,
        in_specs=(
            P("tm", None, "gz", None),
            P("tm", None, "gz", None),
            P("tm", None, "gz", None),
            P("tm", None, "gz", None),
            P(None, "gz", None),
            P("tm", None),
        ),
        out_specs=(P("tm", "gz", None), P("tm", "gz", None)),
        check_vma=False,
    )
```

```python
import jax
import jax.numpy as jnp
from jax import lax
from jax.experimental import pallas as pl
from jax.experimental.pallas import tpu as pltpu
from jax.sharding import PartitionSpec as P

CHIPS = 8
COUNT = 16
SLABS = 8
GROUP = 16
MIB = 1024 * 1024
F32 = jnp.float32


def packed(cells):
    x = cells.shape[0]
    return cells.reshape(x, 4, 4, 128).transpose(0, 2, 1, 3).reshape(x, 2, 8, 128)


def unpacked(cells):
    x = cells.shape[0]
    return cells.reshape(x, 4, 4, 128).transpose(0, 2, 1, 3).reshape(x, 4, 512)


def roll(cells, shift):
    return pltpu.roll(cells, shift % 8, 1)


def places(n):
    sub = lax.broadcasted_iota(jnp.int32, (n, 8, 128), 1)
    return sub, lax.rem(sub, 4), lax.broadcasted_iota(jnp.int32, (n, 8, 128), 2)


def spread(field, speed, row, n, lower, upper):
    sub, z, lane = places(n)
    first, at_start, at_end = sub < 4, lane == 0, lane == 127
    v = [field[pl.ds(row + 1, n), h] for h in (0, 1)]
    k = [speed[pl.ds(row + 1, n), h] for h in (0, 1)]

    def ahead(a, b):
        ra, rb = pltpu.roll(a, 127, 2), pltpu.roll(b, 127, 2)
        qa, qb = roll(ra, 4), roll(rb, 4)
        return (
            jnp.where(at_end, jnp.where(first, qa, qb), ra),
            jnp.where(at_end, jnp.where(first, qb, 0.0), rb),
        )

    def behind(a, b, edge):
        ra, rb = pltpu.roll(a, 1, 2), pltpu.roll(b, 1, 2)
        qa, qb = roll(ra, 4), roll(rb, 4)
        return (
            jnp.where(at_start, jnp.where(first, edge, qa), ra),
            jnp.where(at_start, jnp.where(first, qa, qb), rb),
        )

    v_y, k_y = ahead(*v), ahead(*k)
    f_y = [(k[h] + k_y[h]) * (v_y[h] - v[h]) for h in (0, 1)]
    b_y = behind(*f_y, k[0] * v[0])
    out = []
    for h in (0, 1):
        kv = k[h] * v[h]
        f_z = jnp.where(z == 3, -upper * kv, (k[h] + roll(k[h], -1)) * (roll(v[h], -1) - v[h]))
        b_z = jnp.where(z == 0, lower * kv, roll(f_z, 1))
        f_x = (k[h] + speed[pl.ds(row + 2, n), h]) * (field[pl.ds(row + 2, n), h] - v[h])
        b_x = (k[h] + speed[pl.ds(row, n), h]) * (v[h] - field[pl.ds(row, n), h])
        out.append((f_x - b_x) + (f_y[h] - b_y[h]) + (f_z - b_z))
    return v, out


def widen(scratch, main, before, after, block, blocks):
    rows = main.shape[0]
    scratch[pl.ds(1, rows)] = main[...]
    scratch[pl.ds(0, 1)] = jnp.where(block > 0, before[...], 0.0)
    scratch[pl.ds(rows + 1, 1)] = jnp.where(block < blocks - 1, after[...], 0.0)


def where_am_i():
    me = lax.axis_index("tm")
    return me // 8, lax.rem(me // 2, 4), lax.rem(me, 2)


def series_kernel(coeffs, u, k, p, cos, sin, far_other, far_same, near_other, near_same, ends_other, ends_same, rest_other, rest_same,
                  us, ks, ns, ds, vs, fx, fy, fw, fz, fm, es, in_sem, out_sem, edge_sem):
    cells = u.shape[0] // 16
    rows = cells // CHIPS
    half_rows = rows // 2
    my_z, my_y, my_core = where_am_i()
    slab = lax.axis_index("gz")
    lower, upper = jnp.where(slab == 0, 1.0, 0.0), jnp.where(slab == SLABS - 1, 1.0, 0.0)
    c0, c1, c2, c3 = (coeffs[0, i] for i in range(4))
    sub = lax.broadcasted_iota(jnp.int32, (8, 128), 0)
    lane = lax.broadcasted_iota(jnp.int32, (8, 128), 1)
    z = lax.rem(sub, 4)
    first, at_start, at_end = sub < 4, lane == 0, lane == 127
    open_up, open_down = jnp.where(z == 3, 0.0, 1.0), jnp.where(z == 0, 0.0, 1.0)
    of_u = jnp.where(z == 0, c1, jnp.where(z == 1, c0, jnp.where(z == 2, c3, c2)))
    of_n = jnp.where(z == 1, c1, jnp.where(z == 3, c3, 0.0))
    y_first, y_last = jnp.logical_and(first, at_start), jnp.logical_and(jnp.logical_not(first), at_end)
    outer = jnp.where(z == 0, lower, 0.0) + jnp.where(z == 3, upper, 0.0)

    def arrays():
        return ((u, us, 16), (k, ks, 16), (p, ns, 16), (cos, ds, 0), (sin, vs, 0))

    def loads(c, which):
        return [
            pltpu.make_async_copy(a.at[pl.ds(c * rows * 16, rows * 16)], b.at[pl.ds(c * rows * 16 + off, rows * 16)], in_sem.at[i, c])
            for i, (a, b, off) in enumerate(arrays()) if i in which
        ]

    for c in range(CHIPS):
        for copy in loads(c, (0, 1, 2)):
            copy.start()
        if c:
            for copy in loads(c - 1, (3, 4)):
                copy.start()
    for copy in loads(CHIPS - 1, (3, 4)):
        copy.start()
    nothing = jnp.zeros((16, 128), F32)
    fx[0:16] = nothing
    fz[0:16] = nothing
    for side in (0, 1):
        es[side, 0:16] = nothing
        es[side, (cells + 1) * 16 : (cells + 2) * 16] = nothing
    for ref in (us, ks, ns):
        ref[0:16] = nothing
        ref[(cells + 1) * 16 : (cells + 2) * 16] = nothing

    def at(ref, row, by=0):
        return ref[pl.ds(row + by, 8), :]

    def ahead(ref, row, here):
        return pltpu.roll(jnp.where(at_start, at(ref, row, 4), here), 127, 1)

    def behind(ref, row, here):
        return pltpu.roll(jnp.where(at_end, at(ref, row, -4), here), 1, 1)

    def up(here):
        return pltpu.roll(here, 7, 0)

    def down(here):
        return pltpu.roll(here, 1, 0)

    def first_pass(c):
        def step(i, carry):
            start = (c * rows + i * GROUP + 1) * 16
            kk, uu, kx = {}, {}, {}

            def center(seen, ref, g, h):
                if (g, h) not in seen:
                    seen[g, h] = at(ref, start + g * 16 + h * 8)
                return seen[g, h]

            for h in (0, 1):
                kx[-1, h] = center(kk, ks, -1, h) + center(kk, ks, 0, h)
            for g in range(GROUP):
                for h in (0, 1):
                    row = start + g * 16 + h * 8
                    k0 = center(kk, ks, g, h)
                    kx[g, h] = k0 + center(kk, ks, g + 1, h)
                    ky, kw = k0 + ahead(ks, row, k0), k0 + behind(ks, row, k0)
                    if h == 0:
                        face_w = jnp.where(y_first, k0, kw)
                        face_y, kw = ky, jnp.where(y_first, 0.0, kw)
                    else:
                        face_y = jnp.where(y_last, k0, ky)
                        face_w, ky = kw, jnp.where(y_last, 0.0, ky)
                    kz, kv = (k0 + up(k0)) * open_up, (k0 + down(k0)) * open_down
                    mid = 24.0 - (((kx[g, h] + kx[g - 1, h]) + (face_y + face_w)) + ((kz + kv) + outer * k0))
                    for ref, value in ((fx, kx[g, h]), (fy, ky), (fw, kw), (fz, kz), (fm, mid)):
                        ref[pl.ds(row, 8), :] = value
                    v = center(uu, us, g, h)
                    out = (kx[g, h] * center(uu, us, g + 1, h) + kx[g - 1, h] * center(uu, us, g - 1, h)) + (kz * up(v) + kv * down(v))
                    out = out + (ky * ahead(us, row, v) + kw * behind(us, row, v)) + mid * v
                    ns[pl.ds(row, 8), :] = out * (-1.0 / 12.0) - at(ns, row)
            return carry

        lax.fori_loop(0, rows // GROUP, step, 0)

    def moments(c):
        def spread(ref, row, plane):
            return jnp.where(first, ref[pl.ds(row + plane, 1), :], ref[pl.ds(row + 4 + plane, 1), :])

        def step(i, carry):
            for g in range(2 * GROUP):
                row = (c * rows + 1) * 16 + (i * 2 * GROUP + g) * 8
                for side, plane in ((0, 0), (1, 3)):
                    es[side, pl.ds(row, 8), :] = of_u * spread(us, row, plane) + of_n * spread(ns, row, plane)
            return carry

        lax.fori_loop(0, rows // GROUP, step, 0)

    def second_pass(c):
        def step(i, carry):
            start = (c * rows + i * GROUP + 1) * 16
            nn, kx = {}, {}

            def center(seen, ref, g, h):
                if (g, h) not in seen:
                    seen[g, h] = at(ref, start + g * 16 + h * 8)
                return seen[g, h]

            for g in range(GROUP):
                for h in (0, 1):
                    row = start + g * 16 + h * 8
                    v = center(nn, ns, g, h)
                    kz = at(fz, row)
                    out = center(kx, fx, g, h) * center(nn, ns, g + 1, h) + center(kx, fx, g - 1, h) * center(nn, ns, g - 1, h)
                    out = out + (kz * up(v) + down(kz) * down(v))
                    out = out + (at(fy, row) * ahead(ns, row, v) + at(fw, row) * behind(ns, row, v)) + at(fm, row) * v
                    final = out * (-1.0 / 12.0) - at(us, row)
                    ds[pl.ds(row - 16, 8), :] = at(ds, row, -16) + c0 * v + c1 * final
                    vs[pl.ds(row - 16, 8), :] = at(vs, row, -16) + c2 * v + c3 * final
            return carry

        lax.fori_loop(0, rows // GROUP, step, 0)

    def place(c, core):
        return lax.rem((1 - 2 * core) * (lax.rem(c, 4) - my_y) + 8, 4), lax.rem(c // 4 + my_z, 2)

    def stores(c, core, same, far):
        turn, _ = place(c, core)
        here = pl.ds((c * rows + core * half_rows) * 16, half_rows * 16)
        to = ((far_other, far_same) if far else (near_other, near_same))[same]
        return [pltpu.make_async_copy(a.at[here], to.at[turn, i], out_sem.at[i, core, c]) for i, a in enumerate((ds, vs))]

    def edge_stores(c, core, same, is_end):
        turn, side = place(c, core)
        here = pl.ds((c * rows + core * half_rows) * 16, (half_rows + 2) * 16)
        to = ((ends_other, ends_same) if is_end else (rest_other, rest_same))[same]
        return [pltpu.make_async_copy(es.at[i, here], to.at[lax.rem(turn, 2), side, i], edge_sem.at[i, core, c]) for i in (0, 1)]

    def send(copies, c, core, test):
        for same in (0, 1):
            for kind in (0, 1):
                @pl.when(((my_core == core) == (same == 1)) & (test(*place(c, core)) == (kind == 1)))
                def _():
                    for copy in copies(c, core, same, kind):
                        copy.start()

    def send_edges(c, core):
        send(edge_stores, c, core, lambda turn, side: turn >= 2)

    def send_series(c, core):
        send(stores, c, core, lambda turn, side: side == 1)

    def chunk(c, carry):
        @pl.when(c < CHIPS)
        def _():
            @pl.when(c == 0)
            def _():
                for copy in loads(c, (0, 1, 2)):
                    copy.wait()

            @pl.when(c + 1 < CHIPS)
            def _():
                for copy in loads(c + 1, (0, 1, 2)):
                    copy.wait()

            first_pass(c)
            moments(c)
            send_edges(c, 0)

        @pl.when(c > 0)
        def _():
            send_edges(c - 1, 1)
            for copy in loads(c - 1, (3, 4)):
                copy.wait()
            second_pass(c - 1)
            for core in (0, 1):
                send_series(c - 1, core)

        return carry

    lax.fori_loop(0, CHIPS + 1, chunk, 0)

    def end(c, carry):
        for core in (0, 1):
            for copy in stores(c, core, 1, 1) + edge_stores(c, core, 1, 1):
                copy.wait()
        return carry

    lax.fori_loop(0, CHIPS, end, 0)


def mend_kernel(d, v, low, high, below, above, k, k_low, k_high, d_out, v_out, ds, vs):
    rows = d.shape[0]
    slab = lax.axis_index("gz")
    lower, upper = jnp.where(slab == 0, 1.0, 0.0), jnp.where(slab == SLABS - 1, 1.0, 0.0)
    wide = rows + 2
    z = places(wide)[1]
    factor = []
    for h in (0, 1):
        under = (1.0 - lower) * (k[:, h] + roll(k_low[:, h], -3))
        over = (1.0 - upper) * (k[:, h] + roll(k_high[:, h], 3))
        factor.append(jnp.where(z == 0, under, jnp.where(z == 3, -over, 0.0)) * (1.0 / 12.0))
    from_low = [low[:, h] - below[:, h] for h in (0, 1)]
    from_high = [above[:, h] - high[:, h] for h in (0, 1)]
    direct = []
    for field, slot in ((ds, 0), (vs, 2)):
        for h in (0, 1):
            a = jnp.where(z == 0, roll(from_low[h], -slot), roll(from_high[h], 3 - slot))
            b = jnp.where(z == 0, roll(from_low[h], -slot - 1), roll(from_high[h], 2 - slot))
            w = factor[h] * a
            field[:, h] = w
            direct.append((factor[h] * b + 2.0 * jnp.abs(factor[h]) * w)[1 : rows + 1])
    for field, given, out, direct_of in ((ds, d, d_out, direct[:2]), (vs, v, v_out, direct[2:])):
        w, outflow = spread(field, k, 0, rows, lower, upper)
        for h in (0, 1):
            out[:, h] = given[:, h] + direct_of[h] - outflow[h] * (1.0 / 12.0) - 2.0 * w[h]


ANYWHERE = pl.BlockSpec(memory_space=pl.ANY)
SMEM = pl.BlockSpec(memory_space=pltpu.SMEM)


def params(mib):
    return pltpu.CompilerParams(vmem_limit_bytes=mib * MIB)


def cost(mib):
    return pl.CostEstimate(flops=0, bytes_accessed=mib * MIB, transcendentals=0)


def flat(cells):
    return cells.reshape(-1, 128)


def series(coeffs, u, k, p, cos, sin):
    cells = u.shape[0] // 16
    share = jax.ShapeDtypeStruct((4, 2, cells // COUNT * 16, 128), F32)
    edge = jax.ShapeDtypeStruct((2, 2, 2, (cells // COUNT + 2) * 16, 128), F32)
    wide = pltpu.VMEM(((cells + 2) * 16, 128), F32)
    exact = pltpu.VMEM((cells * 16, 128), F32)
    return pl.pallas_call(
        series_kernel,
        out_shape=(share,) * 4 + (edge,) * 4,
        in_specs=[SMEM] + [ANYWHERE] * 5,
        out_specs=(ANYWHERE,) * 8,
        scratch_shapes=[wide, wide, wide, exact, exact, wide, wide, wide, wide, wide]
        + [
            pltpu.VMEM((2, (cells + 2) * 16, 128), F32),
            pltpu.SemaphoreType.DMA((5, CHIPS)),
            pltpu.SemaphoreType.DMA((2, 2, CHIPS)),
            pltpu.SemaphoreType.DMA((2, 2, CHIPS)),
        ],
        compiler_params=params(56),
        cost_estimate=cost(45),
    )(coeffs, u, k, p, cos, sin)


def mend(d, v, low, high, below, above, k, k_low, k_high):
    shape = jax.ShapeDtypeStruct(d.shape, F32)
    whole = pl.BlockSpec(memory_space=pltpu.VMEM)
    return pl.pallas_call(
        mend_kernel,
        out_shape=(shape, shape),
        in_specs=[whole] * 9,
        out_specs=(whole, whole),
        scratch_shapes=[pltpu.VMEM(k.shape, F32)] * 2,
        compiler_params=params(16),
        cost_estimate=cost(4),
    )(d, v, low, high, below, above, k, k_low, k_high)


CELL = (2, 8, 128)


def along_y(sign):
    def goal(i):
        z, y, core = i // 8, (i // 2) % 4, i % 2
        return z * 8 + ((y + sign * (1 - 2 * core)) % 4) * 2 + core

    return [(i, goal(i)) for i in range(COUNT)]


FORTH, BACK = along_y(1), along_y(-1)
ACROSS = [(i, i ^ 8) for i in range(COUNT)]
SIBLING = [(i, i ^ 1) for i in range(COUNT)]
UP = [(i, i + 1) for i in range(SLABS - 1)]
DOWN = [(i + 1, i) for i in range(SLABS - 1)]


def to_sibling(other):
    return lax.ppermute(other, "tm", SIBLING)


def forth(cells):
    return lax.ppermute(cells, "tm", FORTH)


def back(cells):
    return lax.ppermute(cells, "tm", BACK)


def across(cells):
    return lax.ppermute(cells, "tm", ACROSS)


def after(first, then):
    return lax.optimization_barrier((first, then))[1]


def local(prev_term, last_term, cos_sum, sin_sum, speed_sq, series_coeffs):
    u, p, k = flat(packed(last_term[0])), flat(packed(prev_term[0])), flat(packed(speed_sq))
    cos, sin = flat(packed(cos_sum[0])), flat(packed(sin_sum[0]))
    rows = last_term.shape[1] // COUNT
    me = lax.axis_index("tm")

    outs = series(series_coeffs, u, k, p, cos, sin)
    far_other, far_same, near_other, near_same, ends_other, ends_same, rest_other, rest_same = outs

    ends_came, far_came = to_sibling(ends_other), to_sibling(far_other)
    rest_came = to_sibling(rest_other)
    ends_two = ends_same[0] + ends_came[0]
    near_came = to_sibling(after(ends_two, near_other))
    ends_two = forth(ends_two)
    far_ends = far_same[2:] + far_came[2:]
    ends_came = after(far_ends, ends_came)
    far_ends_came, far_rest_came = across(far_ends), across(far_same[:2] + far_came[:2])
    ends_back = back(ends_same[1] + ends_came[1])

    start = me * rows * 16
    k_here = jnp.concatenate(
        [
            jnp.where(me > 0, lax.dynamic_slice_in_dim(k, jnp.maximum(start - 16, 0), 16), 0.0),
            lax.dynamic_slice_in_dim(k, start, rows * 16),
            jnp.where(me < COUNT - 1, lax.dynamic_slice_in_dim(k, jnp.minimum(start + rows * 16, k.shape[0] - 16), 16), 0.0),
        ]
    )
    k_low, k_high = lax.ppermute(k_here, "gz", UP), lax.ppermute(k_here, "gz", DOWN)

    rest = rest_same + rest_came
    ends_two, rest = lax.optimization_barrier((ends_two, rest))
    ring = forth(rest[1] + ends_two)
    two, direct = (near_same[t] + near_came[t] + far_ends_came[t - 2] for t in (2, 3))
    ring = after((two, direct, k_low, k_high), ring)
    two, direct = forth(two), back(direct)
    edge_far = rest[0, 1] + ends_back[1] + ring[1]
    edge = rest[0, 0] + ends_back[0] + ring[0]
    far_rest_came = after(edge_far, far_rest_came)
    edge_came = across(edge_far)
    last = near_same[1] + near_came[1] + far_rest_came[1] + two
    edge_came = after((last, edge), edge_came)
    last = forth(last)
    low, high = edge[0] + edge_came[0], edge[1] + edge_came[1]
    above, below = lax.ppermute(low, "gz", DOWN), lax.ppermute(high, "gz", UP)
    result = near_same[0] + near_came[0] + far_rest_came[0] + direct + last
    d, v = result[0], result[1]

    wide = (a.reshape(rows + 2, *CELL) for a in (low, high, below, above, k_here, k_low, k_high))
    d, v = mend(d.reshape(rows, *CELL), v.reshape(rows, *CELL), *wide)
    return unpacked(d), unpacked(v)


def solution(mesh):
    return jax.shard_map(
        local,
        mesh=mesh,
        in_specs=(
            P("tm", None, "gz", None),
            P("tm", None, "gz", None),
            P("tm", None, "gz", None),
            P("tm", None, "gz", None),
            P(None, "gz", None),
            P("tm", None),
        ),
        out_specs=(P("tm", "gz", None), P("tm", "gz", None)),
        check_vma=False,
    )
```
